32 devices in a mesh: fsdp: 4 (over z), ctx: 4 (over y, x), tp: 2 (over core).
Axes of the slice: x: 2, y: 2, z: 4, core: 2. Of those that a mesh axis runs over, the one named last changes fastest.
Arguments:
- hidden_in: bfloat16 [2, 4, 1024, 1024], P(None, 'fsdp', 'ctx', 'tp'), may hold values from -6 to 6
- lengths: int32 [2, 4], P(None, 'fsdp'), may hold values from 512 to 1024, as said below
- norm_gains: bfloat16 [2, 2, 1024], replicated, may hold values from 0.5 to 1.5
- mamba_zx: bfloat16 [2, 1024, 2, 1536], P(None, ('fsdp', 'ctx'), None, 'tp'), may hold values from -0.1875 to 0.1875
- mamba_shared: bfloat16 [2, 1024, 280], replicated, may hold values from -0.1875 to 0.1875
- conv_weight: bfloat16 [2, 4, 1792], replicated, may hold values from -3 to 3
- conv_bias: bfloat16 [2, 1792], replicated, may hold values from -2 to 2
- head_params: float32 [2, 3, 24], replicated, may hold values from -14 to 3
- mamba_gain: bfloat16 [2, 1536], replicated, may hold values from 0.5 to 1.5
- mamba_out: bfloat16 [2, 1536, 1024], P(None, 'tp', ('fsdp', 'ctx')), may hold values from -0.15625 to 0.15625
- attn_in: bfloat16 [2, 1024, 2, 384], P(None, ('fsdp', 'ctx'), 'tp'), may hold values from -0.1875 to 0.1875
- attn_out: bfloat16 [2, 512, 1024], P(None, 'tp', ('fsdp', 'ctx')), may hold values from -0.75 to 0.75
- mlp_in: bfloat16 [2, 1024, 2, 2048], P(None, ('fsdp', 'ctx'), None, 'tp'), may hold values from -0.1875 to 0.1875
- mlp_out: bfloat16 [2, 2048, 1024], P(None, 'tp', ('fsdp', 'ctx')), may hold values from -0.125 to 0.125
- out_grad: bfloat16 [2, 4, 1024, 1024], P(None, 'fsdp', 'ctx', 'tp'), may hold values from -6 to 6
Outputs:
- mixed_out: bfloat16 [2, 4, 1024, 1024], P(None, 'fsdp', 'ctx', 'tp')
- input_grad: float32 [2, 4, 1024, 1024], P(None, 'fsdp', 'ctx', 'tp')
- grad_norm_gains: float32 [2, 2, 1024], replicated
- grad_mamba_zx: float32 [2, 1024, 2, 1536], P(None, ('fsdp', 'ctx'), None, 'tp')
- grad_mamba_shared: float32 [2, 1024, 280], replicated
- grad_conv_weight: float32 [2, 4, 1792], replicated
- grad_conv_bias: float32 [2, 1792], replicated
- grad_head_params: float32 [2, 3, 24], replicated
- grad_mamba_gain: float32 [2, 1536], replicated
- grad_mamba_out: float32 [2, 1536, 1024], P(None, 'tp', ('fsdp', 'ctx'))
- grad_attn_in: float32 [2, 1024, 2, 384], P(None, ('fsdp', 'ctx'), 'tp')
- grad_attn_out: float32 [2, 512, 1024], P(None, 'tp', ('fsdp', 'ctx'))
- grad_mlp_in: float32 [2, 1024, 2, 2048], P(None, ('fsdp', 'ctx'), None, 'tp')
- grad_mlp_out: float32 [2, 2048, 1024], P(None, 'tp', ('fsdp', 'ctx'))
The draws below stay inside these ranges and needn't reach their ends.
Inputs may be any that keep to these rules, and one draw needn't show every extreme that they name: `lengths`: for each index along the second dimension one micro-batch, drawn from the seed, holds a sequence of all 1024 positions. Positions at or past a sequence's length are padding.
All inputs are finite; a program needn't handle non-finite values.
Results may differ from the reference program's by a relative error of at most 0.02.
Values may be sent and summed in bfloat16 or wider, within the bound.
No kernel may reach another device: no remote copies, remote signals or barrier semaphores. Data moves between devices by JAX's collectives and lax.ppermute only.
A program may use at most 256 MiB of HBM per device.

```python
import math
import jax
import jax.numpy as jnp
from jax import lax

D = 1024
HEADS = 24
HDIM = 64
STATE = 128
CONV = 4
Q_HEADS = 8
KV_HEADS = 2
ADIM = 64
FF = 2048
SLOT = 1024
MICRO = 2
LAYERS = 2
GROUP = 4
D_SSM = 1536
CONV_CH = 1792
SEQS = 4
N_CTX = 4


def draw_lengths(key, part):
    key = jax.random.fold_in(key, 11)
    first_key, second_key = jax.random.split(key)
    base_lengths = jax.random.randint(first_key, (MICRO, SEQS), SLOT // 2, SLOT + 1)
    full_row = jax.random.randint(second_key, (SEQS,), 0, MICRO)
    micro_rows = jnp.arange(MICRO)[:, None]
    return jnp.where(micro_rows == full_row[None, :], SLOT, base_lengths).astype(jnp.int32)


def draw_head_params(key, part):
    key = jax.random.fold_in(key, 23)
    rate_key, step_key, skip_key = jax.random.split(key, 3)
    shape_pair = (LAYERS, HEADS)
    log_rates = jax.random.uniform(rate_key, shape_pair, jnp.float32, 0.0, math.log(16.0))
    lowest_block = math.log(0.2)
    highest_block = math.log(4.0)
    block_decay = jnp.exp(jax.random.uniform(step_key, shape_pair, jnp.float32, lowest_block, highest_block))
    block_rows = SLOT // N_CTX
    step_values = block_decay / (jnp.exp(log_rates) * block_rows)
    step_bias = step_values + jnp.log(-jnp.expm1(-step_values))
    skip_values = jax.random.uniform(skip_key, shape_pair, jnp.float32, 0.5, 1.5)
    return jnp.stack([log_rates, step_bias, skip_values], axis=1)


def block_scale(own_key, extent, cuts, smallest, top_value):
    level = 1.0
    for dim, parts in cuts:
        draws = jax.random.uniform(jax.random.fold_in(jax.random.fold_in(own_key, 6), dim), (parts,), jnp.float32, smallest / len(cuts), top_value / len(cuts))
        level = level * jnp.repeat(jnp.exp(draws), extent[dim] // parts).reshape((-1,) + (1,) * (len(extent) - 1 - dim))
    return level


def normal_values(stream_key, extent, spread, bound, shards=(), dtype=jnp.bfloat16):
    entries = jax.random.normal(stream_key, extent, jnp.float32) * spread
    if len(shards) > 0:
        entries = block_scale(stream_key, extent, shards, -0.22, 0.18) * entries
    return jnp.clip(entries, min=-bound, max=bound).astype(dtype)


def setup_inputs(seed: int = 0) -> dict:
    key_of = jax.random.split(jax.random.key(seed), 16)
    return {
        "hidden_in": normal_values(key_of[0], (MICRO, SEQS, SLOT, D), 1.0, 6.0, ((1, 4), (2, 4), (3, 2))),
        "lengths": draw_lengths(jax.random.fold_in(key_of[15], 71), 0),
        "norm_gains": jnp.clip(1.0 + 0.1 * jax.random.normal(key_of[2], (LAYERS, 2, D), jnp.float32), 0.5, 1.5).astype(jnp.bfloat16),
        "mamba_zx": normal_values(key_of[3], (LAYERS, D, 2, D_SSM), D ** -0.5, 0.1875, ((1, 16), (3, 2))),
        "mamba_shared": normal_values(key_of[4], (LAYERS, D, 2 * STATE + HEADS), D ** -0.5, 0.1875),
        "conv_weight": normal_values(key_of[5], (LAYERS, CONV, CONV_CH), 0.5, 3.0),
        "conv_bias": normal_values(key_of[6], (LAYERS, CONV_CH), 0.3, 2.0),
        "head_params": draw_head_params(jax.random.fold_in(key_of[15], 71), 0),
        "mamba_gain": jnp.clip(1.0 + 0.1 * jax.random.normal(key_of[8], (LAYERS, D_SSM), jnp.float32), 0.5, 1.5).astype(jnp.bfloat16),
        "mamba_out": normal_values(key_of[9], (LAYERS, D_SSM, D), D_SSM ** -0.5, 0.15625, ((1, 2), (2, 16))),
        "attn_in": normal_values(key_of[10], (LAYERS, D, KV_HEADS, (GROUP + 2) * ADIM), D ** -0.5, 0.1875, ((1, 16), (2, 2))),
        "attn_out": normal_values(key_of[11], (LAYERS, Q_HEADS * ADIM, D), ADIM ** -0.5, 0.75, ((1, 2), (2, 16))),
        "mlp_in": normal_values(key_of[12], (LAYERS, D, 2, FF), D ** -0.5, 0.1875, ((1, 16), (3, 2))),
        "mlp_out": normal_values(key_of[13], (LAYERS, FF, D), FF ** -0.5, 0.125, ((1, 2), (2, 16))),
        "out_grad": normal_values(key_of[14], (MICRO, SEQS, SLOT, D), 1.0, 6.0, ((1, 4), (2, 4), (3, 2))),
    }


EPSILON = 1e-05
THETA = 100000000000.0
HIGHEST_PREC = lax.Precision.HIGHEST

@jax.custom_vjp
def low(v):
    return lax.optimization_barrier(v.astype(jnp.bfloat16)).astype(jnp.float32)

@jax.custom_vjp
def low_back(v):
    return v

def low_keep(v):
    return (low(v), None)

def low_pass(kept, grad):
    return (grad,)

def back_keep(v):
    return (v, None)

def back_low(kept, grad):
    return (low(grad),)
low.defvjp(low_keep, low_pass)
low_back.defvjp(back_keep, back_low)

def multiply_high(left_side, right_side):
    return jnp.dot(left_side, right_side, precision=HIGHEST_PREC)

def unit_rows(values):
    return values * lax.rsqrt(lax.optimization_barrier(jnp.mean(values * values, axis=-1, keepdims=True)) + EPSILON)

def rotate(values, start_row):
    half_width = values.shape[-1] // 2
    places = (start_row + jnp.arange(values.shape[0])).astype(jnp.float32)
    rate_values = jnp.exp(-math.log(THETA) * jnp.arange(half_width).astype(jnp.float32) / half_width)
    angles = places[:, None] * rate_values[None, :]
    cosine = jnp.cos(angles)[:, None, :]
    sine_part = jnp.sin(angles)[:, None, :]
    first_half = values[..., :half_width]
    second = values[..., half_width:]
    return jnp.concatenate([first_half * cosine - second * sine_part, second * cosine + first_half * sine_part], axis=-1)

def convolve(padded, kernel, offset_bias):
    length = padded.shape[0] - kernel.shape[0] + 1
    running_sum = offset_bias[None, :]
    for tap_index in range(kernel.shape[0]):
        running_sum = running_sum + kernel[tap_index][None, :] * padded[tap_index:tap_index + length]
    return jax.nn.silu(running_sum)

def ssd_block(inputs, entry_rows, readout, step_sizes, rate_values, carried):
    log_decay = -step_sizes * rate_values[None, :]
    cumulative = jnp.cumsum(log_decay, axis=0)
    positions = jnp.arange(inputs.shape[0])
    causal = (positions[:, None] >= positions[None, :])[None]
    gap_values = jnp.where(causal, cumulative.T[:, :, None] - cumulative.T[:, None, :], 0.0)
    decay_table = jnp.where(causal, jnp.exp(gap_values), 0.0)
    intersection = jnp.dot(readout, entry_rows.T, precision=HIGHEST_PREC)
    weighted = step_sizes[:, :, None] * inputs
    outputs = jnp.einsum('hts,shp->thp', decay_table * intersection[None], weighted, precision=HIGHEST_PREC)
    outputs = outputs + jnp.exp(cumulative)[:, :, None] * jnp.einsum('tn,hpn->thp', readout, carried, precision=HIGHEST_PREC)
    tail_decay = jnp.exp(cumulative[-1][None, :] - cumulative)
    final_state = jnp.exp(cumulative[-1])[:, None, None] * carried + jnp.einsum('shp,sn->hpn', tail_decay[:, :, None] * weighted, entry_rows, precision=HIGHEST_PREC)
    return (outputs, final_state)

def scan_ssd(inputs, entry_rows, readout, step_sizes, rate_values):
    seg_len = SLOT // N_CTX
    block_count = inputs.shape[0] // seg_len

    def advance(carried, pieces):
        outputs, final_state = ssd_block(pieces[0], pieces[1], pieces[2], pieces[3], rate_values, carried)
        return (final_state, outputs)
    first_state = jnp.zeros((inputs.shape[1], inputs.shape[2], entry_rows.shape[1]), jnp.float32)
    pieces = (inputs.reshape(block_count, seg_len, inputs.shape[1], inputs.shape[2]), entry_rows.reshape(block_count, seg_len, entry_rows.shape[1]), readout.reshape(block_count, seg_len, readout.shape[1]), step_sizes.reshape(block_count, seg_len, step_sizes.shape[1]))
    _, outputs = lax.scan(jax.checkpoint(advance), first_state, pieces)
    return outputs.reshape(inputs.shape)

def attend(queries, key_rows, value_rows):
    seg_len = SLOT // N_CTX
    block_count = queries.shape[0] // seg_len
    group_size = queries.shape[1] // key_rows.shape[1]
    all_keys = jnp.repeat(key_rows, group_size, axis=1)
    all_values = jnp.repeat(value_rows, group_size, axis=1)
    columns = jnp.arange(queries.shape[0])

    def one_block(pieces):
        query_block, start_row = pieces
        scores = low_back(jnp.einsum('qha,kha->hqk', query_block, all_keys, precision=HIGHEST_PREC) * queries.shape[2] ** (-0.5))
        positions = start_row + jnp.arange(seg_len)
        scores = jnp.where((columns[None, :] <= positions[:, None])[None], scores, -1e+30)
        row_top = lax.optimization_barrier(jnp.max(scores, axis=-1, keepdims=True))
        exps = jnp.exp(scores - row_top)
        probs = low(exps / lax.optimization_barrier(jnp.sum(exps, axis=-1, keepdims=True)))
        return jnp.einsum('hqk,kha->qha', probs, all_values, precision=HIGHEST_PREC)
    starts = (jnp.arange(block_count) * seg_len).astype(jnp.int32)
    outputs = lax.map(jax.checkpoint(one_block), (queries.reshape(block_count, seg_len, queries.shape[1], queries.shape[2]), starts))
    return outputs.reshape(queries.shape)

def mixer_and_mlp(hidden, params):
    norm_gain, zx_weight, shared_weight, kernel, offset_bias, head_table, mixer_gain, mixer_out, attn_weight, attn_out_weight, mlp_weight, mlp_out_weight = params
    seq_len = hidden.shape[0]
    normed = low(unit_rows(hidden) * norm_gain[0])
    gate_pre = low_back(multiply_high(normed, zx_weight[:, 0]))
    input_pre = low_back(multiply_high(normed, zx_weight[:, 1]))
    side_rows = multiply_high(normed, shared_weight)
    stacked = low(jnp.concatenate([input_pre, side_rows[:, :2 * STATE]], axis=1))
    step_pre = low_back(side_rows[:, 2 * STATE:])
    padded = jnp.concatenate([jnp.zeros((CONV - 1, stacked.shape[1]), jnp.float32), stacked], axis=0)
    active = convolve(padded, kernel, offset_bias)
    inputs = low(active[:, :D_SSM]).reshape(seq_len, HEADS, HDIM)
    entry_rows = low(active[:, D_SSM:D_SSM + STATE])
    readout = low(active[:, D_SSM + STATE:])
    step_sizes = jax.nn.softplus(step_pre + head_table[1][None, :])
    scanned = scan_ssd(inputs, entry_rows, readout, step_sizes, jnp.exp(head_table[0]))
    mixed_rows = (scanned + head_table[2][None, :, None] * inputs).reshape(seq_len, D_SSM) * jax.nn.silu(gate_pre)
    grouped = unit_rows(mixed_rows.reshape(seq_len, 2, D_SSM // 2)).reshape(seq_len, D_SSM)
    mamba_part = multiply_high(low(grouped * mixer_gain), mixer_out)
    qkv_rows = low_back(multiply_high(normed, attn_weight.reshape(D, -1))).reshape(seq_len, KV_HEADS, GROUP + 2, ADIM)
    queries = low(rotate(qkv_rows[:, :, :GROUP].reshape(seq_len, Q_HEADS, ADIM), 0))
    key_rows = low(rotate(qkv_rows[:, :, GROUP], 0))
    value_rows = low(qkv_rows[:, :, GROUP + 1])
    attended = low(low_back(attend(queries, key_rows, value_rows))).reshape(seq_len, Q_HEADS * ADIM)
    after_mix = hidden + low_back(mamba_part + multiply_high(attended, attn_out_weight))
    normed_two = low(unit_rows(after_mix) * norm_gain[1])
    gate_up = low_back(multiply_high(normed_two, mlp_weight.reshape(D, 2 * FF)))
    activated = low(jax.nn.silu(gate_up[:, :FF]) * gate_up[:, FF:])
    return after_mix + low_back(multiply_high(activated, mlp_out_weight))

def run_layers(params, hidden):
    for layer_index in range(LAYERS):
        hidden = mixer_and_mlp(hidden, tuple((piece[layer_index] for piece in params)))
    return hidden

def reference(hidden_in, lengths, norm_gains, mamba_zx, mamba_shared, conv_weight, conv_bias, head_params, mamba_gain, mamba_out, attn_in, attn_out, mlp_in, mlp_out, out_grad):
    weights = (norm_gains.astype(jnp.float32), mamba_zx.astype(jnp.float32), mamba_shared.astype(jnp.float32), conv_weight.astype(jnp.float32), conv_bias.astype(jnp.float32), head_params.astype(jnp.float32), mamba_gain.astype(jnp.float32), mamba_out.astype(jnp.float32), attn_in.astype(jnp.float32), attn_out.astype(jnp.float32), mlp_in.astype(jnp.float32), mlp_out.astype(jnp.float32))
    seq_total = MICRO * SEQS
    flat_in = hidden_in.reshape(seq_total, SLOT, D)
    flat_grad = out_grad.reshape(seq_total, SLOT, D)
    flat_len = lengths.reshape(seq_total)

    def one_sequence(running, sample_item):
        sample, cotangent, length = sample_item
        keep_mask = (jnp.arange(SLOT) < length).astype(jnp.float32)[:, None]

        def masked(params, hidden):
            return run_layers(params, hidden) * keep_mask
        result, pull_back = jax.vjp(masked, weights, sample.astype(jnp.float32))
        grad_params, grad_input = pull_back(cotangent.astype(jnp.float32))
        return (jax.tree.map(jnp.add, running, grad_params), (result.astype(jnp.bfloat16), grad_input))
    totals, (outputs, input_grads) = lax.scan(one_sequence, jax.tree.map(jnp.zeros_like, weights), (flat_in, flat_grad, flat_len))
    return (outputs.reshape(hidden_in.shape), input_grads.reshape(hidden_in.shape), totals[0], totals[1], totals[2], totals[3], totals[4], totals[5], totals[6], totals[7], totals[8], totals[9], totals[10], totals[11])
```

```python
import functools
import math

import jax
import jax.numpy as jnp
from jax import lax
from jax.experimental import pallas as pl
from jax.experimental.pallas import tpu as pltpu
from jax.sharding import PartitionSpec as P

HDIM = 64
STATE = 128
CONV = 4
ADIM = 64
GROUP = 4
LANES = 128
EPSILON = 1e-05
THETA = 100000000000.0
HIGHEST = lax.Precision.HIGHEST
LOW = jnp.bfloat16
WIDE = jnp.float32
MASKED = -1e30
VMEM_LIMIT = 56 * 1024 * 1024


def dot(a, b, ca=1, cb=0, precision=None):
    return lax.dot_general(
        a, b, (((ca,), (cb,)), ((), ())), preferred_element_type=WIDE, precision=precision
    )


def lane_iota(shape):
    return lax.broadcasted_iota(jnp.int32, shape, len(shape) - 1)


def row_iota(shape):
    return lax.broadcasted_iota(jnp.int32, shape, 0)


def kernel_call(body, grid, in_specs, out_specs, out_shape, scratch=(), flops=0, moved=0):
    return pl.pallas_call(
        body,
        grid=grid,
        in_specs=in_specs,
        out_specs=out_specs,
        out_shape=out_shape,
        scratch_shapes=list(scratch),
        compiler_params=pltpu.CompilerParams(vmem_limit_bytes=VMEM_LIMIT),
        cost_estimate=pl.CostEstimate(flops=flops, bytes_accessed=moved, transcendentals=0),
    )


def whole(shape):
    return pl.BlockSpec(shape, lambda s: (0,) * len(shape))


def rows_block(rows, cols, col=0):
    return pl.BlockSpec((rows, cols), lambda s: (s, col))


def sequence_block(*shape):
    return pl.BlockSpec((None,) + shape, lambda s: (s,) + (0,) * len(shape))


def xor_pairs(count, bit):
    return [(i, i ^ bit) for i in range(count)]


def shifted(x, axis, by):
    count = lax.axis_size(axis)
    pairs = [(i, i + by) for i in range(count) if 0 <= i + by < count]
    return lax.ppermute(x, axis, pairs)


def tp_peer(x):
    return lax.ppermute(x, "tp", xor_pairs(lax.axis_size("tp"), 1))


def tp_join(x):
    peer = tp_peer(x)
    first = lax.axis_index("tp") == 0
    return jnp.where(
        first, jnp.concatenate([x, peer], axis=-1), jnp.concatenate([peer, x], axis=-1)
    )


def tp_sum(partial_sum):
    low = partial_sum.astype(LOW)
    peer = tp_peer(low)
    return low.astype(WIDE) + peer.astype(WIDE)


def halve(values, dim, bit, axis, step):
    mine = lax.dynamic_index_in_dim(values, bit, dim, False)
    other = lax.dynamic_index_in_dim(values, 1 - bit, dim, False)
    came = lax.ppermute(other, axis, xor_pairs(lax.axis_size(axis), step))
    return mine.astype(WIDE) + came.astype(WIDE)


def bits_of(axis):
    return [1 << i for i in range(lax.axis_size(axis).bit_length() - 1)]


def scatter_rows(table):
    fsdp, ctx = lax.axis_size("fsdp"), lax.axis_size("ctx")
    width = table.shape[1]
    rows = table.shape[0] // (fsdp * ctx)
    steps = bits_of("ctx")
    place = lax.axis_index("ctx")
    cut = width // 256 * 128
    done = []
    for order, part in ((steps, table[:, :cut]), (steps[::-1], table[:, cut:])):
        left = steps[::-1]
        v = part.reshape((fsdp,) + (2,) * len(steps) + (rows, part.shape[1]))
        for step in order:
            dim = 1 + left.index(step)
            left = [b for b in left if b != step]
            v = halve(v, dim, jnp.where((place & step) != 0, 1, 0), "ctx", step).astype(LOW)
        done.append(v)
    v = jnp.concatenate(done, axis=-1)
    place = lax.axis_index("fsdp")
    for step in bits_of("fsdp")[::-1]:
        v = v.reshape((2, step, rows, width))
        v = halve(v, 0, jnp.where((place & step) != 0, 1, 0), "fsdp", step)
        if step > 1:
            v = v.astype(LOW)
    return v.reshape(rows, width)


def join_rows(piece):
    v = piece[None]
    for axis in ("ctx", "fsdp"):
        place = lax.axis_index(axis)
        for step in bits_of(axis):
            came = lax.ppermute(v, axis, xor_pairs(lax.axis_size(axis), step))
            v = jnp.where(
                (place & step) == 0,
                jnp.concatenate([v, came], axis=0),
                jnp.concatenate([came, v], axis=0),
            )
    return v.reshape((-1,) + piece.shape[1:])


def sum_everywhere(v):
    for axis in ("ctx", "fsdp"):
        for step in bits_of(axis):
            v = v + lax.ppermute(v, axis, xor_pairs(lax.axis_size(axis), step))
    return v


def turn_tables(start_row, rows):
    half = ADIM // 2
    places = (start_row + jnp.arange(rows)).astype(WIDE)
    rates = jnp.exp(-math.log(THETA) * jnp.arange(half).astype(WIDE) / half)
    angles = places[:, None] * rates[None, :]
    cosine, sine = jnp.cos(angles), jnp.sin(angles)
    one_cos = jnp.concatenate([cosine, cosine], axis=1)
    one_sin = jnp.concatenate([-sine, sine], axis=1)
    still = jnp.ones_like(one_cos)
    return (
        jnp.concatenate([one_cos, one_cos, one_cos, still], axis=1),
        jnp.concatenate([one_sin, one_sin, one_sin, jnp.zeros_like(one_sin)], axis=1),
    )


def turned(values, cosine, sine):
    lanes = lane_iota(values.shape) % ADIM
    swapped = jnp.where(
        lanes < ADIM // 2,
        pltpu.roll(values, LANES - ADIM // 2, 1),
        pltpu.roll(values, ADIM // 2, 1),
    )
    return values * cosine + swapped * sine


def qkv_body(rows_ref, cos_ref, sin_ref, q_ref, kv_ref):
    for pair in range(GROUP // 2):
        lanes = slice(pair * LANES, (pair + 1) * LANES)
        q_ref[:, lanes] = turned(
            rows_ref[:, lanes], cos_ref[:, :LANES], sin_ref[:, :LANES]
        ).astype(LOW)
    width = GROUP * ADIM
    kv_ref[...] = turned(
        rows_ref[:, width : width + LANES], cos_ref[:, LANES:], sin_ref[:, LANES:]
    ).astype(LOW)


def split_qkv(projected, tables, rows, column):
    total = projected.shape[0]
    width = GROUP * ADIM
    return kernel_call(
        qkv_body,
        (total // rows,),
        [rows_block(rows, width + LANES, column), whole((rows, 2 * LANES)), whole((rows, 2 * LANES))],
        [rows_block(rows, width), rows_block(rows, LANES)],
        [
            jax.ShapeDtypeStruct((total, width), LOW),
            jax.ShapeDtypeStruct((total, LANES), LOW),
        ],
        flops=total * 400 * 4,
        moved=total * 384 * 6,
    )(projected, *tables)


def head_lanes(values, head):
    pair = values[:, head // 2 * LANES : (head // 2 + 1) * LANES]
    if head % 2:
        pair = pltpu.roll(pair, ADIM, 1)
    return jnp.where(lane_iota(pair.shape) < ADIM, pair, jnp.zeros_like(pair))


def load_keys(kv_refs, keys):
    rows = kv_refs[0].shape[0]
    for i, ref in enumerate(kv_refs):
        keys[i * rows : (i + 1) * rows, :] = ref[...]


def attention_bias(place, rows, count):
    shape = (rows, rows * count)
    column = lane_iota(shape)
    earlier = (column >= rows) & (column < rows * (place + 1))
    return (column <= row_iota(shape)) | earlier


def attend_body(count, place_ref, q_ref, *refs):
    kv_refs, (out_ref, total_ref, keys) = refs[:count], refs[count:]
    rows = q_ref.shape[0]
    load_keys(kv_refs, keys)
    seen = attention_bias(place_ref[0], rows, count)
    q_all = q_ref[...].astype(WIDE)
    all_keys = keys[...]
    totals = jnp.zeros((rows, LANES), WIDE)
    lanes = lane_iota((rows, LANES))
    outs = []
    for head in range(GROUP):
        query = head_lanes(q_all, head).astype(LOW)
        scores = jnp.where(seen, dot(query, all_keys, 1, 1) * ADIM**-0.5, MASKED)
        top = jnp.max(scores, axis=1, keepdims=True)
        raised = jnp.exp(scores - top)
        total = jnp.sum(raised, axis=1, keepdims=True)
        weights = (raised * (1.0 / total)).astype(LOW)
        outs.append(dot(weights, all_keys))
        totals = jnp.where(lanes == head, top + jnp.log(total), totals)
    total_ref[...] = totals
    for pair in range(GROUP // 2):
        first = pltpu.roll(outs[2 * pair], ADIM, 1)
        out_ref[:, pair * LANES : (pair + 1) * LANES] = jnp.where(
            lanes < ADIM, first, outs[2 * pair + 1]
        ).astype(LOW)


def attend(place, queries, kv_list, rows):
    total = queries.shape[0]
    width = queries.shape[1]
    count = len(kv_list)
    return kernel_call(
        functools.partial(attend_body, count),
        (total // rows,),
        [pl.BlockSpec(memory_space=pltpu.SMEM), rows_block(rows, width)]
        + [rows_block(rows, LANES)] * count,
        [rows_block(rows, width), rows_block(rows, LANES)],
        [
            jax.ShapeDtypeStruct((total, width), LOW),
            jax.ShapeDtypeStruct((total, LANES), WIDE),
        ],
        [pltpu.VMEM((rows * count, LANES), LOW)],
        flops=total * rows * count * GROUP * LANES * 4,
        moved=total * (width * 4 + LANES * 12),
    )(place, queries, *kv_list)


def attend_back_body(count, place_ref, q_ref, grad_ref, total_ref, cos_ref, sin_ref, *refs):
    kv_refs = refs[:count]
    dq_ref = refs[count]
    dkv_refs = refs[count + 1 : 2 * count + 1]
    keys = refs[2 * count + 1]
    rows = q_ref.shape[0]
    load_keys(kv_refs, keys)
    seen = attention_bias(place_ref[0], rows, count)
    q_all = q_ref[...].astype(WIDE)
    grad_all = grad_ref[...].astype(WIDE)
    all_keys = keys[...]
    lanes = lane_iota((rows, LANES))
    grad_kv = None
    dqs = []
    for head in range(GROUP):
        query = head_lanes(q_all, head).astype(LOW)
        upper = pltpu.roll(head_lanes(grad_all, head), ADIM, 1).astype(LOW)
        scores = jnp.where(seen, dot(query, all_keys, 1, 1) * ADIM**-0.5, MASKED)
        probs = jnp.exp(scores - total_ref[:, head : head + 1])
        grad_probs = dot(upper, all_keys, 1, 1)
        inner = jnp.sum(probs * grad_probs, axis=1, keepdims=True)
        grad_scores = (probs * (grad_probs - inner)).astype(LOW)
        dqs.append(dot(grad_scores, all_keys) * ADIM**-0.5)
        fresh = dot(grad_scores, query, 0, 0) * ADIM**-0.5 + dot(
            probs.astype(LOW), upper, 0, 0
        )
        grad_kv = fresh if grad_kv is None else grad_kv + fresh
    for pair in range(GROUP // 2):
        both = jnp.where(lanes < ADIM, dqs[2 * pair], pltpu.roll(dqs[2 * pair + 1], ADIM, 1))
        dq_ref[:, pair * LANES : (pair + 1) * LANES] = turned(
            both, cos_ref[:, :LANES], -sin_ref[:, :LANES]
        ).astype(LOW)
    for i, ref in enumerate(dkv_refs):
        ref[...] = grad_kv[i * rows : (i + 1) * rows].astype(ref.dtype)


def attend_back(place, queries, grad_out, log_total, tables, kv_list, rows):
    total, width = queries.shape
    count = len(kv_list)
    return kernel_call(
        functools.partial(attend_back_body, count),
        (total // rows,),
        [
            pl.BlockSpec(memory_space=pltpu.SMEM),
            rows_block(rows, width),
            rows_block(rows, width),
            rows_block(rows, LANES),
            whole((rows, 2 * LANES)),
            whole((rows, 2 * LANES)),
        ]
        + [rows_block(rows, LANES)] * count,
        [rows_block(rows, width)] + [rows_block(rows, LANES)] * count,
        [jax.ShapeDtypeStruct((total, width), LOW), jax.ShapeDtypeStruct((total, LANES), WIDE)]
        + [jax.ShapeDtypeStruct((total, LANES), LOW)] * (count - 1),
        [pltpu.VMEM((rows * count, LANES), LOW)],
        flops=total * rows * count * GROUP * LANES * 10,
        moved=total * (width * 6 + LANES * 20),
    )(place, queries, grad_out, log_total, *tables, *kv_list)


def key_body(own_ref, *refs):
    came, (cos_ref, sin_ref, out_ref) = refs[:-3], refs[-3:]
    values = own_ref[...]
    for ref in came:
        values = values + ref[...].astype(WIDE)
    out_ref[...] = turned(values, cos_ref[:, LANES:], -sin_ref[:, LANES:]).astype(LOW)


def finish_keys(own, came, tables, rows):
    total = own.shape[0]
    return kernel_call(
        key_body,
        (total // rows,),
        [rows_block(rows, LANES)] * (1 + len(came)) + [whole((rows, 2 * LANES))] * 2,
        rows_block(rows, LANES),
        jax.ShapeDtypeStruct((total, LANES), LOW),
        flops=total * LANES * 10,
        moved=total * LANES * 12,
    )(own, *came, *tables)


def sigmoid(v):
    return 1.0 / (1.0 + jnp.exp(-v))


def softplus(v):
    return jnp.maximum(v, 0.0) + jnp.log1p(jnp.exp(-jnp.abs(v)))


def over_pair(values, pair, shape):
    first = values[:, 2 * pair : 2 * pair + 1]
    second = values[:, 2 * pair + 1 : 2 * pair + 2]
    return jnp.where(lane_iota(shape) < HDIM, first, second)


def lower_ones(rows, flip):
    shape = (rows, rows)
    t, s = row_iota(shape), lane_iota(shape)
    return jnp.where((t <= s) if flip else (t >= s), 1.0, 0.0).astype(WIDE)


def convolved(padded, taps_ref, rows):
    total = taps_ref[CONV : CONV + 1, :]
    for j in range(CONV):
        first = 8 - CONV + 1 + j
        total = total + taps_ref[j : j + 1, :] * padded[first : first + rows, :]
    return total


def scan_body(
    zx_ref, side_ref, rim_ref, taps_ref, heads_ref,
    stk_ref, x_ref, bc_ref, y_ref, state_ref, cum_ref, step_ref, padded,
):
    rows, channels = zx_ref.shape
    heads = channels // HDIM
    stk_ref[:, :channels] = zx_ref[...].astype(LOW)
    stk_ref[:, channels:] = side_ref[:, : 2 * STATE].astype(LOW)
    padded[0:8, :] = rim_ref[...]
    padded[8 : 8 + rows, :] = stk_ref[...].astype(WIDE)
    before = convolved(padded, taps_ref, rows)
    active = (before * sigmoid(before)).astype(LOW)
    x_ref[...] = active[:, :channels]
    bc_ref[...] = active[:, channels:]
    step = softplus(side_ref[:, 2 * STATE :] + heads_ref[1:2, :])
    cum = dot(lower_ones(rows, False), -step * jnp.exp(heads_ref[0:1, :]), precision=HIGHEST)
    step_ref[...] = step
    cum_ref[...] = cum
    cum_rows, step_rows = cum.T, step.T
    tail = jnp.exp(cum[rows - 1 : rows, :] - cum) * step
    entry, readout = bc_ref[:, :STATE], bc_ref[:, STATE:]
    cross = dot(readout, entry, 1, 1)
    shape = (rows, rows)
    causal = row_iota(shape) >= lane_iota(shape)
    lanes = lane_iota((rows, LANES))
    for pair in range(heads // 2):
        block = slice(pair * LANES, (pair + 1) * LANES)
        inputs = x_ref[:, block]
        outs = []
        for head in (2 * pair, 2 * pair + 1):
            gap = cum[:, head : head + 1] - cum_rows[head : head + 1, :]
            decay = jnp.exp(jnp.where(causal, gap, MASKED))
            mixed = (decay * cross * step_rows[head : head + 1, :]).astype(LOW)
            outs.append(dot(mixed, inputs))
        y_ref[:, block] = jnp.where(lanes < HDIM, outs[0], outs[1])
        scaled = (over_pair(tail, pair, (rows, LANES)) * inputs.astype(WIDE)).astype(LOW)
        state_ref[block, :] = dot(scaled, entry, 0, 0)


def scan_local(projected, side, rim, taps, heads, rows, channels):
    total = projected.shape[0]
    count = total // rows
    width = channels + 2 * STATE
    return kernel_call(
        scan_body,
        (count,),
        [
            rows_block(rows, channels, 1),
            rows_block(rows, side.shape[1]),
            sequence_block(8, width),
            whole((8, width)),
            whole((8, LANES)),
        ],
        [
            rows_block(rows, width),
            rows_block(rows, channels),
            rows_block(rows, 2 * STATE),
            rows_block(rows, channels),
            rows_block(channels, STATE),
            rows_block(rows, LANES),
            rows_block(rows, LANES),
        ],
        [
            jax.ShapeDtypeStruct((total, width), LOW),
            jax.ShapeDtypeStruct((total, channels), LOW),
            jax.ShapeDtypeStruct((total, 2 * STATE), LOW),
            jax.ShapeDtypeStruct((total, channels), WIDE),
            jax.ShapeDtypeStruct((count * channels, STATE), WIDE),
            jax.ShapeDtypeStruct((total, LANES), WIDE),
            jax.ShapeDtypeStruct((total, LANES), WIDE),
        ],
        [pltpu.VMEM((rows + 8, width), WIDE)],
        flops=total * rows * channels * 8,
        moved=total * width * 16,
    )(projected, side, rim, taps, heads)


def tail_body(
    y_ref, cum_ref, bc_ref, x_ref, gate_ref, start_ref, heads_ref, gain_ref, out_ref, norm_ref
):
    rows, channels = y_ref.shape
    readout = bc_ref[:, STATE:]
    grown = jnp.exp(cum_ref[...])
    square = jnp.zeros((rows, 1), WIDE)
    for pair in range(channels // LANES):
        block = slice(pair * LANES, (pair + 1) * LANES)
        carried = dot(readout, start_ref[block, :].astype(LOW), 1, 1)
        y = y_ref[:, block] + over_pair(grown, pair, carried.shape) * carried
        out_ref[:, block] = y
        skip = over_pair(heads_ref[2:3, :], pair, (1, LANES))
        gate = gate_ref[:, block]
        mixed = (y + skip * x_ref[:, block].astype(WIDE)) * (gate * sigmoid(gate))
        square = square + jnp.sum(mixed * mixed, axis=1, keepdims=True)
    scale = lax.rsqrt(square * (1.0 / channels) + EPSILON)
    for pair in range(channels // LANES):
        block = slice(pair * LANES, (pair + 1) * LANES)
        skip = over_pair(heads_ref[2:3, :], pair, (1, LANES))
        gate = gate_ref[:, block]
        mixed = (out_ref[:, block] + skip * x_ref[:, block].astype(WIDE)) * (gate * sigmoid(gate))
        norm_ref[:, block] = (mixed * scale * gain_ref[:, block]).astype(LOW)


def gate_tail(y, cum, bc, x, projected, start, heads, gain, rows):
    total, channels = y.shape
    return kernel_call(
        tail_body,
        (total // rows,),
        [
            rows_block(rows, channels),
            rows_block(rows, LANES),
            rows_block(rows, 2 * STATE),
            rows_block(rows, channels),
            rows_block(rows, channels, 0),
            rows_block(channels, STATE),
            whole((8, LANES)),
            whole((1, channels)),
        ],
        [rows_block(rows, channels), rows_block(rows, channels)],
        [
            jax.ShapeDtypeStruct((total, channels), WIDE),
            jax.ShapeDtypeStruct((total, channels), LOW),
        ],
        flops=total * channels * (2 * STATE + 40),
        moved=total * channels * 18,
    )(y, cum, bc, x, projected, start, heads, gain)


def tail_back_body(
    dn_ref, y_ref, cum_ref, bc_ref, x_ref, gate_ref, heads_ref, gain_ref,
    du_ref, dgate_ref, state_ref, sums_ref,
):
    rows, channels = y_ref.shape
    readout = bc_ref[:, STATE:]
    grown = jnp.exp(cum_ref[...])
    square = jnp.zeros((rows, 1), WIDE)
    inner = jnp.zeros((rows, 1), WIDE)
    for pair in range(channels // LANES):
        block = slice(pair * LANES, (pair + 1) * LANES)
        skip = over_pair(heads_ref[2:3, :], pair, (1, LANES))
        gate = gate_ref[:, block]
        mixed = (y_ref[:, block] + skip * x_ref[:, block].astype(WIDE)) * (gate * sigmoid(gate))
        square = square + jnp.sum(mixed * mixed, axis=1, keepdims=True)
        inner = inner + jnp.sum(
            dn_ref[:, block] * gain_ref[:, block] * mixed, axis=1, keepdims=True
        )
    scale = lax.rsqrt(square * (1.0 / channels) + EPSILON)
    inner = inner * scale * (1.0 / channels)
    sums_ref[...] = jnp.zeros(sums_ref.shape, WIDE)
    for pair in range(channels // LANES):
        block = slice(pair * LANES, (pair + 1) * LANES)
        skip = over_pair(heads_ref[2:3, :], pair, (1, LANES))
        gate = gate_ref[:, block]
        inputs = x_ref[:, block].astype(WIDE)
        sigma = sigmoid(gate)
        value = y_ref[:, block] + skip * inputs
        unit = value * (gate * sigma) * scale
        upstream = dn_ref[:, block]
        dmixed = scale * (upstream * gain_ref[:, block] - unit * inner)
        du = dmixed * gate * sigma
        du_ref[:, block] = du
        dgate_ref[:, block] = (
            dmixed * value * (sigma * (1.0 + gate * (1.0 - sigma)))
        ).astype(LOW)
        sums_ref[0:1, block] = jnp.sum(upstream * unit, axis=0, keepdims=True)
        sums_ref[1:2, block] = jnp.sum(du * inputs, axis=0, keepdims=True)
        state_ref[block, :] = dot(
            (over_pair(grown, pair, du.shape) * du).astype(LOW), readout, 0, 0
        )


def gate_tail_back(dn, y, cum, bc, x, projected, heads, gain, rows):
    total, channels = y.shape
    count = total // rows
    return kernel_call(
        tail_back_body,
        (count,),
        [
            rows_block(rows, channels),
            rows_block(rows, channels),
            rows_block(rows, LANES),
            rows_block(rows, 2 * STATE),
            rows_block(rows, channels),
            rows_block(rows, channels, 0),
            whole((8, LANES)),
            whole((1, channels)),
        ],
        [
            rows_block(rows, channels),
            rows_block(rows, channels),
            rows_block(channels, STATE),
            sequence_block(8, channels),
        ],
        [
            jax.ShapeDtypeStruct((total, channels), WIDE),
            jax.ShapeDtypeStruct((total, channels), LOW),
            jax.ShapeDtypeStruct((count * channels, STATE), WIDE),
            jax.ShapeDtypeStruct((count, 8, channels), WIDE),
        ],
        flops=total * channels * (2 * STATE + 60),
        moved=total * channels * 22,
    )(dn, y, cum, bc, x, projected, heads, gain)


def lane_sums(values):
    first = lane_iota(values.shape) < HDIM
    return (
        jnp.sum(jnp.where(first, values, 0.0), axis=1, keepdims=True),
        jnp.sum(jnp.where(first, 0.0, values), axis=1, keepdims=True),
    )


def scan_back_body(
    du_ref, x_ref, bc_ref, stk_ref, rim_ref, cum_ref, step_ref, side_ref, start_ref, later_ref,
    taps_ref, heads_ref,
    dstk_ref, drim_ref, dstep_ref, dtaps_ref, dheads_ref, padded, dact, after,
):
    rows, channels = du_ref.shape
    heads = channels // HDIM
    width = channels + 2 * STATE
    entry, readout = bc_ref[:, :STATE], bc_ref[:, STATE:]
    cum, step = cum_ref[...], step_ref[...]
    cum_rows = cum.T
    last = cum[rows - 1 : rows, :]
    grown = jnp.exp(cum)
    decayed = jnp.exp(last - cum)
    tail = decayed * step
    cross = dot(entry, readout, 1, 1)
    shape = (rows, rows)
    causal = row_iota(shape) <= lane_iota(shape)
    lanes = lane_iota((rows, LANES))
    small = lane_iota((1, LANES))
    dcross = jnp.zeros(shape, WIDE)
    entry_grad = jnp.zeros((rows, STATE), WIDE)
    readout_grad = jnp.zeros((rows, STATE), WIDE)
    pulled = jnp.zeros((rows, LANES), WIDE)
    arrived = []
    carried_sum = jnp.zeros((rows, LANES), WIDE)
    final_sum = jnp.zeros((rows, LANES), WIDE)
    state_sum = jnp.zeros((1, LANES), WIDE)
    for pair in range(heads // 2):
        block = slice(pair * LANES, (pair + 1) * LANES)
        inputs = x_ref[:, block]
        inputs_wide = inputs.astype(WIDE)
        du = du_ref[:, block]
        du_low = du.astype(LOW)
        start = start_ref[block, :]
        later = later_ref[block, :]
        start_low, later_low = start.astype(LOW), later.astype(LOW)
        pulls = []
        for k in range(2):
            head = 2 * pair + k
            own = (lanes < HDIM) if k == 0 else (lanes >= HDIM)
            gap = cum_rows[head : head + 1, :] - cum[:, head : head + 1]
            decay = jnp.exp(jnp.where(causal, gap, MASKED))
            pulls.append(dot((decay * cross).astype(LOW), du_low))
            dmix = dot(jnp.where(own, inputs, jnp.zeros_like(inputs)), du_low, 1, 1) * decay
            stepped = step[:, head : head + 1]
            dcross = dcross + dmix * stepped
            dgap = dmix * cross
            pulled = jnp.where(lanes == head, jnp.sum(dgap, axis=1, keepdims=True), pulled)
            arrived.append(jnp.sum(dgap * stepped, axis=0, keepdims=True))
        pull = jnp.where(lanes < HDIM, pulls[0], pulls[1])
        grown_pair = over_pair(grown, pair, du.shape)
        grown_du = grown_pair * du
        readout_grad = readout_grad + dot(grown_du.astype(LOW), start_low)
        sums = lane_sums(grown_du * dot(readout, start_low, 1, 1))
        carried_sum = jnp.where(lanes == 2 * pair, sums[0], carried_sum)
        carried_sum = jnp.where(lanes == 2 * pair + 1, sums[1], carried_sum)
        tail_pair = over_pair(tail, pair, du.shape)
        from_later = dot(entry, later_low, 1, 1)
        entry_grad = entry_grad + dot((tail_pair * inputs_wide).astype(LOW), later_low)
        sums = lane_sums(inputs_wide * from_later)
        final_sum = jnp.where(lanes == 2 * pair, sums[0], final_sum)
        final_sum = jnp.where(lanes == 2 * pair + 1, sums[1], final_sum)
        product = start * later
        for k in range(2):
            total = jnp.sum(
                jnp.sum(product[k * HDIM : (k + 1) * HDIM], axis=0, keepdims=True),
                axis=1,
                keepdims=True,
            )
            state_sum = jnp.where(small == 2 * pair + k, total, state_sum)
        skip = over_pair(heads_ref[2:3, :], pair, (1, LANES))
        dact[:, block] = (
            skip * du + over_pair(step, pair, du.shape) * pull + tail_pair * from_later
        )
    dcross_low = dcross.astype(LOW)
    dact[:, channels : channels + STATE] = entry_grad + dot(dcross_low, readout)
    dact[:, channels + STATE :] = readout_grad + dot(dcross_low, entry, 0, 0)
    arrived.append(jnp.zeros((LANES - heads, rows), WIDE))
    arrived_columns = jnp.concatenate(arrived, axis=0).T
    weighted = tail * final_sum
    dcum = arrived_columns - step * pulled + carried_sum - weighted
    at_last = jnp.sum(weighted, axis=0, keepdims=True) + jnp.exp(last) * state_sum
    dcum = dcum + jnp.where(row_iota(dcum.shape) == rows - 1, at_last, 0.0)
    dlog = dot(lower_ones(rows, True), dcum, precision=HIGHEST)
    rate = jnp.exp(heads_ref[0:1, :])
    dstep = pulled + decayed * final_sum - rate * dlog
    dstep_pre = dstep * sigmoid(side_ref[...] + heads_ref[1:2, :])
    dstep_pre = jnp.where(lanes < heads, dstep_pre, 0.0)
    dstep_ref[...] = dstep_pre.astype(LOW)
    dheads_ref[...] = jnp.zeros(dheads_ref.shape, WIDE)
    dheads_ref[0:1, :] = -rate * jnp.sum(step * dlog, axis=0, keepdims=True)
    dheads_ref[1:2, :] = jnp.sum(dstep_pre, axis=0, keepdims=True)

    padded[0:8, :] = rim_ref[...]
    padded[8 : 8 + rows, :] = stk_ref[...].astype(WIDE)
    before = convolved(padded, taps_ref, rows)
    sigma = sigmoid(before)
    dbefore = dact[...] * sigma * (1.0 + before * (1.0 - sigma))
    after[0:8, :] = jnp.zeros((8, width), WIDE)
    after[8 : 8 + rows, :] = dbefore
    after[8 + rows : 16 + rows, :] = jnp.zeros((8, width), WIDE)
    dtaps_ref[...] = jnp.zeros(dtaps_ref.shape, WIDE)
    back = None
    for j in range(CONV):
        first = 8 - CONV + 1 + j
        dtaps_ref[j : j + 1, :] = jnp.sum(
            after[8 : 8 + rows, :] * padded[first : first + rows, :], axis=0, keepdims=True
        )
        first = CONV - 1 - j
        term = taps_ref[j : j + 1, :] * after[first : first + rows + 8, :]
        back = term if back is None else back + term
    dtaps_ref[CONV : CONV + 1, :] = jnp.sum(after[8 : 8 + rows, :], axis=0, keepdims=True)
    drim_ref[...] = back[0:8]
    dstk_ref[...] = back[8:]


def scan_back(du, x, bc, stk, rim, cum, step, side, start, later, taps, heads, rows):
    total, channels = du.shape
    count = total // rows
    width = channels + 2 * STATE
    return kernel_call(
        scan_back_body,
        (count,),
        [
            rows_block(rows, channels),
            rows_block(rows, channels),
            rows_block(rows, 2 * STATE),
            rows_block(rows, width),
            sequence_block(8, width),
            rows_block(rows, LANES),
            rows_block(rows, LANES),
            rows_block(rows, LANES, 2 * STATE // LANES),
            rows_block(channels, STATE),
            rows_block(channels, STATE),
            whole((8, width)),
            whole((8, LANES)),
        ],
        [
            rows_block(rows, width),
            sequence_block(8, width),
            rows_block(rows, LANES),
            sequence_block(8, width),
            sequence_block(8, LANES),
        ],
        [
            jax.ShapeDtypeStruct((total, width), WIDE),
            jax.ShapeDtypeStruct((count, 8, width), WIDE),
            jax.ShapeDtypeStruct((total, LANES), LOW),
            jax.ShapeDtypeStruct((count, 8, width), WIDE),
            jax.ShapeDtypeStruct((count, 8, LANES), WIDE),
        ],
        [
            pltpu.VMEM((rows + 8, width), WIDE),
            pltpu.VMEM((rows, width), WIDE),
            pltpu.VMEM((rows + 16, width), WIDE),
        ],
        flops=total * rows * channels * 20,
        moved=total * width * 24,
    )(du, x, bc, stk, rim, cum, step, side, start, later, taps, heads)


def pass_states(states, decays, heads, forward):
    count = lax.axis_size("ctx")
    place = lax.axis_index("ctx")
    sequences = decays.shape[0]
    channels = states.shape[0] // sequences
    high = decays.astype(LOW)
    low = (decays - high.astype(WIDE)).astype(LOW)
    extra = jnp.concatenate(
        [high[..., None], low[..., None], jnp.zeros((sequences, LANES, 14), LOW)], axis=2
    ).transpose(0, 2, 1)
    parcel = jnp.concatenate([states.reshape(sequences, channels, STATE).astype(LOW), extra], axis=1)
    total = None
    for by in range(count - 1, 0, -1):
        came = shifted(parcel, "ctx", by if forward else -by).astype(WIDE)
        fresh = came[:, :channels]
        if total is not None:
            factor = (came[:, channels] + came[:, channels + 1])[:, :heads]
            fresh = fresh + jnp.repeat(factor, HDIM, axis=1)[:, :, None] * total
        total = fresh
    return total.reshape(states.shape)


def unit_scale(values):
    return lax.rsqrt(jnp.mean(values * values, axis=-1, keepdims=True) + EPSILON)


def normalize(values, gain):
    return (values * unit_scale(values) * gain).astype(LOW)


def norm_grad(kept, gain, upstream):
    scale = unit_scale(kept)
    unit = kept * scale
    scaled = upstream * gain
    inner = jnp.mean(scaled * unit, axis=-1, keepdims=True)
    return scale * (scaled - unit * inner), jnp.sum(upstream * unit, axis=0)


def product(a, b):
    return jnp.dot(a, b, preferred_element_type=WIDE)


def against_rows(a, b):
    return dot(a, b, 1, 1)


def over_rows(a, b):
    return dot(a, b, 0, 0).astype(LOW)


def gathered(piece):
    return lax.all_gather(piece, ("fsdp", "ctx"), axis=0, tiled=True)


def fetch(layer, pieces):
    zx, mix, attn, attn_out, mlp, mlp_out = (p[layer] for p in pieces)
    rows = zx.shape[0]
    return (
        gathered(jnp.concatenate([zx.reshape(rows, -1), attn.reshape(rows, -1)], axis=1)),
        gathered(jnp.concatenate([mix.T, attn_out.T], axis=1)),
        gathered(mlp.reshape(rows, -1)),
        gathered(mlp_out.T),
    )


def own_part(values, size, axis):
    return lax.dynamic_slice_in_dim(values, lax.axis_index("tp") * size, size, axis)


def padded_to(values, rows, lanes):
    return jnp.pad(values, ((0, rows - values.shape[0]), (0, lanes - values.shape[1])))


def local_small(layer, norm_gains, mamba_shared, conv_weight, conv_bias, head_params, mamba_gain):
    tp = lax.axis_size("tp")
    heads = head_params.shape[2] // tp
    full_ssm = mamba_gain.shape[1]
    channels = full_ssm // tp
    shared_all = mamba_shared[layer]
    shared = jnp.concatenate(
        [
            shared_all[:, : 2 * STATE],
            own_part(shared_all[:, 2 * STATE :], heads, 1),
            jnp.zeros((shared_all.shape[0], LANES - heads), LOW),
        ],
        axis=1,
    )
    taps_all = jnp.concatenate([conv_weight[layer], conv_bias[layer][None]], axis=0).astype(WIDE)
    taps = jnp.concatenate(
        [own_part(taps_all[:, :full_ssm], channels, 1), taps_all[:, full_ssm:]], axis=1
    )
    return (
        norm_gains[layer].astype(WIDE),
        shared,
        padded_to(taps, 8, taps.shape[1]),
        padded_to(own_part(head_params[layer], heads, 1), 8, LANES),
        own_part(mamba_gain[layer].astype(WIDE), channels, 0)[None],
    )


def layer_forward(hidden, weights, small, tables, place, sequences):
    zx_w, mix_w, mlp_w, mlp_out_w = weights
    gains, shared, taps, heads, gain = small
    rows = hidden.shape[0] // sequences
    channels = gain.shape[1]
    head_count = channels // HDIM
    normed = normalize(hidden, gains[0])
    projected = product(normed, zx_w)
    side = product(normed, shared)
    edge = jnp.concatenate(
        [projected[:, channels : 2 * channels], side[:, : 2 * STATE]], axis=1
    ).reshape(sequences, rows, -1)[:, rows - CONV + 1 :]
    came = shifted(edge.astype(LOW), "ctx", 1).astype(WIDE)
    rim = jnp.pad(came, ((0, 0), (8 - CONV + 1, 0), (0, 0)))
    queries, kv = split_qkv(projected, tables, rows, 2 * channels // (zx_w.shape[1] - 2 * channels))
    kv_list = [kv] + [shifted(kv, "ctx", by) for by in range(1, lax.axis_size("ctx"))]
    stk, x, bc, y_local, states, cum, step = scan_local(
        projected, side, rim, taps, heads, rows, channels
    )
    decays = jnp.exp(cum.reshape(sequences, rows, LANES)[:, -1])
    start = pass_states(states, decays, head_count, True)
    attended, log_total = attend(place, queries, kv_list, rows)
    y, mamba_norm = gate_tail(y_local, cum, bc, x, projected, start, heads, gain, rows)
    both = jnp.concatenate([mamba_norm, attended], axis=1)
    after_mix = hidden + tp_sum(against_rows(both, mix_w))
    normed_two = normalize(after_mix, gains[1])
    gate_up = product(normed_two, mlp_w)
    ff = gate_up.shape[1] // 2
    activated = (jax.nn.silu(gate_up[:, :ff]) * gate_up[:, ff:]).astype(LOW)
    result = after_mix + tp_sum(against_rows(activated, mlp_out_w))
    saved = (
        hidden, normed, projected, side, rim, queries, kv_list, stk, x, bc, cum, step, decays,
        start, log_total, y, both, after_mix, normed_two, gate_up, activated,
    )
    return result, saved


def layer_backward(upstream, saved, weights, small, tables, place, sequences):
    (
        hidden, normed, projected, side, rim, queries, kv_list, stk, x, bc, cum, step, decays,
        start, log_total, y, both, after_mix, normed_two, gate_up, activated,
    ) = saved
    zx_w, mix_w, mlp_w, mlp_out_w = weights
    gains, shared, taps, heads, gain = small
    rows = hidden.shape[0] // sequences
    channels = gain.shape[1]
    head_count = channels // HDIM
    grad_mlp = upstream.astype(LOW)
    grad_mlp_out = scatter_rows(over_rows(grad_mlp, activated))
    grad_act = product(grad_mlp, mlp_out_w)
    ff = grad_act.shape[1]
    gate_part, up_part = gate_up[:, :ff], gate_up[:, ff:]
    sigma = jax.nn.sigmoid(gate_part)
    grad_gu = jnp.concatenate(
        [
            grad_act * up_part * sigma * (1.0 + gate_part * (1.0 - sigma)),
            grad_act * gate_part * sigma,
        ],
        axis=1,
    ).astype(LOW)
    grad_mlp_in = scatter_rows(over_rows(normed_two, grad_gu))
    mid_part, grad_gain_two = norm_grad(
        after_mix, gains[1], tp_sum(against_rows(grad_gu, mlp_w))
    )
    grad_mid = upstream + mid_part
    grad_mix = grad_mid.astype(LOW)
    grad_mix_out = scatter_rows(over_rows(grad_mix, both))
    grad_norm = product(grad_mix, mix_w[:, :channels])
    grad_attended = product(grad_mix, mix_w[:, channels:]).astype(LOW)
    du, grad_gate, state_grads, tail_sums = gate_tail_back(
        grad_norm, y, cum, bc, x, projected, heads, gain, rows
    )
    later = pass_states(state_grads, decays, head_count, False)
    grad_q, own_kv, *sent_kv = attend_back(
        place, queries, grad_attended, log_total, tables, kv_list, rows
    )
    came_kv = [shifted(v, "ctx", -by) for by, v in enumerate(sent_kv, 1)]
    dstk, drim, grad_step, dtaps, dheads = scan_back(
        du, x, bc, stk, rim, cum, step, side, start, later, taps, heads, rows
    )
    returned = shifted(drim[:, 8 - CONV + 1 :], "ctx", -1)
    dstk = (
        dstk.reshape(sequences, rows, -1)
        + jnp.pad(returned, ((0, 0), (rows - CONV + 1, 0), (0, 0)))
    ).reshape(dstk.shape)
    grad_kv = finish_keys(own_kv, came_kv, tables, rows)
    grad_first = jnp.concatenate(
        [grad_gate, dstk[:, :channels].astype(LOW), grad_q, grad_kv], axis=1
    )
    grad_side = jnp.concatenate([dstk[:, channels:].astype(LOW), grad_step], axis=1)
    grad_in = scatter_rows(over_rows(normed, jnp.concatenate([grad_first, grad_side], axis=1)))
    below, grad_gain_one = norm_grad(
        hidden,
        gains[0],
        tp_sum(against_rows(grad_first, zx_w) + against_rows(grad_side, shared)),
    )
    tail_sums = jnp.sum(tail_sums, axis=0)
    dheads = jnp.sum(dheads, axis=0)
    skip_grad = jnp.sum(tail_sums[1].reshape(head_count, HDIM), axis=1)
    small_grads = (
        jnp.stack([grad_gain_one, grad_gain_two]),
        jnp.sum(dtaps, axis=0)[: CONV + 1],
        jnp.concatenate([dheads[:2, :head_count], skip_grad[None]], axis=0),
        tail_sums[0],
    )
    return grad_mid + below, (grad_in, grad_mix_out, grad_mlp_in, grad_mlp_out), small_grads


def settle_small(small_grads, side_grad, full_ssm, heads_total):
    gains, taps, heads, gain = small_grads
    channels = gain.shape[0]
    shapes = [v.shape for v in small_grads]
    flat = [jnp.pad(v.reshape(-1), (0, -v.size % LANES)) for v in small_grads]
    sizes = [v.shape[0] for v in flat]
    packed = sum_everywhere(jnp.concatenate(flat).reshape(-1, LANES)).reshape(-1)
    own = []
    first = 0
    for size, shape in zip(sizes, shapes):
        own.append(packed[first : first + math.prod(shape)].reshape(shape))
        first += size
    shifted_in = tp_peer(packed)
    peer = []
    first = 0
    for size, shape in zip(sizes, shapes):
        peer.append(shifted_in[first : first + math.prod(shape)].reshape(shape))
        first += size
    low_half = lax.axis_index("tp") == 0

    def ordered(a, b):
        return jnp.where(
            low_half, jnp.concatenate([a, b], axis=-1), jnp.concatenate([b, a], axis=-1)
        )

    gains_full = jnp.where(low_half, own[0], peer[0])
    taps_full = jnp.concatenate(
        [
            ordered(own[1][:, :channels], peer[1][:, :channels]),
            own[1][:, channels:] + peer[1][:, channels:],
        ],
        axis=1,
    )
    half_heads = heads_total // lax.axis_size("tp")
    side_peer = tp_peer(side_grad)
    side = jnp.concatenate(
        [
            side_grad[:, : 2 * STATE] + side_peer[:, : 2 * STATE],
            ordered(
                side_grad[:, 2 * STATE : 2 * STATE + half_heads],
                side_peer[:, 2 * STATE : 2 * STATE + half_heads],
            ),
        ],
        axis=1,
    )
    return (
        gains_full,
        join_rows(side),
        taps_full[:CONV],
        taps_full[CONV],
        ordered(own[2], peer[2]),
        ordered(own[3], peer[3]),
    )


def local(
    hidden_in, lengths, norm_gains, mamba_zx, mamba_shared, conv_weight, conv_bias, head_params,
    mamba_gain, mamba_out, attn_in, attn_out, mlp_in, mlp_out, out_grad,
):
    layers = norm_gains.shape[0]
    micro, own_seqs, rows, features = hidden_in.shape
    sequences = micro * own_seqs
    full_ssm = mamba_gain.shape[1]
    heads_total = head_params.shape[2]
    ctx_place = lax.axis_index("ctx")
    start_row = ctx_place * rows
    place = ctx_place.astype(jnp.int32).reshape(1)
    tables = turn_tables(start_row, rows)
    pieces = (mamba_zx, mamba_out, attn_in, attn_out, mlp_in, mlp_out)
    smalls = [
        local_small(l, norm_gains, mamba_shared, conv_weight, conv_bias, head_params, mamba_gain)
        for l in range(layers)
    ]
    weights = [fetch(l, pieces) for l in range(layers)]
    keep = (
        (start_row + jnp.arange(rows))[None, :] < lengths.reshape(sequences)[:, None]
    ).astype(WIDE).reshape(sequences * rows, 1)
    hidden = tp_join(hidden_in.reshape(sequences * rows, features)).astype(WIDE)
    upstream = tp_join(out_grad.reshape(sequences * rows, features)).astype(WIDE) * keep
    saved = []
    for l in range(layers):
        hidden, kept = layer_forward(hidden, weights[l], smalls[l], tables, place, sequences)
        saved.append(kept)
    mixed_out = own_part(hidden * keep, features, 1).astype(LOW).reshape(hidden_in.shape)
    big, rest = [None] * layers, [None] * layers
    for l in reversed(range(layers)):
        upstream, big[l], small_grads = layer_backward(
            upstream, saved[l], weights[l], smalls[l], tables, place, sequences
        )
        side_grad = big[l][0][:, -3 * LANES :]
        rest[l] = settle_small(small_grads, side_grad, full_ssm, heads_total)
    input_grad = own_part(upstream, features, 1).reshape(hidden_in.shape)

    def stacked(pick):
        return jnp.stack([pick(l) for l in range(layers)])

    zx_width = mamba_zx.shape[2] * mamba_zx.shape[3]
    attn_width = attn_in.shape[2] * attn_in.shape[3]
    channels = mamba_out.shape[1]
    return (
        mixed_out,
        input_grad,
        stacked(lambda l: rest[l][0]),
        stacked(lambda l: big[l][0][:, :zx_width]).reshape(mamba_zx.shape),
        stacked(lambda l: rest[l][1]),
        stacked(lambda l: rest[l][2]),
        stacked(lambda l: rest[l][3]),
        stacked(lambda l: rest[l][4]),
        stacked(lambda l: rest[l][5]),
        stacked(lambda l: big[l][1][:, :channels].T),
        stacked(lambda l: big[l][0][:, zx_width : zx_width + attn_width]).reshape(attn_in.shape),
        stacked(lambda l: big[l][1][:, channels:].T),
        stacked(lambda l: big[l][2]).reshape(mlp_in.shape),
        stacked(lambda l: big[l][3].T),
    )


def solution(mesh):
    placed = (
        P(None, "fsdp", "ctx", "tp"),
        P(None, "fsdp"),
        P(),
        P(None, ("fsdp", "ctx"), None, "tp"),
        P(),
        P(),
        P(),
        P(),
        P(),
        P(None, "tp", ("fsdp", "ctx")),
        P(None, ("fsdp", "ctx"), "tp", None),
        P(None, "tp", ("fsdp", "ctx")),
        P(None, ("fsdp", "ctx"), None, "tp"),
        P(None, "tp", ("fsdp", "ctx")),
        P(None, "fsdp", "ctx", "tp"),
    )
    return jax.shard_map(
        local,
        mesh=mesh,
        in_specs=placed,
        out_specs=(
            P(None, "fsdp", "ctx", "tp"),
            P(None, "fsdp", "ctx", "tp"),
            P(),
            P(None, ("fsdp", "ctx"), None, "tp"),
            P(),
            P(),
            P(),
            P(),
            P(),
            P(None, "tp", ("fsdp", "ctx")),
            P(None, ("fsdp", "ctx"), "tp", None),
            P(None, "tp", ("fsdp", "ctx")),
            P(None, ("fsdp", "ctx"), None, "tp"),
            P(None, "tp", ("fsdp", "ctx")),
        ),
        check_vma=False,
    )
```

```python
import functools
import math

import jax
import jax.numpy as jnp
from jax import lax
from jax.experimental import pallas as pl
from jax.experimental.pallas import tpu as pltpu
from jax.sharding import PartitionSpec as P

HDIM = 64
STATE = 128
CONV = 4
ADIM = 64
GROUP = 4
LANES = 128
EPSILON = 1e-05
THETA = 100000000000.0
HIGHEST = lax.Precision.HIGHEST
LOW = jnp.bfloat16
WIDE = jnp.float32
MASKED = -1e30
VMEM_LIMIT = 56 * 1024 * 1024
PARCEL_ROWS = 16


def dot(a, b, ca=1, cb=0, precision=None):
    return lax.dot_general(
        a, b, (((ca,), (cb,)), ((), ())), preferred_element_type=WIDE, precision=precision
    )


def lane_iota(shape):
    return lax.broadcasted_iota(jnp.int32, shape, len(shape) - 1)


def row_iota(shape):
    return lax.broadcasted_iota(jnp.int32, shape, 0)


def kernel_call(body, grid, in_specs, out_specs, out_shape, scratch=(), flops=0, moved=0):
    return pl.pallas_call(
        body,
        grid=grid,
        in_specs=in_specs,
        out_specs=out_specs,
        out_shape=out_shape,
        scratch_shapes=list(scratch),
        compiler_params=pltpu.CompilerParams(vmem_limit_bytes=VMEM_LIMIT),
        cost_estimate=pl.CostEstimate(flops=flops, bytes_accessed=moved, transcendentals=0),
    )


def whole(shape):
    return pl.BlockSpec(shape, lambda s: (0,) * len(shape))


def rows_block(rows, cols, col=0):
    return pl.BlockSpec((rows, cols), lambda s: (s, col))


def sequence_block(*shape):
    return pl.BlockSpec((None,) + shape, lambda s: (s,) + (0,) * len(shape))


def xor_pairs(count, bit):
    return [(i, i ^ bit) for i in range(count)]


def next_half(x, forward):
    firsts = range(0, lax.axis_size("ctx"), 2)
    return lax.ppermute(x, "ctx", [(i, i + 1) if forward else (i + 1, i) for i in firsts])


STRAIGHT = ((0, 0), (2, 1), (1, 2), (3, 3))
CROSSED = ((1, 0), (3, 1), (0, 2), (2, 3))


def to_halves_moves(quarters):
    place = lax.axis_index("ctx")
    a = lax.ppermute(pick(quarters, place % 2, 0), "ctx", STRAIGHT)
    b = lax.ppermute(pick(quarters, 1 - place % 2, 0), "ctx", CROSSED)
    return a, b


def to_halves(a, b):
    place = lax.axis_index("ctx")
    return jnp.where(place < 2, jnp.concatenate([a, b]), jnp.concatenate([b, a]))


def to_quarters(half):
    place = lax.axis_index("ctx")
    parts = half.reshape((2, -1) + half.shape[1:])
    late = place // 2
    a = lax.ppermute(pick(parts, late, 0), "ctx", [(j, i) for i, j in STRAIGHT])
    b = lax.ppermute(pick(parts, 1 - late, 0), "ctx", [(j, i) for i, j in CROSSED])
    return jnp.where(place % 2 == 0, jnp.stack([a, b]), jnp.stack([b, a]))


def tp_peer(x):
    return lax.ppermute(x, "tp", xor_pairs(lax.axis_size("tp"), 1))


def tp_join(x):
    peer = tp_peer(x)
    first = lax.axis_index("tp") == 0
    return jnp.where(
        first, jnp.concatenate([x, peer], axis=-1), jnp.concatenate([peer, x], axis=-1)
    )


def tp_sum(partial_sum):
    low = partial_sum.astype(LOW)
    peer = tp_peer(low)
    return low.astype(WIDE) + peer.astype(WIDE)


def bits_of(axis):
    return [1 << i for i in range(lax.axis_size(axis).bit_length() - 1)]


def together(values, anchor):
    return lax.optimization_barrier((tuple(values), anchor))


def added(*parts):
    total = parts[0].astype(WIDE)
    for part in parts[1:]:
        total = total + part.astype(WIDE)
    return total


def ctx_swap(values, step):
    return lax.ppermute(values, "ctx", xor_pairs(lax.axis_size("ctx"), step))


def pick(values, place, dim):
    return lax.dynamic_index_in_dim(values, place, dim, False)


def half_lanes(width):
    return width // 256 * 128


FLIPS = (0, 1, 3, 2)


def own_order(features, dtype):
    fsdp, ctx = lax.axis_size("fsdp"), lax.axis_size("ctx")
    rows = features // (fsdp * ctx)
    own = jnp.arange(features)
    flip, rest = jnp.array(FLIPS)[own // (fsdp * rows)], own % (fsdp * rows)
    common = (rest // rows) * ctx * rows + (flip ^ lax.axis_index("ctx")) * rows + rest % rows
    return (jnp.arange(features)[:, None] == common[None, :]).astype(dtype)


def spread_first(block):
    return ctx_swap(block, 1), ctx_swap(block, 2)


def spread_parts(came):
    cut = half_lanes(came[0].shape[-1])
    return came[0][..., :cut], came[1][..., cut:]


def spread_second(parts):
    return ctx_swap(parts[0], 2), ctx_swap(parts[1], 1)


def spread_whole(block, came, far):
    width = block.shape[-1]
    return jnp.concatenate(
        [v.reshape(-1, width) for v in (block, came[0], jnp.concatenate(far, axis=-1), came[1])], axis=0
    )


def fsdp_moves(piece):
    count = lax.axis_size("fsdp")
    if count > 4:
        return ()
    return tuple(lax.ppermute(piece, "fsdp", xor_pairs(count, step)) for step in range(1, count))


def fsdp_join(piece, came):
    if not came:
        return lax.all_gather(piece, "fsdp", axis=0)
    place = lax.axis_index("fsdp")
    shape = (len(came) + 1,) + piece.shape
    out = lax.dynamic_update_index_in_dim(jnp.zeros(shape, piece.dtype), piece, place, 0)
    for step, values in enumerate(came, 1):
        out = lax.dynamic_update_index_in_dim(out, values, place ^ step, 0)
    return out


def gathered_blocks(pieces, anchor):
    following, anchor = together((pieces[1], jnp.concatenate(pieces[2:], axis=1)), anchor)
    blocks = [lax.all_gather(following[0], "fsdp", axis=0)]
    rest = lax.all_gather(following[1], "fsdp", axis=0)
    first = 0
    for piece in pieces[2:]:
        blocks.append(rest[..., first : first + piece.shape[1]])
        first += piece.shape[1]
    return blocks, anchor


class Gathers:
    def __init__(self, blocks):
        self.blocks = blocks
        self.near = [None] * len(blocks)
        self.far = [None] * len(blocks)
        self.first = 0
        self.near[0] = spread_first(self.blocks[0])

    def step(self, anchor):
        i = self.first
        if i >= len(self.blocks):
            return anchor
        self.near[i], anchor = together(self.near[i], anchor)
        parts = spread_parts(self.near[i])
        self.far[i] = spread_second(parts)
        _, anchor = together(parts, anchor)
        self.first = i + 1
        return anchor

    def begin(self, anchor):
        i = self.first
        if i < len(self.blocks) and self.near[i] is None:
            (self.blocks[i],), anchor = together((self.blocks[i],), anchor)
            self.near[i] = spread_first(self.blocks[i])
        return anchor

    def take(self, i):
        if self.first <= i:
            self.step(self.near[i][0])
        return spread_whole(self.blocks[i], self.near[i], self.far[i])


def gathered_ctx(block, near, count):
    far = spread_second(spread_parts(near))
    rows = spread_whole(block, near, far).reshape((4,) + block.shape[1:])
    width = rows.shape[-1] // count
    return [rows[..., i * width : (i + 1) * width] for i in range(count)]


def table_body(spans, *refs):
    count = len(spans)
    left_refs, a_refs, b_refs = (refs[i * count : (i + 1) * count] for i in range(3))
    up_ref, across_ref, x_ref, y_ref, own_a_ref, own_b_ref, turned_ref = refs[3 * count :]
    size = own_a_ref.shape[0]
    place = pl.program_id(0)
    for left_ref, a_ref, b_ref, (first, last) in zip(left_refs, a_refs, b_refs, spans):

        @pl.when(place == first)
        def _(left_ref=left_ref):
            turned_ref[...] = left_ref[...].astype(WIDE).T.astype(LOW)

        @pl.when((place >= first) & (place < last))
        def _(a_ref=a_ref, b_ref=b_ref):
            table = dot(turned_ref[...], a_ref[...]).astype(LOW)
            own_a_ref[...] = table[:size]
            x_ref[...] = table[size : 2 * size]
            up_ref[...] = table[2 * size :]
            table = dot(turned_ref[...], b_ref[...]).astype(LOW)
            own_b_ref[...] = table[:size]
            across_ref[...] = table[size : 3 * size]
            y_ref[...] = table[3 * size :]


def tables(pairs, tile):
    rows, features = pairs[0][0].shape
    size = features // len(FLIPS)
    spans, first = [], 0
    for _, right in pairs:
        spans.append((first, first + right.shape[1] // (2 * tile)))
        first = spans[-1][1]
    width = first * tile

    def columns(first, last, skip):
        return pl.BlockSpec(
            (rows, tile), lambda j: (0, skip + jnp.clip(j, first, last - 1) - first)
        )

    def tall(height):
        return pl.BlockSpec((height, tile), lambda j: (0, j))

    heights = (2 * size, 2 * size, size, size, size, size)
    return kernel_call(
        functools.partial(table_body, tuple(spans)),
        (first,),
        [whole((rows, features))] * len(pairs)
        + [columns(*span, 0) for span in spans]
        + [columns(*span, span[1] - span[0]) for span in spans],
        [tall(h) for h in heights],
        [jax.ShapeDtypeStruct((h, width), LOW) for h in heights],
        [pltpu.VMEM((features, rows), LOW)],
        flops=4 * rows * features * width,
        moved=width * (4 * rows + 4 * features),
    )(*[p[0] for p in pairs], *[p[1] for p in pairs], *[p[1] for p in pairs])


def fsdp_table_body(left_ref, right_ref, out_ref, turned_ref):
    @pl.when(pl.program_id(0) == 0)
    def _():
        turned_ref[...] = left_ref[...].astype(WIDE).T.astype(LOW)

    table = dot(turned_ref[...], right_ref[...])
    fsdp, flips, rows, _ = out_ref.shape
    for flip in range(flips):
        for place in range(fsdp):
            first = (flip * fsdp + place) * rows
            out_ref[place, flip] = table[first : first + rows].astype(LOW)


def fsdp_table(left, right, tile):
    rows, features = left.shape
    width = right.shape[1]
    fsdp, flips = lax.axis_size("fsdp"), len(FLIPS)
    shape = (fsdp, flips, features // (fsdp * flips))
    return kernel_call(
        fsdp_table_body,
        (width // tile,),
        [whole((rows, features)), pl.BlockSpec((rows, tile), lambda j: (0, j))],
        pl.BlockSpec(shape + (tile,), lambda j: (0, 0, 0, j)),
        jax.ShapeDtypeStruct(shape + (width,), LOW),
        [pltpu.VMEM((features, rows), LOW)],
        flops=2 * rows * features * width,
        moved=width * (2 * rows + 2 * features),
    )(left, right)


def pass_body(x_ref, y_ref, from_y_ref, from_x_ref, to_x_ref, to_y_ref):
    size = x_ref.shape[0]
    to_x_ref[...] = (x_ref[...].astype(WIDE) + from_y_ref[:size].astype(WIDE)).astype(LOW)
    to_y_ref[...] = (y_ref[...].astype(WIDE) + from_x_ref[size:].astype(WIDE)).astype(LOW)


def keep_body(own_a_ref, own_b_ref, from_y_ref, from_x_ref, last_x_ref, last_y_ref, out_ref):
    size, width = own_a_ref.shape
    out_ref[:, :width] = (
        own_a_ref[...].astype(WIDE) + from_y_ref[size:].astype(WIDE) + last_x_ref[...].astype(WIDE)
    ).astype(LOW)
    out_ref[:, width:] = (
        own_b_ref[...].astype(WIDE) + from_x_ref[:size].astype(WIDE) + last_y_ref[...].astype(WIDE)
    ).astype(LOW)


def once(body, out_shapes, *operands):
    outs = [jax.ShapeDtypeStruct(shape, LOW) for shape in out_shapes]
    return kernel_call(
        body,
        (1,),
        [whole(v.shape) for v in operands],
        [whole(shape) for shape in out_shapes],
        outs,
        moved=sum(v.size * 2 for v in operands) + sum(2 * math.prod(x) for x in out_shapes),
    )(*operands)


def ctx_scatter(cuts, waits):
    up, across, x, y, own_a, own_b = cuts
    from_y, from_x = yield (ctx_swap(up, 2), ctx_swap(across, 1)), waits[0], (up, across)
    to_x, to_y = once(pass_body, (x.shape, y.shape), x, y, from_y, from_x)
    last_x, last_y = yield (ctx_swap(to_x, 1), ctx_swap(to_y, 2)), waits[1], (to_x, to_y)
    size, width = own_a.shape
    (out,) = once(keep_body, ((size, 2 * width),), own_a, own_b, from_y, from_x, last_x, last_y)
    return out


def fsdp_scatter(table, direct):
    count = lax.axis_size("fsdp")
    if count > 4 or not direct:
        total = lax.psum_scatter(table, "fsdp", scatter_dimension=0, tiled=False)
        if direct is None:
            (total,) = yield (total,), 0, (table,)
        else:
            yield (), 0, (table,)
        return total.astype(WIDE)
    place = lax.axis_index("fsdp")
    came = tuple(
        lax.ppermute(pick(table, place ^ step, 0), "fsdp", xor_pairs(count, step))
        for step in range(1, count)
    )
    came = yield came, 0, (table,)
    return added(pick(table, place, 0), *came)


class Scatters:
    def __init__(self):
        self.active = []

    def add(self, pairs, tile, direct, waits, done):
        cuts = tables(pairs, tile)

        def run():
            part = yield from ctx_scatter(cuts, waits)
            fsdp = lax.axis_size("fsdp")
            part = part.reshape(fsdp, -1, part.shape[1])
            done((yield from fsdp_scatter(part, direct)))

        self.begin(run())
        return cuts[0]

    def add_fsdp_first(self, left, right, waits, done):
        table = fsdp_table(left, right, 256)
        fsdp, flips, rows, width = table.shape

        def run():
            moved = table.reshape(fsdp, flips * rows, width)
            total = lax.psum_scatter(moved, "fsdp", scatter_dimension=0, tiled=False)
            (total,) = yield (total,), waits, (moved,)
            cut = half_lanes(width)
            own, x, far, y = (total[i * rows : (i + 1) * rows] for i in range(flips))
            cuts = (
                total[2 * rows :, :cut],
                total[rows : 3 * rows, cut:],
                x[:, :cut],
                y[:, cut:],
                own[:, :cut],
                own[:, cut:],
            )
            done((yield from ctx_scatter(cuts, (0, 0))).astype(WIDE))

        self.begin(run())
        return table

    def begin(self, work):
        self.active.append([work, *next(work)])

    def step(self, anchor):
        ready = [item for item in self.active if anchor is None or item[2] == 0]
        for item in self.active:
            item[2] = max(item[2] - 1, 0)
        values = [v for item in ready for v in item[1]]
        if anchor is not None:
            values, anchor = together(values, anchor)
        elif values:
            values = lax.optimization_barrier(tuple(values))
        first, sent = 0, ()
        for item in ready:
            came = tuple(values[first : first + len(item[1])])
            first += len(item[1])
            try:
                item[1:] = item[0].send(came)
                sent += item[3]
            except StopIteration:
                self.active.remove(item)
        if sent and anchor is not None:
            _, anchor = together(sent, anchor)
        return anchor

    def finish(self):
        while self.active:
            self.step(None)


def join_rows(piece):
    v = piece[None, None]
    for dim, axis in enumerate(("fsdp", "ctx")):
        place = lax.axis_index(axis)
        for step in bits_of(axis):
            (came,) = yield (lax.ppermute(v, axis, xor_pairs(lax.axis_size(axis), step)),), 0, ()
            v = jnp.where(
                (place & step) == 0,
                jnp.concatenate([v, came], axis=dim),
                jnp.concatenate([came, v], axis=dim),
            )
    return v


def sum_everywhere(v):
    for axis in ("fsdp", "ctx"):
        for step in bits_of(axis):
            (came,) = yield (lax.ppermute(v, axis, xor_pairs(lax.axis_size(axis), step)),), 0, ()
            v = v + came
    return v


def turn_tables(start_row, rows):
    half = ADIM // 2
    places = (start_row + jnp.arange(rows)).astype(WIDE)
    rates = jnp.exp(-math.log(THETA) * jnp.arange(half).astype(WIDE) / half)
    angles = places[:, None] * rates[None, :]
    cosine, sine = jnp.cos(angles), jnp.sin(angles)
    one_cos = jnp.concatenate([cosine, cosine], axis=1)
    one_sin = jnp.concatenate([-sine, sine], axis=1)
    still = jnp.ones_like(one_cos)
    return (
        jnp.concatenate([one_cos, one_cos, one_cos, still], axis=1),
        jnp.concatenate([one_sin, one_sin, one_sin, jnp.zeros_like(one_sin)], axis=1),
    )


def turned(values, cosine, sine):
    lanes = lane_iota(values.shape) % ADIM
    swapped = jnp.where(
        lanes < ADIM // 2,
        pltpu.roll(values, LANES - ADIM // 2, 1),
        pltpu.roll(values, ADIM // 2, 1),
    )
    return values * cosine + swapped * sine


def qkv_body(rows_ref, cos_ref, sin_ref, q_ref, kv_ref):
    for pair in range(GROUP // 2):
        lanes = slice(pair * LANES, (pair + 1) * LANES)
        q_ref[:, lanes] = turned(
            rows_ref[:, lanes], cos_ref[:, :LANES], sin_ref[:, :LANES]
        ).astype(LOW)
    width = GROUP * ADIM
    kv_ref[...] = turned(
        rows_ref[:, width : width + LANES], cos_ref[:, LANES:], sin_ref[:, LANES:]
    ).astype(LOW)


def split_qkv(projected, tables, rows, column):
    total = projected.shape[0]
    width = GROUP * ADIM
    return kernel_call(
        qkv_body,
        (total // rows,),
        [rows_block(rows, width + LANES, column)] + [rows_block(rows, 2 * LANES)] * 2,
        [rows_block(rows, width), rows_block(rows, LANES)],
        [
            jax.ShapeDtypeStruct((total, width), LOW),
            jax.ShapeDtypeStruct((total, LANES), LOW),
        ],
        flops=total * 400 * 4,
        moved=total * 384 * 6,
    )(projected, *tables)


def head_lanes(values, head):
    pair = values[:, head // 2 * LANES : (head // 2 + 1) * LANES]
    if head % 2:
        pair = pltpu.roll(pair, ADIM, 1)
    return jnp.where(lane_iota(pair.shape) < ADIM, pair, jnp.zeros_like(pair))


def seen_keys(place, rows, total):
    shape = (rows, 2 * total)
    column = lane_iota(shape)
    own = (column < total) & (column <= row_iota(shape) + pl.program_id(0) * rows)
    return own | ((column >= total) & (column < total * (1 + place)))


def attend_body(place_ref, q_ref, own_ref, came_ref, out_ref, total_ref, keys):
    rows, total = q_ref.shape[0], own_ref.shape[0]
    keys[:total, :] = own_ref[...]
    keys[total:, :] = came_ref[...]
    seen = seen_keys(place_ref[0], rows, total)
    q_all = q_ref[...].astype(WIDE)
    all_keys = keys[...]
    totals = jnp.zeros((rows, LANES), WIDE)
    lanes = lane_iota((rows, LANES))
    outs = []
    for head in range(GROUP):
        query = head_lanes(q_all, head).astype(LOW)
        scores = jnp.where(seen, dot(query, all_keys, 1, 1) * ADIM**-0.5, MASKED)
        top = jnp.max(scores, axis=1, keepdims=True)
        raised = jnp.exp(scores - top)
        row_total = jnp.sum(raised, axis=1, keepdims=True)
        weights = (raised * (1.0 / row_total)).astype(LOW)
        outs.append(dot(weights, all_keys))
        totals = jnp.where(lanes == head, top + jnp.log(row_total), totals)
    total_ref[...] = totals
    for pair in range(GROUP // 2):
        first = pltpu.roll(outs[2 * pair], ADIM, 1)
        out_ref[:, pair * LANES : (pair + 1) * LANES] = jnp.where(
            lanes < ADIM, first, outs[2 * pair + 1]
        ).astype(LOW)


def attend(place, queries, own, came, rows):
    total, width = queries.shape
    return kernel_call(
        attend_body,
        (total // rows,),
        [
            pl.BlockSpec(memory_space=pltpu.SMEM),
            rows_block(rows, width),
            whole((total, LANES)),
            whole((total, LANES)),
        ],
        [rows_block(rows, width), rows_block(rows, LANES)],
        [
            jax.ShapeDtypeStruct((total, width), LOW),
            jax.ShapeDtypeStruct((total, LANES), WIDE),
        ],
        [pltpu.VMEM((2 * total, LANES), LOW)],
        flops=total * total * 2 * GROUP * LANES * 4,
        moved=total * (width * 4 + LANES * 12),
    )(place, queries, own, came)


def attend_back_body(
    place_ref, q_ref, grad_ref, total_ref, cos_ref, sin_ref, own_ref, came_ref,
    dq_ref, own_grad_ref, came_grad_ref, keys, grads,
):
    rows, total = q_ref.shape[0], own_ref.shape[0]
    keys[:total, :] = own_ref[...]
    keys[total:, :] = came_ref[...]
    seen = seen_keys(place_ref[0], rows, total)
    q_all = q_ref[...].astype(WIDE)
    grad_all = grad_ref[...].astype(WIDE)
    all_keys = keys[...]
    lanes = lane_iota((rows, LANES))
    grad_kv = None
    dqs = []
    for head in range(GROUP):
        query = head_lanes(q_all, head).astype(LOW)
        upper = pltpu.roll(head_lanes(grad_all, head), ADIM, 1).astype(LOW)
        scores = jnp.where(seen, dot(query, all_keys, 1, 1) * ADIM**-0.5, MASKED)
        probs = jnp.exp(scores - total_ref[:, head : head + 1])
        grad_probs = dot(upper, all_keys, 1, 1)
        inner = jnp.sum(probs * grad_probs, axis=1, keepdims=True)
        grad_scores = (probs * (grad_probs - inner)).astype(LOW)
        dqs.append(dot(grad_scores, all_keys) * ADIM**-0.5)
        fresh = dot(grad_scores, query, 0, 0) * ADIM**-0.5 + dot(
            probs.astype(LOW), upper, 0, 0
        )
        grad_kv = fresh if grad_kv is None else grad_kv + fresh
    for pair in range(GROUP // 2):
        both = jnp.where(lanes < ADIM, dqs[2 * pair], pltpu.roll(dqs[2 * pair + 1], ADIM, 1))
        dq_ref[:, pair * LANES : (pair + 1) * LANES] = turned(
            both, cos_ref[:, :LANES], -sin_ref[:, :LANES]
        ).astype(LOW)
    place = pl.program_id(0)

    @pl.when(place == 0)
    def _():
        grads[...] = grad_kv

    @pl.when(place > 0)
    def _():
        grads[...] += grad_kv

    own_grad_ref[...] = grads[:total, :]
    came_grad_ref[...] = grads[total:, :].astype(LOW)


def attend_back(place, queries, grad_out, log_total, tables, own, came, rows):
    total, width = queries.shape
    return kernel_call(
        attend_back_body,
        (total // rows,),
        [
            pl.BlockSpec(memory_space=pltpu.SMEM),
            rows_block(rows, width),
            rows_block(rows, width),
            rows_block(rows, LANES),
            rows_block(rows, 2 * LANES),
            rows_block(rows, 2 * LANES),
            whole((total, LANES)),
            whole((total, LANES)),
        ],
        [rows_block(rows, width), whole((total, LANES)), whole((total, LANES))],
        [
            jax.ShapeDtypeStruct((total, width), LOW),
            jax.ShapeDtypeStruct((total, LANES), WIDE),
            jax.ShapeDtypeStruct((total, LANES), LOW),
        ],
        [pltpu.VMEM((2 * total, LANES), LOW), pltpu.VMEM((2 * total, LANES), WIDE)],
        flops=total * total * 2 * GROUP * LANES * 10,
        moved=total * (width * 6 + LANES * 20),
    )(place, queries, grad_out, log_total, *tables, own, came)


def key_body(own_ref, *refs):
    came, (cos_ref, sin_ref, out_ref) = refs[:-3], refs[-3:]
    values = own_ref[...]
    for ref in came:
        values = values + ref[...].astype(WIDE)
    out_ref[...] = turned(values, cos_ref[:, LANES:], -sin_ref[:, LANES:]).astype(LOW)


def finish_keys(own, came, tables, rows):
    total = own.shape[0]
    return kernel_call(
        key_body,
        (total // rows,),
        [rows_block(rows, LANES)] * (1 + len(came)) + [rows_block(rows, 2 * LANES)] * 2,
        rows_block(rows, LANES),
        jax.ShapeDtypeStruct((total, LANES), LOW),
        flops=total * LANES * 10,
        moved=total * LANES * 12,
    )(own, *came, *tables)


def sigmoid(v):
    return 1.0 / (1.0 + jnp.exp(-v))


def softplus(v):
    return jnp.maximum(v, 0.0) + jnp.log1p(jnp.exp(-jnp.abs(v)))


def over_pair(values, pair, shape):
    first = values[:, 2 * pair : 2 * pair + 1]
    second = values[:, 2 * pair + 1 : 2 * pair + 2]
    return jnp.where(lane_iota(shape) < HDIM, first, second)


def down_pair(values, pair):
    shape = (LANES, LANES)
    first = jnp.broadcast_to(values[:, 2 * pair : 2 * pair + 1], shape)
    second = jnp.broadcast_to(values[:, 2 * pair + 1 : 2 * pair + 2], shape)
    return jnp.where(row_iota(shape) < HDIM, first, second)


def lower_ones(rows, flip):
    shape = (rows, rows)
    t, s = row_iota(shape), lane_iota(shape)
    return jnp.where((t <= s) if flip else (t >= s), 1.0, 0.0).astype(WIDE)


def convolved(padded, taps_ref, rows):
    total = taps_ref[CONV : CONV + 1, :]
    for j in range(CONV):
        first = 8 - CONV + 1 + j
        total = total + taps_ref[j : j + 1, :] * padded[first : first + rows, :]
    return total


def scan_body(
    zx_ref, side_ref, rim_ref, taps_ref, heads_ref,
    stk_ref, x_ref, bc_ref, y_ref, first_ref, parcel_ref, cum_ref, all_ref, step_ref,
    padded, state, before_it,
):
    rows, channels = zx_ref.shape
    heads = channels // HDIM
    place = pl.program_id(0)

    @pl.when(place == 0)
    def _():
        padded[0:8, :] = rim_ref[...]
        state[...] = jnp.zeros(state.shape, WIDE)
        before_it[...] = jnp.zeros(before_it.shape, WIDE)

    @pl.when(place > 0)
    def _():
        padded[0:8, :] = padded[rows : rows + 8, :]

    stk_ref[:, :channels] = zx_ref[...].astype(LOW)
    stk_ref[:, channels:] = side_ref[:, : 2 * STATE].astype(LOW)
    padded[8 : 8 + rows, :] = stk_ref[...].astype(WIDE)
    before = convolved(padded, taps_ref, rows)
    active = (before * sigmoid(before)).astype(LOW)
    x_ref[...] = active[:, :channels]
    bc_ref[...] = active[:, channels:]
    step = softplus(side_ref[:, 2 * STATE :] + heads_ref[1:2, :])
    cum = dot(lower_ones(rows, False), -step * jnp.exp(heads_ref[0:1, :]), precision=HIGHEST)
    step_ref[...] = step
    cum_ref[...] = cum
    all_ref[...] = cum + before_it[0:1, :]
    cum_rows, step_rows = cum.T, step.T
    last = cum[rows - 1 : rows, :]
    before_it[...] = jnp.broadcast_to(before_it[0:1, :] + last, before_it.shape)
    tail = jnp.exp(last - cum) * step
    grown, faded = jnp.exp(cum), jnp.exp(last)
    entry, readout = bc_ref[:, :STATE], bc_ref[:, STATE:]
    cross = dot(readout, entry, 1, 1)
    shape = (rows, rows)
    causal = row_iota(shape) >= lane_iota(shape)
    lanes = lane_iota((rows, LANES))
    for pair in range(heads // 2):
        block = slice(pair * LANES, (pair + 1) * LANES)
        inputs = x_ref[:, block]
        outs = []
        for head in (2 * pair, 2 * pair + 1):
            gap = cum[:, head : head + 1] - cum_rows[head : head + 1, :]
            decay = jnp.exp(jnp.where(causal, gap, MASKED))
            mixed = (decay * cross * step_rows[head : head + 1, :]).astype(LOW)
            outs.append(dot(mixed, inputs))
        carried = dot(readout, state[block, :].astype(LOW), 1, 1)
        y_ref[:, block] = jnp.where(lanes < HDIM, outs[0], outs[1]) + carried * over_pair(
            grown, pair, (rows, LANES)
        )
        scaled = (over_pair(tail, pair, (rows, LANES)) * inputs.astype(WIDE)).astype(LOW)
        fresh = down_pair(faded, pair) * state[block, :] + dot(scaled, entry, 0, 0)
        state[block, :] = fresh
        parcel_ref[block, :] = fresh.astype(LOW)
    write_decays(parcel_ref, channels, before_it[0:1, :])

    @pl.when(place == 0)
    def _():
        first_ref[...] = state[...]


def scan_local(projected, side, rim, taps, heads, rows, channels):
    total = projected.shape[0]
    count = total // rows
    width = channels + 2 * STATE
    return kernel_call(
        scan_body,
        (count,),
        [
            rows_block(rows, channels, 1),
            rows_block(rows, side.shape[1]),
            whole((8, width)),
            whole((8, width)),
            whole((8, LANES)),
        ],
        [
            rows_block(rows, width),
            rows_block(rows, channels),
            rows_block(rows, 2 * STATE),
            rows_block(rows, channels),
            whole((channels, STATE)),
            whole((channels + PARCEL_ROWS, STATE)),
            rows_block(rows, LANES),
            rows_block(rows, LANES),
            rows_block(rows, LANES),
        ],
        [
            jax.ShapeDtypeStruct((total, width), LOW),
            jax.ShapeDtypeStruct((total, channels), LOW),
            jax.ShapeDtypeStruct((total, 2 * STATE), LOW),
            jax.ShapeDtypeStruct((total, channels), WIDE),
            jax.ShapeDtypeStruct((channels, STATE), WIDE),
            jax.ShapeDtypeStruct((channels + PARCEL_ROWS, STATE), LOW),
            jax.ShapeDtypeStruct((total, LANES), WIDE),
            jax.ShapeDtypeStruct((total, LANES), WIDE),
            jax.ShapeDtypeStruct((total, LANES), WIDE),
        ],
        [
            pltpu.VMEM((rows + 8, width), WIDE),
            pltpu.VMEM((channels, STATE), WIDE),
            pltpu.VMEM((8, LANES), WIDE),
        ],
        flops=total * rows * channels * 8,
        moved=total * width * 16,
    )(projected, side, rim, taps, heads)


def tail_body(
    y_ref, cum_ref, bc_ref, x_ref, gate_ref, heads_ref, gain_ref, parcel_ref, out_ref, norm_ref
):
    rows, channels = y_ref.shape
    readout = bc_ref[:, STATE:]
    grown = jnp.exp(cum_ref[...])
    square = jnp.zeros((rows, 1), WIDE)
    for pair in range(channels // LANES):
        block = slice(pair * LANES, (pair + 1) * LANES)
        carried = dot(readout, parcel_ref[block, :], 1, 1)
        y = y_ref[:, block] + over_pair(grown, pair, carried.shape) * carried
        out_ref[:, block] = y
        skip = over_pair(heads_ref[2:3, :], pair, (1, LANES))
        gate = gate_ref[:, block]
        mixed = (y + skip * x_ref[:, block].astype(WIDE)) * (gate * sigmoid(gate))
        square = square + jnp.sum(mixed * mixed, axis=1, keepdims=True)
    scale = lax.rsqrt(square * (1.0 / channels) + EPSILON)
    for pair in range(channels // LANES):
        block = slice(pair * LANES, (pair + 1) * LANES)
        skip = over_pair(heads_ref[2:3, :], pair, (1, LANES))
        gate = gate_ref[:, block]
        mixed = (out_ref[:, block] + skip * x_ref[:, block].astype(WIDE)) * (gate * sigmoid(gate))
        norm_ref[:, block] = (mixed * scale * gain_ref[:, block]).astype(LOW)


def gate_tail(y, cum, bc, x, projected, heads, gain, parcel, rows):
    total, channels = y.shape
    return kernel_call(
        tail_body,
        (total // rows,),
        [
            rows_block(rows, channels),
            rows_block(rows, LANES),
            rows_block(rows, 2 * STATE),
            rows_block(rows, channels),
            rows_block(rows, channels, 0),
            whole((8, LANES)),
            whole((1, channels)),
            whole((channels + PARCEL_ROWS, STATE)),
        ],
        [rows_block(rows, channels), rows_block(rows, channels)],
        [
            jax.ShapeDtypeStruct((total, channels), WIDE),
            jax.ShapeDtypeStruct((total, channels), LOW),
        ],
        flops=total * channels * (2 * STATE + 40),
        moved=total * channels * 18,
    )(y, cum, bc, x, projected, heads, gain, parcel)


def tail_back_body(
    dn_ref, y_ref, cum_ref, bc_ref, x_ref, gate_ref, heads_ref, gain_ref,
    du_ref, dgate_ref, parcel_ref, sums_ref, state,
):
    @pl.when(pl.program_id(0) == 0)
    def _():
        state[...] = jnp.zeros(state.shape, WIDE)

    rows, channels = y_ref.shape
    readout = bc_ref[:, STATE:]
    grown = jnp.exp(cum_ref[...])
    square = jnp.zeros((rows, 1), WIDE)
    inner = jnp.zeros((rows, 1), WIDE)
    for pair in range(channels // LANES):
        block = slice(pair * LANES, (pair + 1) * LANES)
        skip = over_pair(heads_ref[2:3, :], pair, (1, LANES))
        gate = gate_ref[:, block]
        mixed = (y_ref[:, block] + skip * x_ref[:, block].astype(WIDE)) * (gate * sigmoid(gate))
        square = square + jnp.sum(mixed * mixed, axis=1, keepdims=True)
        inner = inner + jnp.sum(
            dn_ref[:, block] * gain_ref[:, block] * mixed, axis=1, keepdims=True
        )
    scale = lax.rsqrt(square * (1.0 / channels) + EPSILON)
    inner = inner * scale * (1.0 / channels)
    sums_ref[...] = jnp.zeros(sums_ref.shape, WIDE)
    for pair in range(channels // LANES):
        block = slice(pair * LANES, (pair + 1) * LANES)
        skip = over_pair(heads_ref[2:3, :], pair, (1, LANES))
        gate = gate_ref[:, block]
        inputs = x_ref[:, block].astype(WIDE)
        sigma = sigmoid(gate)
        value = y_ref[:, block] + skip * inputs
        unit = value * (gate * sigma) * scale
        upstream = dn_ref[:, block]
        dmixed = scale * (upstream * gain_ref[:, block] - unit * inner)
        du = dmixed * gate * sigma
        du_ref[:, block] = du
        dgate_ref[:, block] = (
            dmixed * value * (sigma * (1.0 + gate * (1.0 - sigma)))
        ).astype(LOW)
        sums_ref[0:1, block] = jnp.sum(upstream * unit, axis=0, keepdims=True)
        sums_ref[1:2, block] = jnp.sum(du * inputs, axis=0, keepdims=True)
        fresh = state[block, :] + dot(
            (over_pair(grown, pair, du.shape) * du).astype(LOW), readout, 0, 0
        )
        state[block, :] = fresh
        parcel_ref[block, :] = fresh.astype(LOW)
    write_decays(parcel_ref, channels, cum_ref[rows - 1 : rows, :])


def gate_tail_back(dn, y, cum, bc, x, projected, heads, gain, rows):
    total, channels = y.shape
    count = total // rows
    return kernel_call(
        tail_back_body,
        (count,),
        [
            rows_block(rows, channels),
            rows_block(rows, channels),
            rows_block(rows, LANES),
            rows_block(rows, 2 * STATE),
            rows_block(rows, channels),
            rows_block(rows, channels, 0),
            whole((8, LANES)),
            whole((1, channels)),
        ],
        [
            rows_block(rows, channels),
            rows_block(rows, channels),
            whole((channels + PARCEL_ROWS, STATE)),
            sequence_block(8, channels),
        ],
        [
            jax.ShapeDtypeStruct((total, channels), WIDE),
            jax.ShapeDtypeStruct((total, channels), LOW),
            jax.ShapeDtypeStruct((channels + PARCEL_ROWS, STATE), LOW),
            jax.ShapeDtypeStruct((count, 8, channels), WIDE),
        ],
        [pltpu.VMEM((channels, STATE), WIDE)],
        flops=total * channels * (2 * STATE + 60),
        moved=total * channels * 22,
    )(dn, y, cum, bc, x, projected, heads, gain)


def write_decays(parcel_ref, channels, last):
    high = jnp.broadcast_to(jnp.exp(last), (PARCEL_ROWS, LANES))
    top = high.astype(LOW).astype(WIDE)
    row = row_iota(high.shape)
    parcel_ref[channels:, :] = jnp.where(
        row == 0, top, jnp.where(row == 1, high - top, 0.0)
    ).astype(LOW)


def lane_sums(values):
    first = lane_iota(values.shape) < HDIM
    return (
        jnp.sum(jnp.where(first, values, 0.0), axis=1, keepdims=True),
        jnp.sum(jnp.where(first, 0.0, values), axis=1, keepdims=True),
    )


def scan_back_body(
    du_ref, x_ref, bc_ref, stk_ref, prior_ref, rim_ref, cum_ref, all_ref, step_ref, side_ref,
    first_ref, parcel_ref, later_ref, taps_ref, heads_ref,
    dstk_ref, drim_ref, dstep_ref, dtaps_ref, dheads_ref, padded, dact, after, behind,
):
    place = pl.program_id(0)
    second = jnp.where(place == 0, 1.0, 0.0).astype(WIDE)
    rows, channels = du_ref.shape
    heads = channels // HDIM
    width = channels + 2 * STATE
    entry, readout = bc_ref[:, :STATE], bc_ref[:, STATE:]
    cum, step = cum_ref[...], step_ref[...]
    cum_rows = cum.T
    last = cum[rows - 1 : rows, :]
    faded, arriving = jnp.exp(last), jnp.exp(all_ref[0:1, :] - cum[0:1, :])

    @pl.when(place == 0)
    def _():
        behind[...] = later_ref[:channels, :].astype(WIDE)
        after[8 + rows : 16 + rows, :] = jnp.zeros((8, width), WIDE)
        padded[0:8, :] = prior_ref[8:16, :].astype(WIDE)

    @pl.when(place > 0)
    def _():
        after[8 + rows : 16 + rows, :] = after[8:16, :]
        padded[0:8, :] = rim_ref[...]

    grown = jnp.exp(cum)
    decayed = jnp.exp(last - cum)
    tail = decayed * step
    cross = dot(entry, readout, 1, 1)
    shape = (rows, rows)
    causal = row_iota(shape) <= lane_iota(shape)
    lanes = lane_iota((rows, LANES))
    small = lane_iota((1, LANES))
    dcross = jnp.zeros(shape, WIDE)
    entry_grad = jnp.zeros((rows, STATE), WIDE)
    readout_grad = jnp.zeros((rows, STATE), WIDE)
    pulled = jnp.zeros((rows, LANES), WIDE)
    arrived = []
    carried_sum = jnp.zeros((rows, LANES), WIDE)
    final_sum = jnp.zeros((rows, LANES), WIDE)
    state_sum = jnp.zeros((1, LANES), WIDE)
    for pair in range(heads // 2):
        block = slice(pair * LANES, (pair + 1) * LANES)
        inputs = x_ref[:, block]
        inputs_wide = inputs.astype(WIDE)
        du = du_ref[:, block]
        du_low = du.astype(LOW)
        start = down_pair(arriving, pair) * parcel_ref[block, :].astype(WIDE)
        start = start + second * first_ref[block, :]
        later = behind[block, :]
        start_low, later_low = start.astype(LOW), later.astype(LOW)
        pulls = []
        for k in range(2):
            head = 2 * pair + k
            own = (lanes < HDIM) if k == 0 else (lanes >= HDIM)
            gap = cum_rows[head : head + 1, :] - cum[:, head : head + 1]
            decay = jnp.exp(jnp.where(causal, gap, MASKED))
            pulls.append(dot((decay * cross).astype(LOW), du_low))
            dmix = dot(jnp.where(own, inputs, jnp.zeros_like(inputs)), du_low, 1, 1) * decay
            stepped = step[:, head : head + 1]
            dcross = dcross + dmix * stepped
            dgap = dmix * cross
            pulled = jnp.where(lanes == head, jnp.sum(dgap, axis=1, keepdims=True), pulled)
            arrived.append(jnp.sum(dgap * stepped, axis=0, keepdims=True))
        pull = jnp.where(lanes < HDIM, pulls[0], pulls[1])
        grown_pair = over_pair(grown, pair, du.shape)
        grown_du = grown_pair * du
        grown_low = grown_du.astype(LOW)
        behind[block, :] = down_pair(faded, pair) * later + dot(grown_low, readout, 0, 0)
        readout_grad = readout_grad + dot(grown_low, start_low)
        sums = lane_sums(grown_du * dot(readout, start_low, 1, 1))
        carried_sum = jnp.where(lanes == 2 * pair, sums[0], carried_sum)
        carried_sum = jnp.where(lanes == 2 * pair + 1, sums[1], carried_sum)
        tail_pair = over_pair(tail, pair, du.shape)
        from_later = dot(entry, later_low, 1, 1)
        entry_grad = entry_grad + dot((tail_pair * inputs_wide).astype(LOW), later_low)
        sums = lane_sums(inputs_wide * from_later)
        final_sum = jnp.where(lanes == 2 * pair, sums[0], final_sum)
        final_sum = jnp.where(lanes == 2 * pair + 1, sums[1], final_sum)
        product = start * later
        for k in range(2):
            total = jnp.sum(
                jnp.sum(product[k * HDIM : (k + 1) * HDIM], axis=0, keepdims=True),
                axis=1,
                keepdims=True,
            )
            state_sum = jnp.where(small == 2 * pair + k, total, state_sum)
        skip = over_pair(heads_ref[2:3, :], pair, (1, LANES))
        dact[:, block] = (
            skip * du + over_pair(step, pair, du.shape) * pull + tail_pair * from_later
        )
    dcross_low = dcross.astype(LOW)
    dact[:, channels : channels + STATE] = entry_grad + dot(dcross_low, readout)
    dact[:, channels + STATE :] = readout_grad + dot(dcross_low, entry, 0, 0)
    arrived.append(jnp.zeros((LANES - heads, rows), WIDE))
    arrived_columns = jnp.concatenate(arrived, axis=0).T
    weighted = tail * final_sum
    dcum = arrived_columns - step * pulled + carried_sum - weighted
    at_last = jnp.sum(weighted, axis=0, keepdims=True) + faded * state_sum
    dcum = dcum + jnp.where(row_iota(dcum.shape) == rows - 1, at_last, 0.0)
    dlog = dot(lower_ones(rows, True), dcum, precision=HIGHEST)
    rate = jnp.exp(heads_ref[0:1, :])
    dstep = pulled + decayed * final_sum - rate * dlog
    dstep_pre = dstep * sigmoid(side_ref[...] + heads_ref[1:2, :])
    dstep_pre = jnp.where(lanes < heads, dstep_pre, 0.0)
    dstep_ref[...] = dstep_pre.astype(LOW)
    dheads_ref[...] = jnp.zeros(dheads_ref.shape, WIDE)
    dheads_ref[0:1, :] = -rate * jnp.sum(step * dlog, axis=0, keepdims=True)
    dheads_ref[1:2, :] = jnp.sum(dstep_pre, axis=0, keepdims=True)

    padded[8 : 8 + rows, :] = stk_ref[...].astype(WIDE)
    before = convolved(padded, taps_ref, rows)
    sigma = sigmoid(before)
    dbefore = dact[...] * sigma * (1.0 + before * (1.0 - sigma))
    after[0:8, :] = jnp.zeros((8, width), WIDE)
    after[8 : 8 + rows, :] = dbefore
    dtaps_ref[...] = jnp.zeros(dtaps_ref.shape, WIDE)
    back = None
    for j in range(CONV):
        first = 8 - CONV + 1 + j
        dtaps_ref[j : j + 1, :] = jnp.sum(
            after[8 : 8 + rows, :] * padded[first : first + rows, :], axis=0, keepdims=True
        )
        first = CONV - 1 - j
        term = taps_ref[j : j + 1, :] * after[first : first + rows + 8, :]
        back = term if back is None else back + term
    dtaps_ref[CONV : CONV + 1, :] = jnp.sum(after[8 : 8 + rows, :], axis=0, keepdims=True)
    drim_ref[...] = back[0:8]
    dstk_ref[...] = back[8:]


def scan_back(
    du, x, bc, stk, rim, cum, all_cum, step, side, first, parcel, later, taps, heads, rows
):
    total, channels = du.shape
    count = total // rows
    width = channels + 2 * STATE

    def back_block(cols, col=0):
        return pl.BlockSpec((rows, cols), lambda s: (count - 1 - s, col))

    return kernel_call(
        scan_back_body,
        (count,),
        [
            back_block(channels),
            back_block(channels),
            back_block(2 * STATE),
            back_block(width),
            pl.BlockSpec((16, width), lambda s: (rows // 16 - 1, 0)),
            whole((8, width)),
            back_block(LANES),
            back_block(LANES),
            back_block(LANES),
            back_block(LANES, 2 * STATE // LANES),
            whole((channels, STATE)),
            whole((channels + PARCEL_ROWS, STATE)),
            whole((channels + PARCEL_ROWS, STATE)),
            whole((8, width)),
            whole((8, LANES)),
        ],
        [
            back_block(width),
            whole((8, width)),
            back_block(LANES),
            sequence_block(8, width),
            sequence_block(8, LANES),
        ],
        [
            jax.ShapeDtypeStruct((total, width), WIDE),
            jax.ShapeDtypeStruct((8, width), WIDE),
            jax.ShapeDtypeStruct((total, LANES), LOW),
            jax.ShapeDtypeStruct((count, 8, width), WIDE),
            jax.ShapeDtypeStruct((count, 8, LANES), WIDE),
        ],
        [
            pltpu.VMEM((rows + 8, width), WIDE),
            pltpu.VMEM((rows, width), WIDE),
            pltpu.VMEM((rows + 16, width), WIDE),
            pltpu.VMEM((channels, STATE), WIDE),
        ],
        flops=total * rows * channels * 20,
        moved=total * width * 24,
    )(du, x, bc, stk, stk, rim, cum, all_cum, step, side, first, parcel, later, taps, heads)


def unit_scale(values):
    return lax.rsqrt(jnp.mean(values * values, axis=-1, keepdims=True) + EPSILON)


def normalize(values, gain):
    return (values * unit_scale(values) * gain).astype(LOW)


def norm_grad_body(
    kept_ref, gain_ref, own_ref, peer_ref, base_ref, out_ref, low_ref, sums_ref
):
    kept = kept_ref[...]
    scale = unit_scale(kept)
    unit = kept * scale
    upstream = own_ref[...].astype(WIDE) + peer_ref[...].astype(WIDE)
    scaled = upstream * gain_ref[...]
    inner = jnp.mean(scaled * unit, axis=-1, keepdims=True)
    out = base_ref[...] + scale * (scaled - unit * inner)
    out_ref[...] = out
    low_ref[...] = out.astype(LOW)
    sums = jnp.sum(upstream * unit, axis=0, keepdims=True)

    @pl.when(pl.program_id(0) == 0)
    def _():
        sums_ref[...] = jnp.broadcast_to(sums, sums_ref.shape)

    @pl.when(pl.program_id(0) > 0)
    def _():
        sums_ref[...] += jnp.broadcast_to(sums, sums_ref.shape)


def norm_grad(kept, gain, partial_grad, base):
    own = partial_grad.astype(LOW)
    rows, features = kept.shape
    tile = min(rows, 512)
    out, low, sums = kernel_call(
        norm_grad_body,
        (rows // tile,),
        [rows_block(tile, features), whole((1, features))] + [rows_block(tile, features)] * 3,
        [rows_block(tile, features), rows_block(tile, features), whole((8, features))],
        [
            jax.ShapeDtypeStruct((rows, features), WIDE),
            jax.ShapeDtypeStruct((rows, features), LOW),
            jax.ShapeDtypeStruct((8, features), WIDE),
        ],
        flops=rows * features * 12,
        moved=rows * features * 18,
    )(kept, gain[None], own, tp_peer(own), base)
    return out, low, sums[0]


def product(a, b):
    return jnp.dot(a, b, preferred_element_type=WIDE)


def against_rows(a, b):
    return dot(a, b, 1, 1)


def halves(values):
    cut = half_lanes(values.shape[1])
    return values[:, :cut], values[:, cut:]


def over_rows(a, b):
    return dot(a, b, 0, 0).astype(LOW)


def weight_rows(layer, pieces):
    zx, mix, attn, attn_out, mlp, mlp_out = (p[layer] for p in pieces)
    rows = zx.shape[0]
    return (
        jnp.concatenate([zx.reshape(rows, -1), attn.reshape(rows, -1)], axis=1),
        jnp.concatenate([mix.T, attn_out.T, mlp.reshape(rows, -1)], axis=1),
        mlp_out.T,
    )


def own_part(values, size, axis):
    return lax.dynamic_slice_in_dim(values, lax.axis_index("tp") * size, size, axis)


def padded_to(values, rows, lanes):
    return jnp.pad(values, ((0, rows - values.shape[0]), (0, lanes - values.shape[1])))


def local_small(order, layer, norm_gains, mamba_shared, conv_weight, conv_bias, head_params, mamba_gain):
    tp = lax.axis_size("tp")
    heads = head_params.shape[2] // tp
    full_ssm = mamba_gain.shape[1]
    channels = full_ssm // tp
    shared_all = mamba_shared[layer]
    shared = jnp.concatenate(
        [
            shared_all[:, : 2 * STATE],
            own_part(shared_all[:, 2 * STATE :], heads, 1),
            jnp.zeros((shared_all.shape[0], LANES - heads), LOW),
        ],
        axis=1,
    )
    taps_all = jnp.concatenate([conv_weight[layer], conv_bias[layer][None]], axis=0).astype(WIDE)
    taps = jnp.concatenate(
        [own_part(taps_all[:, :full_ssm], channels, 1), taps_all[:, full_ssm:]], axis=1
    )
    return (
        product(norm_gains[layer], order),
        dot(order, shared, 0, 0).astype(LOW),
        padded_to(taps, 8, taps.shape[1]),
        padded_to(own_part(head_params[layer], heads, 1), 8, LANES),
        own_part(mamba_gain[layer].astype(WIDE), channels, 0)[None],
    )


def layer_forward(hidden, layer, gathers, late, small, tables, place, sequences, moves):
    zx_w = gathers.take(2 * layer)
    gains, shared, taps, heads, gain = small
    rows = hidden.shape[0] // sequences
    channels = gain.shape[1]
    head_count = channels // HDIM
    normed = normalize(hidden, gains[0])
    projected = product(normed, zx_w)
    side = product(normed, shared)
    if layer == 0:
        late[:], projected = together(late, projected)
        late[:] = [lax.all_gather(v, "fsdp", axis=1).reshape(-1, v.shape[-1]) for v in late]
    mlp_out_w = late[layer]
    if layer > 0:
        (mlp_out_w,), projected = together((mlp_out_w,), projected)
    edge = jnp.concatenate(
        [projected[-CONV + 1 :, channels : 2 * channels], side[-CONV + 1 :, : 2 * STATE]], axis=1
    )
    came = next_half(edge.astype(LOW), True).astype(WIDE)
    rim = jnp.pad(came, ((8 - CONV + 1, 0), (0, 0)))
    queries, kv = split_qkv(projected, tables, rows, 2 * channels // (zx_w.shape[1] - 2 * channels))
    kv_came = next_half(kv, True)
    (kv_came,), rim = together((kv_came,), rim)
    rim = gathers.begin(rim)
    stk, x, bc, y_local, first, parcel_out, cum, all_cum, step = scan_local(
        projected, side, rim, taps, heads, rows, channels
    )
    parcel = next_half(parcel_out, True)
    attended, log_total = attend(place, queries, kv, kv_came, rows)
    if layer > 0:
        moves, parcel = together(moves, parcel)
    (attended, parcel), y_local = together((attended, parcel), y_local)
    parcel = gathers.step(parcel)
    parcel = gathers.begin(parcel)
    y, mamba_norm = gate_tail(y_local, all_cum, bc, x, projected, heads, gain, parcel, rows)
    both = jnp.concatenate([mamba_norm, attended], axis=1)
    rest = gathers.take(2 * layer + 1)
    mix_w, mlp_w = rest[:, : both.shape[1]], rest[:, both.shape[1] :]
    after_mix = hidden + tp_sum(against_rows(both, mix_w))
    normed_two = normalize(after_mix, gains[1])
    gate_up = product(normed_two, mlp_w)
    ff = gate_up.shape[1] // 2
    activated = (jax.nn.silu(gate_up[:, :ff]) * gate_up[:, ff:]).astype(LOW)
    if gathers.near[-1] is None:
        activated = gathers.step(activated)
    result = after_mix + tp_sum(against_rows(activated, mlp_out_w))
    saved = (
        hidden, normed, projected, side, rim, queries, kv, kv_came, stk, x, bc, cum, all_cum, step,
        first, parcel, log_total, y, both, after_mix, normed_two, gate_up, activated,
    )
    return result, saved, (zx_w, mix_w, mlp_w, mlp_out_w), moves


def layer_backward(
    upstream, grad_mlp, saved, weights, small, tables, place, sequences, scatters, split, done, extra
):
    (
        hidden, normed, projected, side, rim, queries, kv, kv_came, stk, x, bc, cum, all_cum, step,
        first, parcel, log_total, y, both, after_mix, normed_two, gate_up, activated,
    ) = saved
    zx_w, mix_w, mlp_w, mlp_out_w = weights
    gains, shared, taps, heads, gain = small
    rows = hidden.shape[0] // sequences
    channels = gain.shape[1]
    head_count = channels // HDIM
    grad_act = product(grad_mlp, mlp_out_w)
    ff = grad_act.shape[1]
    gate_part, up_part = gate_up[:, :ff], gate_up[:, ff:]
    sigma = jax.nn.sigmoid(gate_part)
    grad_gu = jnp.concatenate(
        [
            grad_act * up_part * sigma * (1.0 + gate_part * (1.0 - sigma)),
            grad_act * gate_part * sigma,
        ],
        axis=1,
    ).astype(LOW)
    table = scatters.add_fsdp_first(normed_two, grad_gu, 2, functools.partial(done, 3))
    _, grad_gu = together((table,), grad_gu)
    grad_mid, grad_mix, grad_gain_two = norm_grad(
        after_mix, gains[1], against_rows(grad_gu, mlp_w), upstream
    )
    grad_mid = scatters.step(grad_mid)
    if extra:
        extra[:], grad_mid = together(extra, grad_mid)
    table = scatters.add(
        [(grad_mlp, activated), (grad_mix, both)],
        256,
        None if split else False,
        (0, 0),
        functools.partial(done, 0),
    )
    _, grad_mix = together((table,), grad_mix)
    grad_norm = product(grad_mix, mix_w[:, :channels])
    grad_attended = product(grad_mix, mix_w[:, channels:]).astype(LOW)
    du, grad_gate, state_grads, tail_sums = gate_tail_back(
        grad_norm, y, all_cum, bc, x, projected, heads, gain, rows
    )
    later = next_half(state_grads, False)
    grad_q, own_kv, sent_kv = attend_back(
        place, queries, grad_attended, log_total, tables, kv, kv_came, rows
    )
    came_kv = [next_half(sent_kv, False)]
    (later, *came_kv), grad_gate = together((later, *came_kv), grad_gate)
    later = scatters.step(later)
    if split:
        mid = jnp.concatenate([grad_gate, grad_q], axis=1)
        table = scatters.add([(normed, mid)], 256, True, (0, 0), functools.partial(done, 2))
        _, later = together((table,), later)
    dstk, drim, grad_step, dtaps, dheads = scan_back(
        du, x, bc, stk, rim, cum, all_cum, step, side, first, parcel, later, taps, heads, rows
    )
    drim = scatters.step(drim)
    returned = next_half(drim[8 - CONV + 1 :], False)
    dstk = dstk + jnp.pad(returned, ((dstk.shape[0] - CONV + 1, 0), (0, 0)))
    grad_kv = finish_keys(own_kv, came_kv, tables, rows)
    grad_late = jnp.concatenate([dstk[:, :channels].astype(LOW), grad_kv], axis=1)
    grad_first = jnp.concatenate(
        [grad_gate, grad_late[:, :channels], grad_q, grad_late[:, channels:]], axis=1
    )
    grad_side = jnp.concatenate([dstk[:, channels:].astype(LOW), grad_step], axis=1)
    if split:
        late, tile = [grad_late, grad_side], 640
    else:
        late = [grad_gate, grad_q, grad_late[:, channels:], grad_late[:, :channels], grad_side]
        tile = 384
    late = jnp.concatenate(late, axis=1)
    table = scatters.add([(normed, late)], tile, split, (0, 0), functools.partial(done, 1))
    _, grad_first = together((table,), grad_first)
    below, grad_mlp, grad_gain_one = norm_grad(
        hidden,
        gains[0],
        against_rows(grad_first, zx_w) + against_rows(grad_side, shared),
        grad_mid,
    )
    tail_sums = jnp.sum(tail_sums, axis=0)
    dheads = jnp.sum(dheads, axis=0)
    skip_grad = jnp.sum(tail_sums[1].reshape(head_count, HDIM), axis=1)
    small_grads = (
        jnp.stack([grad_gain_one, grad_gain_two]),
        jnp.sum(dtaps, axis=0)[: CONV + 1],
        jnp.concatenate([dheads[:2, :head_count], skip_grad[None]], axis=0),
        tail_sums[0],
    )
    return scatters.step(below), grad_mlp, small_grads


def tp_ordered(a, b):
    low_half = lax.axis_index("tp") == 0
    return jnp.where(
        low_half, jnp.concatenate([a, b], axis=-1), jnp.concatenate([b, a], axis=-1)
    )


def settle_side(scatters, sums, half_heads, done):
    def run():
        fsdp = lax.axis_size("fsdp")
        layers = sums
        own = layers[0]
        rows = own.shape[0]
        wide = jnp.stack([v[:, : 2 * STATE].reshape(rows, 2, STATE) for v in layers])
        place = lax.axis_index("tp")
        (came,) = yield (tp_peer(pick(wide, 1 - place, 2)),), 0, ()
        mine = pick(wide, place, 2) + came
        steps = jnp.stack([v[:, 2 * STATE : 2 * STATE + half_heads] for v in layers]).reshape(-1)
        packed = jnp.concatenate([mine.reshape(-1), steps])
        packed = jnp.pad(packed, (0, -packed.size % (16 * LANES))).reshape(-1, LANES)
        joined = yield from join_rows(packed.astype(LOW))
        (theirs,) = yield (tp_peer(joined),), 0, ()
        count = len(layers)
        places = fsdp * lax.axis_size("ctx")

        def taken(values):
            flat = values.reshape(places, -1)
            wide_size = count * rows * STATE
            first = flat[:, :wide_size].reshape(places, count, rows, STATE)
            second = flat[:, wide_size : wide_size + count * rows * half_heads]
            return first, second.reshape(places, count, rows, half_heads)

        (wide_own, step_own), (wide_peer, step_peer) = taken(joined), taken(theirs)
        full = jnp.concatenate(
            [tp_ordered(wide_own, wide_peer), tp_ordered(step_own, step_peer)], axis=-1
        )
        done(full.transpose(1, 0, 2, 3).reshape(count, places * rows, -1).astype(WIDE))

    scatters.begin(run())


def settle_small(scatters, small_grads, done):
    def run():
        layers = len(small_grads)
        shapes = [v.shape for v in small_grads[0]]
        flat = [jnp.pad(v.reshape(-1), (0, -v.size % LANES)) for grads in small_grads for v in grads]
        packed = yield from sum_everywhere(jnp.concatenate(flat).reshape(-1, LANES))
        (packed_peer,) = yield (tp_peer(packed),), 0, ()
        own, peer = [], []
        first = 0
        for values, shape in zip(flat, shapes * layers):
            for source, parts in ((packed, own), (packed_peer, peer)):
                piece = source.reshape(-1)[first : first + math.prod(shape)]
                parts.append(piece.reshape(shape))
            first += values.shape[0]
        count = len(shapes)
        for l in range(layers):
            (gains, taps, heads, gain), (gains_p, taps_p, heads_p, gain_p) = (
                v[l * count : (l + 1) * count] for v in (own, peer)
            )
            channels = gain.shape[0]
            taps_full = jnp.concatenate(
                [
                    tp_ordered(taps[:, :channels], taps_p[:, :channels]),
                    taps[:, channels:] + taps_p[:, channels:],
                ],
                axis=1,
            )
            done(
                l,
                (
                    jnp.where(lax.axis_index("tp") == 0, gains, gains_p),
                    taps_full[:CONV],
                    taps_full[CONV],
                    tp_ordered(heads, heads_p),
                    tp_ordered(gain, gain_p),
                ),
            )

    scatters.begin(run())


def local(
    hidden_in, lengths, norm_gains, mamba_zx, mamba_shared, conv_weight, conv_bias, head_params,
    mamba_gain, mamba_out, attn_in, attn_out, mlp_in, mlp_out, out_grad,
):
    layers = norm_gains.shape[0]
    micro, own_seqs, rows, features = hidden_in.shape
    sequences = micro * own_seqs
    full_ssm = mamba_gain.shape[1]
    heads_total = head_params.shape[2]
    ctx_place = lax.axis_index("ctx")
    place = (ctx_place % 2).astype(jnp.int32).reshape(1)
    start_row = ctx_place % 2 * rows * 2
    tables = turn_tables(start_row, 2 * rows)
    pieces = (mamba_zx, mamba_out, attn_in, attn_out, mlp_in, mlp_out)
    shards = [weight_rows(l, pieces) for l in range(layers)]
    quarters = (sequences, rows, features)
    moves = to_halves_moves(hidden_in.reshape(quarters))
    first_shards = [shards[l][i] for l in range(layers) for i in range(2)]
    came = fsdp_moves(first_shards[0])
    late_block = jnp.concatenate([shards[l][2] for l in range(layers)], axis=1)[None]
    near = spread_first(late_block)
    moved = lax.optimization_barrier(moves + came + near)
    given = to_halves(*moved[:2])
    first_block = fsdp_join(first_shards[0], moved[2:-2])
    blocks, first_block = gathered_blocks(first_shards, first_block)
    gathers = Gathers([first_block] + blocks)
    late = gathered_ctx(late_block, moved[-2:], layers)
    order = own_order(features * lax.axis_size("tp"), LOW)
    smalls = [
        local_small(
            order, l, norm_gains, mamba_shared, conv_weight, conv_bias, head_params, mamba_gain
        )
        for l in range(layers)
    ]
    length = pick(lengths.reshape(sequences), ctx_place // 2, 0)
    keep = (start_row + jnp.arange(2 * rows) < length).astype(WIDE)[:, None]
    hidden = product(tp_join(given), order)
    saved, weights = [], []
    for l in range(layers):
        if l == layers - 1:
            (cotangent,), hidden = together((out_grad.reshape(quarters),), hidden)
            moves = to_halves_moves(cotangent)
        hidden, kept, used, moves = layer_forward(
            hidden, l, gathers, late, smalls[l], tables, place, sequences, moves
        )
        saved.append(kept)
        weights.append(used)
    upstream = product(tp_join(to_halves(*moves)), order) * keep
    own_rows = own_part(order, features, 0)
    mixed_out = against_rows((hidden * keep).astype(LOW), own_rows).astype(LOW)
    mixed_out = to_quarters(mixed_out)
    big, rest = [[None] * 4 for _ in range(layers)], [None] * layers
    scatters = Scatters()
    side_total = []

    def finished(layer, part, total):
        big[layer][part] = total
        if layer == 0 and part == 1:
            sides = [big[l][1][:, -3 * LANES :] for l in range(layers)]
            settle_side(scatters, sides, heads_total // lax.axis_size("tp"), side_total.append)

    small_grads = [None] * layers
    grad_low = upstream.astype(LOW)
    extra = [mixed_out]
    for l in reversed(range(layers)):
        upstream, grad_low, small_grads[l] = layer_backward(
            upstream, grad_low, saved[l], weights[l], smalls[l], tables, place, sequences,
            scatters, l == 0, functools.partial(finished, l), extra if l == layers - 1 else [],
        )
    input_grad = dot(upstream, own_rows.astype(WIDE), 1, 1, HIGHEST)
    input_grad = to_quarters(input_grad.astype(LOW)).astype(WIDE).reshape(hidden_in.shape)
    gains = jnp.concatenate([grads[0] for grads in small_grads], axis=0)
    gains = dot(gains, order.astype(WIDE), 1, 1, HIGHEST)
    small_grads = [
        (gains[2 * l : 2 * l + 2],) + small_grads[l][1:] for l in range(layers)
    ]
    settle_small(scatters, small_grads, rest.__setitem__)
    scatters.finish()
    channels = mamba_out.shape[1]
    ff = mlp_out.shape[1]
    zx_grads, attn_grads, mix_grads, up_grads, down_grads = [], [], [], [], []
    for l in range(layers):
        early, late, mid, up = big[l]
        half = early.shape[1] // 2
        firsts, seconds = early[:, :half], early[:, half:]

        def rejoined(first, last):
            return jnp.concatenate([firsts[:, first:last], seconds[:, first:last]], axis=1)

        down_grads.append(rejoined(0, ff // 2).T)
        up_grads.append(up)
        both = rejoined(ff // 2, half)
        mix_grads.append((both[:, :channels].T, both[:, channels:].T))
        if mid is None:
            half = late.shape[1] // 2
            gate, x_part = late[:, :channels], late[:, half : half + channels]
            attn_grads.append(late[:, channels:half])
        else:
            gate, x_part = mid[:, :channels], late[:, :channels]
            keys = late[:, channels : channels + LANES]
            attn_grads.append(jnp.concatenate([mid[:, channels:], keys], axis=1))
        zx_grads.append(jnp.concatenate([gate, x_part], axis=1))

    def stacked(pick):
        return jnp.stack([pick(l) for l in range(layers)])

    return (
        extra[0].reshape(hidden_in.shape),
        input_grad,
        stacked(lambda l: rest[l][0]),
        jnp.stack(zx_grads).reshape(mamba_zx.shape),
        side_total[0],
        stacked(lambda l: rest[l][1]),
        stacked(lambda l: rest[l][2]),
        stacked(lambda l: rest[l][3]),
        stacked(lambda l: rest[l][4]),
        stacked(lambda l: mix_grads[l][0]),
        jnp.stack(attn_grads).reshape(attn_in.shape),
        stacked(lambda l: mix_grads[l][1]),
        jnp.stack(up_grads).reshape(mlp_in.shape),
        jnp.stack(down_grads),
    )


def solution(mesh):
    placed = (
        P(None, "fsdp", "ctx", "tp"),
        P(None, "fsdp"),
        P(),
        P(None, ("fsdp", "ctx"), None, "tp"),
        P(),
        P(),
        P(),
        P(),
        P(),
        P(None, "tp", ("fsdp", "ctx")),
        P(None, ("fsdp", "ctx"), "tp", None),
        P(None, "tp", ("fsdp", "ctx")),
        P(None, ("fsdp", "ctx"), None, "tp"),
        P(None, "tp", ("fsdp", "ctx")),
        P(None, "fsdp", "ctx", "tp"),
    )
    return jax.shard_map(
        local,
        mesh=mesh,
        in_specs=placed,
        out_specs=(
            P(None, "fsdp", "ctx", "tp"),
            P(None, "fsdp", "ctx", "tp"),
            P(),
            P(None, ("fsdp", "ctx"), None, "tp"),
            P(),
            P(),
            P(),
            P(),
            P(),
            P(None, "tp", ("fsdp", "ctx")),
            P(None, ("fsdp", "ctx"), "tp", None),
            P(None, "tp", ("fsdp", "ctx")),
            P(None, ("fsdp", "ctx"), None, "tp"),
            P(None, "tp", ("fsdp", "ctx")),
        ),
        check_vma=False,
    )
```

```python
import functools
import math

import jax
import jax.numpy as jnp
from jax import lax
from jax.experimental import pallas as pl
from jax.experimental.pallas import tpu as pltpu
from jax.sharding import PartitionSpec as P

HDIM = 64
STATE = 128
CONV = 4
ADIM = 64
GROUP = 4
LANES = 128
EPSILON = 1e-05
THETA = 100000000000.0
HIGHEST = lax.Precision.HIGHEST
LOW = jnp.bfloat16
WIDE = jnp.float32
MASKED = -1e30
VMEM_LIMIT = 56 * 1024 * 1024
PARCEL_ROWS = 16


def dot(a, b, ca=1, cb=0, precision=None):
    return lax.dot_general(
        a, b, (((ca,), (cb,)), ((), ())), preferred_element_type=WIDE, precision=precision
    )


def lane_iota(shape):
    return lax.broadcasted_iota(jnp.int32, shape, len(shape) - 1)


def row_iota(shape):
    return lax.broadcasted_iota(jnp.int32, shape, 0)


def kernel_call(body, grid, in_specs, out_specs, out_shape, scratch=(), flops=0, moved=0):
    return pl.pallas_call(
        body,
        grid=grid,
        in_specs=in_specs,
        out_specs=out_specs,
        out_shape=out_shape,
        scratch_shapes=list(scratch),
        compiler_params=pltpu.CompilerParams(vmem_limit_bytes=VMEM_LIMIT),
        cost_estimate=pl.CostEstimate(flops=flops, bytes_accessed=moved, transcendentals=0),
    )


def whole(shape):
    return pl.BlockSpec(shape, lambda s: (0,) * len(shape))


def rows_block(rows, cols, col=0):
    return pl.BlockSpec((rows, cols), lambda s: (s, col))


def sequence_block(*shape):
    return pl.BlockSpec((None,) + shape, lambda s: (s,) + (0,) * len(shape))


def xor_pairs(count, bit):
    return [(i, i ^ bit) for i in range(count)]


def next_half(x, forward):
    firsts = range(0, lax.axis_size("ctx"), 2)
    return lax.ppermute(x, "ctx", [(i, i + 1) if forward else (i + 1, i) for i in firsts])


STRAIGHT = ((0, 0), (2, 1), (1, 2), (3, 3))
CROSSED = ((1, 0), (3, 1), (0, 2), (2, 3))


def to_halves_moves(quarters):
    place = lax.axis_index("ctx")
    a = lax.ppermute(pick(quarters, place % 2, 0), "ctx", STRAIGHT)
    b = lax.ppermute(pick(quarters, 1 - place % 2, 0), "ctx", CROSSED)
    return a, b


def to_halves(a, b):
    place = lax.axis_index("ctx")
    return jnp.where(place < 2, jnp.concatenate([a, b]), jnp.concatenate([b, a]))


def to_quarters(half):
    place = lax.axis_index("ctx")
    parts = half.reshape((2, -1) + half.shape[1:])
    late = place // 2
    a = lax.ppermute(pick(parts, late, 0), "ctx", [(j, i) for i, j in STRAIGHT])
    b = lax.ppermute(pick(parts, 1 - late, 0), "ctx", [(j, i) for i, j in CROSSED])
    return jnp.where(place % 2 == 0, jnp.stack([a, b]), jnp.stack([b, a]))


def tp_peer(x):
    return lax.ppermute(x, "tp", xor_pairs(lax.axis_size("tp"), 1))


def tp_join(x):
    peer = tp_peer(x)
    first = lax.axis_index("tp") == 0
    return jnp.where(
        first, jnp.concatenate([x, peer], axis=-1), jnp.concatenate([peer, x], axis=-1)
    )


def tp_sum(partial_sum):
    low = partial_sum.astype(LOW)
    peer = tp_peer(low)
    return low.astype(WIDE) + peer.astype(WIDE)


def bits_of(axis):
    return [1 << i for i in range(lax.axis_size(axis).bit_length() - 1)]


def together(values, anchor):
    return lax.optimization_barrier((tuple(values), anchor))


def added(*parts):
    total = parts[0].astype(WIDE)
    for part in parts[1:]:
        total = total + part.astype(WIDE)
    return total


def ctx_swap(values, step):
    return lax.ppermute(values, "ctx", xor_pairs(lax.axis_size("ctx"), step))


def pick(values, place, dim):
    return lax.dynamic_index_in_dim(values, place, dim, False)


def half_lanes(width):
    return width // 256 * 128


FLIPS = (0, 1, 3, 2)


def own_order(features, dtype):
    fsdp, ctx = lax.axis_size("fsdp"), lax.axis_size("ctx")
    rows = features // (fsdp * ctx)
    own = jnp.arange(features)
    flip, rest = jnp.array(FLIPS)[own // (fsdp * rows)], own % (fsdp * rows)
    common = (rest // rows) * ctx * rows + (flip ^ lax.axis_index("ctx")) * rows + rest % rows
    return (jnp.arange(features)[:, None] == common[None, :]).astype(dtype)


def spread_first(block):
    return ctx_swap(block, 1), ctx_swap(block, 2)


def spread_parts(came):
    cut = half_lanes(came[0].shape[-1])
    return came[0][..., :cut], came[1][..., cut:]


def spread_second(parts):
    return ctx_swap(parts[0], 2), ctx_swap(parts[1], 1)


def spread_whole(block, came, far):
    width = block.shape[-1]
    return jnp.concatenate(
        [v.reshape(-1, width) for v in (block, came[0], jnp.concatenate(far, axis=-1), came[1])], axis=0
    )


def fsdp_moves(piece):
    count = lax.axis_size("fsdp")
    if count > 4:
        return ()
    return tuple(lax.ppermute(piece, "fsdp", xor_pairs(count, step)) for step in range(1, count))


def fsdp_join(piece, came):
    if not came:
        return lax.all_gather(piece, "fsdp", axis=0)
    place = lax.axis_index("fsdp")
    shape = (len(came) + 1,) + piece.shape
    out = lax.dynamic_update_index_in_dim(jnp.zeros(shape, piece.dtype), piece, place, 0)
    for step, values in enumerate(came, 1):
        out = lax.dynamic_update_index_in_dim(out, values, place ^ step, 0)
    return out


def gathered_blocks(pieces, anchor):
    following, anchor = together((pieces[1], jnp.concatenate(pieces[2:], axis=1)), anchor)
    blocks = [lax.all_gather(following[0], "fsdp", axis=0)]
    rest = lax.all_gather(following[1], "fsdp", axis=0)
    first = 0
    for piece in pieces[2:]:
        blocks.append(rest[..., first : first + piece.shape[1]])
        first += piece.shape[1]
    return blocks, anchor


class Gathers:
    def __init__(self, blocks):
        self.blocks = blocks
        self.near = [None] * len(blocks)
        self.far = [None] * len(blocks)
        self.first = 0
        self.near[0] = spread_first(self.blocks[0])

    def step(self, anchor):
        i = self.first
        if i >= len(self.blocks):
            return anchor
        self.near[i], anchor = together(self.near[i], anchor)
        parts = spread_parts(self.near[i])
        self.far[i] = spread_second(parts)
        _, anchor = together(parts, anchor)
        self.first = i + 1
        return anchor

    def begin(self, anchor):
        i = self.first
        if i < len(self.blocks) and self.near[i] is None:
            (self.blocks[i],), anchor = together((self.blocks[i],), anchor)
            self.near[i] = spread_first(self.blocks[i])
        return anchor

    def take(self, i):
        if self.first <= i:
            self.step(self.near[i][0])
        return spread_whole(self.blocks[i], self.near[i], self.far[i])


def gathered_ctx(block, near, widths):
    far = spread_second(spread_parts(near))
    rows = spread_whole(block, near, far).reshape((4,) + block.shape[1:])
    out, first = [], 0
    for width in widths:
        out.append(rows[..., first : first + width])
        first += width
    return out


def table_body(spans, *refs):
    count = len(spans)
    left_refs, a_refs, b_refs = (refs[i * count : (i + 1) * count] for i in range(3))
    up_ref, across_ref, x_ref, y_ref, own_a_ref, own_b_ref, turned_ref = refs[3 * count :]
    size = own_a_ref.shape[0]
    place = pl.program_id(0)
    for left_ref, a_ref, b_ref, (first, last) in zip(left_refs, a_refs, b_refs, spans):

        @pl.when(place == first)
        def _(left_ref=left_ref):
            turned_ref[...] = left_ref[...].astype(WIDE).T.astype(LOW)

        @pl.when((place >= first) & (place < last))
        def _(a_ref=a_ref, b_ref=b_ref):
            table = dot(turned_ref[...], a_ref[...]).astype(LOW)
            own_a_ref[...] = table[:size]
            x_ref[...] = table[size : 2 * size]
            up_ref[...] = table[2 * size :]
            table = dot(turned_ref[...], b_ref[...]).astype(LOW)
            own_b_ref[...] = table[:size]
            across_ref[...] = table[size : 3 * size]
            y_ref[...] = table[3 * size :]


def tables(pairs, tile):
    rows, features = pairs[0][0].shape
    size = features // len(FLIPS)
    spans, first = [], 0
    for _, right in pairs:
        spans.append((first, first + right.shape[1] // (2 * tile)))
        first = spans[-1][1]
    width = first * tile

    def columns(first, last, skip):
        return pl.BlockSpec(
            (rows, tile), lambda j: (0, skip + jnp.clip(j, first, last - 1) - first)
        )

    def tall(height):
        return pl.BlockSpec((height, tile), lambda j: (0, j))

    heights = (2 * size, 2 * size, size, size, size, size)
    return kernel_call(
        functools.partial(table_body, tuple(spans)),
        (first,),
        [whole((rows, features))] * len(pairs)
        + [columns(*span, 0) for span in spans]
        + [columns(*span, span[1] - span[0]) for span in spans],
        [tall(h) for h in heights],
        [jax.ShapeDtypeStruct((h, width), LOW) for h in heights],
        [pltpu.VMEM((features, rows), LOW)],
        flops=4 * rows * features * width,
        moved=width * (4 * rows + 4 * features),
    )(*[p[0] for p in pairs], *[p[1] for p in pairs], *[p[1] for p in pairs])


def fsdp_table_body(left_ref, right_ref, out_ref, turned_ref):
    @pl.when(pl.program_id(0) == 0)
    def _():
        turned_ref[...] = left_ref[...].astype(WIDE).T.astype(LOW)

    table = dot(turned_ref[...], right_ref[...])
    fsdp, flips, rows, _ = out_ref.shape
    for flip in range(flips):
        for place in range(fsdp):
            first = (flip * fsdp + place) * rows
            out_ref[place, flip] = table[first : first + rows].astype(LOW)


def fsdp_table(left, right, tile):
    rows, features = left.shape
    width = right.shape[1]
    fsdp, flips = lax.axis_size("fsdp"), len(FLIPS)
    shape = (fsdp, flips, features // (fsdp * flips))
    return kernel_call(
        fsdp_table_body,
        (width // tile,),
        [whole((rows, features)), pl.BlockSpec((rows, tile), lambda j: (0, j))],
        pl.BlockSpec(shape + (tile,), lambda j: (0, 0, 0, j)),
        jax.ShapeDtypeStruct(shape + (width,), LOW),
        [pltpu.VMEM((features, rows), LOW)],
        flops=2 * rows * features * width,
        moved=width * (2 * rows + 2 * features),
    )(left, right)


def pass_body(x_ref, y_ref, from_y_ref, from_x_ref, to_x_ref, to_y_ref):
    size = x_ref.shape[0]
    to_x_ref[...] = (x_ref[...].astype(WIDE) + from_y_ref[:size].astype(WIDE)).astype(LOW)
    to_y_ref[...] = (y_ref[...].astype(WIDE) + from_x_ref[size:].astype(WIDE)).astype(LOW)


def keep_body(own_a_ref, own_b_ref, from_y_ref, from_x_ref, last_x_ref, last_y_ref, out_ref):
    size, width = own_a_ref.shape
    out_ref[:, :width] = (
        own_a_ref[...].astype(WIDE) + from_y_ref[size:].astype(WIDE) + last_x_ref[...].astype(WIDE)
    ).astype(LOW)
    out_ref[:, width:] = (
        own_b_ref[...].astype(WIDE) + from_x_ref[:size].astype(WIDE) + last_y_ref[...].astype(WIDE)
    ).astype(LOW)


def once(body, out_shapes, *operands):
    outs = [jax.ShapeDtypeStruct(shape, LOW) for shape in out_shapes]
    return kernel_call(
        body,
        (1,),
        [whole(v.shape) for v in operands],
        [whole(shape) for shape in out_shapes],
        outs,
        moved=sum(v.size * 2 for v in operands) + sum(2 * math.prod(x) for x in out_shapes),
    )(*operands)


def ctx_scatter(cuts, waits):
    up, across, x, y, own_a, own_b = cuts
    from_y, from_x = yield (ctx_swap(up, 2), ctx_swap(across, 1)), waits[0], (up, across)
    to_x, to_y = once(pass_body, (x.shape, y.shape), x, y, from_y, from_x)
    last_x, last_y = yield (ctx_swap(to_x, 1), ctx_swap(to_y, 2)), waits[1], (to_x, to_y)
    size, width = own_a.shape
    (out,) = once(keep_body, ((size, 2 * width),), own_a, own_b, from_y, from_x, last_x, last_y)
    return out


def fsdp_scatter(table, direct):
    count = lax.axis_size("fsdp")
    if count > 4 or not direct:
        total = lax.psum_scatter(table, "fsdp", scatter_dimension=0, tiled=False)
        if direct is None:
            (total,) = yield (total,), 0, (table,)
        else:
            yield (), 0, (table,)
        return total.astype(WIDE)
    place = lax.axis_index("fsdp")
    came = tuple(
        lax.ppermute(pick(table, place ^ step, 0), "fsdp", xor_pairs(count, step))
        for step in range(1, count)
    )
    came = yield came, 0, (table,)
    return added(pick(table, place, 0), *came)


class Scatters:
    def __init__(self):
        self.active = []

    def add(self, pairs, tile, direct, waits, done):
        cuts = tables(pairs, tile)

        def run():
            part = yield from ctx_scatter(cuts, waits)
            fsdp = lax.axis_size("fsdp")
            part = part.reshape(fsdp, -1, part.shape[1])
            done((yield from fsdp_scatter(part, direct)))

        self.begin(run())
        return cuts[0]

    def add_fsdp_first(self, left, right, waits, done):
        table = fsdp_table(left, right, 512)
        fsdp, flips, rows, width = table.shape

        def run():
            moved = table.reshape(fsdp, flips * rows, width)
            total = lax.psum_scatter(moved, "fsdp", scatter_dimension=0, tiled=False)
            (total,) = yield (total,), waits, (moved,)
            cut = half_lanes(width)
            own, x, far, y = (total[i * rows : (i + 1) * rows] for i in range(flips))
            cuts = (
                total[2 * rows :, :cut],
                total[rows : 3 * rows, cut:],
                x[:, :cut],
                y[:, cut:],
                own[:, :cut],
                own[:, cut:],
            )
            done((yield from ctx_scatter(cuts, (0, 0))).astype(WIDE))

        self.begin(run())
        return table

    def begin(self, work):
        self.active.append([work, *next(work)])

    def step(self, anchor):
        ready = [item for item in self.active if anchor is None or item[2] == 0]
        for item in self.active:
            item[2] = max(item[2] - 1, 0)
        values = [v for item in ready for v in item[1]]
        if anchor is not None:
            values, anchor = together(values, anchor)
        elif values:
            values = lax.optimization_barrier(tuple(values))
        first, sent = 0, ()
        for item in ready:
            came = tuple(values[first : first + len(item[1])])
            first += len(item[1])
            try:
                item[1:] = item[0].send(came)
                sent += item[3]
            except StopIteration:
                self.active.remove(item)
        if sent and anchor is not None:
            _, anchor = together(sent, anchor)
        return anchor

    def finish(self):
        while self.active:
            self.step(None)


def join_rows(piece):
    v = piece[None, None]
    for dim, axis in enumerate(("fsdp", "ctx")):
        place = lax.axis_index(axis)
        for step in bits_of(axis):
            (came,) = yield (lax.ppermute(v, axis, xor_pairs(lax.axis_size(axis), step)),), 0, ()
            v = jnp.where(
                (place & step) == 0,
                jnp.concatenate([v, came], axis=dim),
                jnp.concatenate([came, v], axis=dim),
            )
    return v


def sum_everywhere(v):
    for axis in ("fsdp", "ctx"):
        for step in bits_of(axis):
            (came,) = yield (lax.ppermute(v, axis, xor_pairs(lax.axis_size(axis), step)),), 0, ()
            v = v + came
    return v


def turn_tables(start_row, rows):
    half = ADIM // 2
    places = (start_row + jnp.arange(rows)).astype(WIDE)
    rates = jnp.exp(-math.log(THETA) * jnp.arange(half).astype(WIDE) / half)
    angles = places[:, None] * rates[None, :]
    cosine, sine = jnp.cos(angles), jnp.sin(angles)
    one_cos = jnp.concatenate([cosine, cosine], axis=1)
    one_sin = jnp.concatenate([-sine, sine], axis=1)
    still = jnp.ones_like(one_cos)
    return (
        jnp.concatenate([one_cos, one_cos, one_cos, still], axis=1),
        jnp.concatenate([one_sin, one_sin, one_sin, jnp.zeros_like(one_sin)], axis=1),
    )


def turned(values, cosine, sine):
    lanes = lane_iota(values.shape) % ADIM
    swapped = jnp.where(
        lanes < ADIM // 2,
        pltpu.roll(values, LANES - ADIM // 2, 1),
        pltpu.roll(values, ADIM // 2, 1),
    )
    return values * cosine + swapped * sine


def qkv_body(rows_ref, cos_ref, sin_ref, q_ref, kv_ref):
    for pair in range(GROUP // 2):
        lanes = slice(pair * LANES, (pair + 1) * LANES)
        q_ref[:, lanes] = turned(
            rows_ref[:, lanes], cos_ref[:, :LANES], sin_ref[:, :LANES]
        ).astype(LOW)
    width = GROUP * ADIM
    kv_ref[...] = turned(
        rows_ref[:, width : width + LANES], cos_ref[:, LANES:], sin_ref[:, LANES:]
    ).astype(LOW)


def split_qkv(projected, tables, rows, column):
    total = projected.shape[0]
    width = GROUP * ADIM
    return kernel_call(
        qkv_body,
        (total // rows,),
        [rows_block(rows, width + LANES, column)] + [rows_block(rows, 2 * LANES)] * 2,
        [rows_block(rows, width), rows_block(rows, LANES)],
        [
            jax.ShapeDtypeStruct((total, width), LOW),
            jax.ShapeDtypeStruct((total, LANES), LOW),
        ],
        flops=total * 400 * 4,
        moved=total * 384 * 6,
    )(projected, *tables)


def head_lanes(values, head):
    pair = values[:, head // 2 * LANES : (head // 2 + 1) * LANES]
    if head % 2:
        pair = pltpu.roll(pair, ADIM, 1)
    return jnp.where(lane_iota(pair.shape) < ADIM, pair, jnp.zeros_like(pair))


def seen_keys(place, rows, total):
    shape = (rows, 2 * total)
    column = lane_iota(shape)
    own = (column < total) & (column <= row_iota(shape) + pl.program_id(0) * rows)
    return own | ((column >= total) & (column < total * (1 + place)))


def attend_body(place_ref, q_ref, own_ref, came_ref, out_ref, total_ref, keys):
    rows, total = q_ref.shape[0], own_ref.shape[0]
    keys[:total, :] = own_ref[...]
    keys[total:, :] = came_ref[...]
    seen = seen_keys(place_ref[0], rows, total)
    q_all = q_ref[...].astype(WIDE)
    all_keys = keys[...]
    totals = jnp.zeros((rows, LANES), WIDE)
    lanes = lane_iota((rows, LANES))
    outs = []
    for head in range(GROUP):
        query = head_lanes(q_all, head).astype(LOW)
        scores = jnp.where(seen, dot(query, all_keys, 1, 1) * ADIM**-0.5, MASKED)
        top = jnp.max(scores, axis=1, keepdims=True)
        raised = jnp.exp(scores - top)
        row_total = jnp.sum(raised, axis=1, keepdims=True)
        weights = (raised * (1.0 / row_total)).astype(LOW)
        outs.append(dot(weights, all_keys))
        totals = jnp.where(lanes == head, top + jnp.log(row_total), totals)
    total_ref[...] = totals
    for pair in range(GROUP // 2):
        first = pltpu.roll(outs[2 * pair], ADIM, 1)
        out_ref[:, pair * LANES : (pair + 1) * LANES] = jnp.where(
            lanes < ADIM, first, outs[2 * pair + 1]
        ).astype(LOW)


def attend(place, queries, own, came, rows):
    total, width = queries.shape
    return kernel_call(
        attend_body,
        (total // rows,),
        [
            pl.BlockSpec(memory_space=pltpu.SMEM),
            rows_block(rows, width),
            whole((total, LANES)),
            whole((total, LANES)),
        ],
        [rows_block(rows, width), rows_block(rows, LANES)],
        [
            jax.ShapeDtypeStruct((total, width), LOW),
            jax.ShapeDtypeStruct((total, LANES), WIDE),
        ],
        [pltpu.VMEM((2 * total, LANES), LOW)],
        flops=total * total * 2 * GROUP * LANES * 4,
        moved=total * (width * 4 + LANES * 12),
    )(place, queries, own, came)


def attend_back_body(
    place_ref, q_ref, grad_ref, total_ref, cos_ref, sin_ref, own_ref, came_ref,
    dq_ref, own_grad_ref, came_grad_ref, keys, grads,
):
    rows, total = q_ref.shape[0], own_ref.shape[0]
    keys[:total, :] = own_ref[...]
    keys[total:, :] = came_ref[...]
    seen = seen_keys(place_ref[0], rows, total)
    q_all = q_ref[...].astype(WIDE)
    grad_all = grad_ref[...].astype(WIDE)
    all_keys = keys[...]
    lanes = lane_iota((rows, LANES))
    grad_kv = None
    dqs = []
    for head in range(GROUP):
        query = head_lanes(q_all, head).astype(LOW)
        upper = pltpu.roll(head_lanes(grad_all, head), ADIM, 1).astype(LOW)
        scores = jnp.where(seen, dot(query, all_keys, 1, 1) * ADIM**-0.5, MASKED)
        probs = jnp.exp(scores - total_ref[:, head : head + 1])
        grad_probs = dot(upper, all_keys, 1, 1)
        inner = jnp.sum(probs * grad_probs, axis=1, keepdims=True)
        grad_scores = (probs * (grad_probs - inner)).astype(LOW)
        dqs.append(dot(grad_scores, all_keys) * ADIM**-0.5)
        fresh = dot(grad_scores, query, 0, 0) * ADIM**-0.5 + dot(
            probs.astype(LOW), upper, 0, 0
        )
        grad_kv = fresh if grad_kv is None else grad_kv + fresh
    for pair in range(GROUP // 2):
        both = jnp.where(lanes < ADIM, dqs[2 * pair], pltpu.roll(dqs[2 * pair + 1], ADIM, 1))
        dq_ref[:, pair * LANES : (pair + 1) * LANES] = turned(
            both, cos_ref[:, :LANES], -sin_ref[:, :LANES]
        ).astype(LOW)
    place = pl.program_id(0)

    @pl.when(place == 0)
    def _():
        grads[...] = grad_kv

    @pl.when(place > 0)
    def _():
        grads[...] += grad_kv

    own_grad_ref[...] = grads[:total, :]
    came_grad_ref[...] = grads[total:, :].astype(LOW)


def attend_back(place, queries, grad_out, log_total, tables, own, came, rows):
    total, width = queries.shape
    return kernel_call(
        attend_back_body,
        (total // rows,),
        [
            pl.BlockSpec(memory_space=pltpu.SMEM),
            rows_block(rows, width),
            rows_block(rows, width),
            rows_block(rows, LANES),
            rows_block(rows, 2 * LANES),
            rows_block(rows, 2 * LANES),
            whole((total, LANES)),
            whole((total, LANES)),
        ],
        [rows_block(rows, width), whole((total, LANES)), whole((total, LANES))],
        [
            jax.ShapeDtypeStruct((total, width), LOW),
            jax.ShapeDtypeStruct((total, LANES), WIDE),
            jax.ShapeDtypeStruct((total, LANES), LOW),
        ],
        [pltpu.VMEM((2 * total, LANES), LOW), pltpu.VMEM((2 * total, LANES), WIDE)],
        flops=total * total * 2 * GROUP * LANES * 10,
        moved=total * (width * 6 + LANES * 20),
    )(place, queries, grad_out, log_total, *tables, own, came)


def key_body(own_ref, *refs):
    came, (cos_ref, sin_ref, out_ref) = refs[:-3], refs[-3:]
    values = own_ref[...]
    for ref in came:
        values = values + ref[...].astype(WIDE)
    out_ref[...] = turned(values, cos_ref[:, LANES:], -sin_ref[:, LANES:]).astype(LOW)


def finish_keys(own, came, tables, rows):
    total = own.shape[0]
    return kernel_call(
        key_body,
        (total // rows,),
        [rows_block(rows, LANES)] * (1 + len(came)) + [rows_block(rows, 2 * LANES)] * 2,
        rows_block(rows, LANES),
        jax.ShapeDtypeStruct((total, LANES), LOW),
        flops=total * LANES * 10,
        moved=total * LANES * 12,
    )(own, *came, *tables)


def sigmoid(v):
    return 1.0 / (1.0 + jnp.exp(-v))


def softplus(v):
    return jnp.maximum(v, 0.0) + jnp.log1p(jnp.exp(-jnp.abs(v)))


def over_pair(values, pair, shape):
    first = values[:, 2 * pair : 2 * pair + 1]
    second = values[:, 2 * pair + 1 : 2 * pair + 2]
    return jnp.where(lane_iota(shape) < HDIM, first, second)


def down_pair(values, pair):
    shape = (LANES, LANES)
    first = jnp.broadcast_to(values[:, 2 * pair : 2 * pair + 1], shape)
    second = jnp.broadcast_to(values[:, 2 * pair + 1 : 2 * pair + 2], shape)
    return jnp.where(row_iota(shape) < HDIM, first, second)


def lower_ones(rows, flip):
    shape = (rows, rows)
    t, s = row_iota(shape), lane_iota(shape)
    return jnp.where((t <= s) if flip else (t >= s), 1.0, 0.0).astype(WIDE)


def convolved(padded, taps_ref, rows):
    total = taps_ref[CONV : CONV + 1, :]
    for j in range(CONV):
        first = 8 - CONV + 1 + j
        total = total + taps_ref[j : j + 1, :] * padded[first : first + rows, :]
    return total


def scan_body(
    zx_ref, side_ref, rim_ref, taps_ref, heads_ref,
    stk_ref, x_ref, bc_ref, y_ref, first_ref, parcel_ref, cum_ref, all_ref, step_ref,
    padded, state, before_it,
):
    rows, channels = zx_ref.shape
    heads = channels // HDIM
    place = pl.program_id(0)

    @pl.when(place == 0)
    def _():
        padded[0:8, :] = rim_ref[...]
        state[...] = jnp.zeros(state.shape, WIDE)
        before_it[...] = jnp.zeros(before_it.shape, WIDE)

    @pl.when(place > 0)
    def _():
        padded[0:8, :] = padded[rows : rows + 8, :]

    stk_ref[:, :channels] = zx_ref[...].astype(LOW)
    stk_ref[:, channels:] = side_ref[:, : 2 * STATE].astype(LOW)
    padded[8 : 8 + rows, :] = stk_ref[...].astype(WIDE)
    before = convolved(padded, taps_ref, rows)
    active = (before * sigmoid(before)).astype(LOW)
    x_ref[...] = active[:, :channels]
    bc_ref[...] = active[:, channels:]
    step = softplus(side_ref[:, 2 * STATE :] + heads_ref[1:2, :])
    cum = dot(lower_ones(rows, False), -step * jnp.exp(heads_ref[0:1, :]), precision=HIGHEST)
    step_ref[...] = step
    cum_ref[...] = cum
    all_ref[...] = cum + before_it[0:1, :]
    cum_rows, step_rows = cum.T, step.T
    last = cum[rows - 1 : rows, :]
    before_it[...] = jnp.broadcast_to(before_it[0:1, :] + last, before_it.shape)
    tail = jnp.exp(last - cum) * step
    grown, faded = jnp.exp(cum), jnp.exp(last)
    entry, readout = bc_ref[:, :STATE], bc_ref[:, STATE:]
    cross = dot(readout, entry, 1, 1)
    shape = (rows, rows)
    causal = row_iota(shape) >= lane_iota(shape)
    lanes = lane_iota((rows, LANES))
    for pair in range(heads // 2):
        block = slice(pair * LANES, (pair + 1) * LANES)
        inputs = x_ref[:, block]
        outs = []
        for head in (2 * pair, 2 * pair + 1):
            gap = cum[:, head : head + 1] - cum_rows[head : head + 1, :]
            decay = jnp.exp(jnp.where(causal, gap, MASKED))
            mixed = (decay * cross * step_rows[head : head + 1, :]).astype(LOW)
            outs.append(dot(mixed, inputs))
        carried = dot(readout, state[block, :].astype(LOW), 1, 1)
        y_ref[:, block] = jnp.where(lanes < HDIM, outs[0], outs[1]) + carried * over_pair(
            grown, pair, (rows, LANES)
        )
        scaled = (over_pair(tail, pair, (rows, LANES)) * inputs.astype(WIDE)).astype(LOW)
        fresh = down_pair(faded, pair) * state[block, :] + dot(scaled, entry, 0, 0)
        state[block, :] = fresh
        parcel_ref[block, :] = fresh.astype(LOW)
    write_decays(parcel_ref, channels, before_it[0:1, :])

    @pl.when(place == 0)
    def _():
        first_ref[...] = state[...]


def scan_local(projected, side, rim, taps, heads, rows, channels):
    total = projected.shape[0]
    count = total // rows
    width = channels + 2 * STATE
    return kernel_call(
        scan_body,
        (count,),
        [
            rows_block(rows, channels, 1),
            rows_block(rows, side.shape[1]),
            whole((8, width)),
            whole((8, width)),
            whole((8, LANES)),
        ],
        [
            rows_block(rows, width),
            rows_block(rows, channels),
            rows_block(rows, 2 * STATE),
            rows_block(rows, channels),
            whole((channels, STATE)),
            whole((channels + PARCEL_ROWS, STATE)),
            rows_block(rows, LANES),
            rows_block(rows, LANES),
            rows_block(rows, LANES),
        ],
        [
            jax.ShapeDtypeStruct((total, width), LOW),
            jax.ShapeDtypeStruct((total, channels), LOW),
            jax.ShapeDtypeStruct((total, 2 * STATE), LOW),
            jax.ShapeDtypeStruct((total, channels), WIDE),
            jax.ShapeDtypeStruct((channels, STATE), WIDE),
            jax.ShapeDtypeStruct((channels + PARCEL_ROWS, STATE), LOW),
            jax.ShapeDtypeStruct((total, LANES), WIDE),
            jax.ShapeDtypeStruct((total, LANES), WIDE),
            jax.ShapeDtypeStruct((total, LANES), WIDE),
        ],
        [
            pltpu.VMEM((rows + 8, width), WIDE),
            pltpu.VMEM((channels, STATE), WIDE),
            pltpu.VMEM((8, LANES), WIDE),
        ],
        flops=total * rows * channels * 8,
        moved=total * width * 16,
    )(projected, side, rim, taps, heads)


def tail_body(
    y_ref, cum_ref, bc_ref, x_ref, gate_ref, heads_ref, gain_ref, parcel_ref, out_ref, norm_ref
):
    rows, channels = y_ref.shape
    readout = bc_ref[:, STATE:]
    grown = jnp.exp(cum_ref[...])
    square = jnp.zeros((rows, 1), WIDE)
    for pair in range(channels // LANES):
        block = slice(pair * LANES, (pair + 1) * LANES)
        carried = dot(readout, parcel_ref[block, :], 1, 1)
        y = y_ref[:, block] + over_pair(grown, pair, carried.shape) * carried
        out_ref[:, block] = y
        skip = over_pair(heads_ref[2:3, :], pair, (1, LANES))
        gate = gate_ref[:, block]
        mixed = (y + skip * x_ref[:, block].astype(WIDE)) * (gate * sigmoid(gate))
        square = square + jnp.sum(mixed * mixed, axis=1, keepdims=True)
    scale = lax.rsqrt(square * (1.0 / channels) + EPSILON)
    for pair in range(channels // LANES):
        block = slice(pair * LANES, (pair + 1) * LANES)
        skip = over_pair(heads_ref[2:3, :], pair, (1, LANES))
        gate = gate_ref[:, block]
        mixed = (out_ref[:, block] + skip * x_ref[:, block].astype(WIDE)) * (gate * sigmoid(gate))
        norm_ref[:, block] = (mixed * scale * gain_ref[:, block]).astype(LOW)


def gate_tail(y, cum, bc, x, projected, heads, gain, parcel, rows):
    total, channels = y.shape
    return kernel_call(
        tail_body,
        (total // rows,),
        [
            rows_block(rows, channels),
            rows_block(rows, LANES),
            rows_block(rows, 2 * STATE),
            rows_block(rows, channels),
            rows_block(rows, channels, 0),
            whole((8, LANES)),
            whole((1, channels)),
            whole((channels + PARCEL_ROWS, STATE)),
        ],
        [rows_block(rows, channels), rows_block(rows, channels)],
        [
            jax.ShapeDtypeStruct((total, channels), WIDE),
            jax.ShapeDtypeStruct((total, channels), LOW),
        ],
        flops=total * channels * (2 * STATE + 40),
        moved=total * channels * 18,
    )(y, cum, bc, x, projected, heads, gain, parcel)


def tail_back_body(
    dn_ref, y_ref, cum_ref, bc_ref, x_ref, gate_ref, heads_ref, gain_ref,
    du_ref, dgate_ref, parcel_ref, sums_ref, state,
):
    @pl.when(pl.program_id(0) == 0)
    def _():
        state[...] = jnp.zeros(state.shape, WIDE)

    rows, channels = y_ref.shape
    readout = bc_ref[:, STATE:]
    grown = jnp.exp(cum_ref[...])
    square = jnp.zeros((rows, 1), WIDE)
    inner = jnp.zeros((rows, 1), WIDE)
    for pair in range(channels // LANES):
        block = slice(pair * LANES, (pair + 1) * LANES)
        skip = over_pair(heads_ref[2:3, :], pair, (1, LANES))
        gate = gate_ref[:, block]
        mixed = (y_ref[:, block] + skip * x_ref[:, block].astype(WIDE)) * (gate * sigmoid(gate))
        square = square + jnp.sum(mixed * mixed, axis=1, keepdims=True)
        inner = inner + jnp.sum(
            dn_ref[:, block] * gain_ref[:, block] * mixed, axis=1, keepdims=True
        )
    scale = lax.rsqrt(square * (1.0 / channels) + EPSILON)
    inner = inner * scale * (1.0 / channels)
    sums_ref[...] = jnp.zeros(sums_ref.shape, WIDE)
    for pair in range(channels // LANES):
        block = slice(pair * LANES, (pair + 1) * LANES)
        skip = over_pair(heads_ref[2:3, :], pair, (1, LANES))
        gate = gate_ref[:, block]
        inputs = x_ref[:, block].astype(WIDE)
        sigma = sigmoid(gate)
        value = y_ref[:, block] + skip * inputs
        unit = value * (gate * sigma) * scale
        upstream = dn_ref[:, block]
        dmixed = scale * (upstream * gain_ref[:, block] - unit * inner)
        du = dmixed * gate * sigma
        du_ref[:, block] = du
        dgate_ref[:, block] = (
            dmixed * value * (sigma * (1.0 + gate * (1.0 - sigma)))
        ).astype(LOW)
        sums_ref[0:1, block] = jnp.sum(upstream * unit, axis=0, keepdims=True)
        sums_ref[1:2, block] = jnp.sum(du * inputs, axis=0, keepdims=True)
        fresh = state[block, :] + dot(
            (over_pair(grown, pair, du.shape) * du).astype(LOW), readout, 0, 0
        )
        state[block, :] = fresh
        parcel_ref[block, :] = fresh.astype(LOW)
    write_decays(parcel_ref, channels, cum_ref[rows - 1 : rows, :])


def gate_tail_back(dn, y, cum, bc, x, projected, heads, gain, rows):
    total, channels = y.shape
    count = total // rows
    return kernel_call(
        tail_back_body,
        (count,),
        [
            rows_block(rows, channels),
            rows_block(rows, channels),
            rows_block(rows, LANES),
            rows_block(rows, 2 * STATE),
            rows_block(rows, channels),
            rows_block(rows, channels, 0),
            whole((8, LANES)),
            whole((1, channels)),
        ],
        [
            rows_block(rows, channels),
            rows_block(rows, channels),
            whole((channels + PARCEL_ROWS, STATE)),
            sequence_block(8, channels),
        ],
        [
            jax.ShapeDtypeStruct((total, channels), WIDE),
            jax.ShapeDtypeStruct((total, channels), LOW),
            jax.ShapeDtypeStruct((channels + PARCEL_ROWS, STATE), LOW),
            jax.ShapeDtypeStruct((count, 8, channels), WIDE),
        ],
        [pltpu.VMEM((channels, STATE), WIDE)],
        flops=total * channels * (2 * STATE + 60),
        moved=total * channels * 22,
    )(dn, y, cum, bc, x, projected, heads, gain)


def write_decays(parcel_ref, channels, last):
    high = jnp.broadcast_to(jnp.exp(last), (PARCEL_ROWS, LANES))
    top = high.astype(LOW).astype(WIDE)
    row = row_iota(high.shape)
    parcel_ref[channels:, :] = jnp.where(
        row == 0, top, jnp.where(row == 1, high - top, 0.0)
    ).astype(LOW)


def lane_sums(values):
    first = lane_iota(values.shape) < HDIM
    return (
        jnp.sum(jnp.where(first, values, 0.0), axis=1, keepdims=True),
        jnp.sum(jnp.where(first, 0.0, values), axis=1, keepdims=True),
    )


def scan_back_body(
    du_ref, x_ref, bc_ref, stk_ref, prior_ref, rim_ref, cum_ref, all_ref, step_ref, side_ref,
    first_ref, parcel_ref, later_ref, taps_ref, heads_ref,
    dstk_ref, drim_ref, dstep_ref, dtaps_ref, dheads_ref, padded, dact, after, behind,
):
    place = pl.program_id(0)
    second = jnp.where(place == 0, 1.0, 0.0).astype(WIDE)
    rows, channels = du_ref.shape
    heads = channels // HDIM
    width = channels + 2 * STATE
    entry, readout = bc_ref[:, :STATE], bc_ref[:, STATE:]
    cum, step = cum_ref[...], step_ref[...]
    cum_rows = cum.T
    last = cum[rows - 1 : rows, :]
    faded, arriving = jnp.exp(last), jnp.exp(all_ref[0:1, :] - cum[0:1, :])

    @pl.when(place == 0)
    def _():
        behind[...] = later_ref[:channels, :].astype(WIDE)
        after[8 + rows : 16 + rows, :] = jnp.zeros((8, width), WIDE)
        padded[0:8, :] = prior_ref[8:16, :].astype(WIDE)

    @pl.when(place > 0)
    def _():
        after[8 + rows : 16 + rows, :] = after[8:16, :]
        padded[0:8, :] = rim_ref[...]

    grown = jnp.exp(cum)
    decayed = jnp.exp(last - cum)
    tail = decayed * step
    cross = dot(entry, readout, 1, 1)
    shape = (rows, rows)
    causal = row_iota(shape) <= lane_iota(shape)
    lanes = lane_iota((rows, LANES))
    small = lane_iota((1, LANES))
    dcross = jnp.zeros(shape, WIDE)
    entry_grad = jnp.zeros((rows, STATE), WIDE)
    readout_grad = jnp.zeros((rows, STATE), WIDE)
    pulled = jnp.zeros((rows, LANES), WIDE)
    arrived = []
    carried_sum = jnp.zeros((rows, LANES), WIDE)
    final_sum = jnp.zeros((rows, LANES), WIDE)
    state_sum = jnp.zeros((1, LANES), WIDE)
    for pair in range(heads // 2):
        block = slice(pair * LANES, (pair + 1) * LANES)
        inputs = x_ref[:, block]
        inputs_wide = inputs.astype(WIDE)
        du = du_ref[:, block]
        du_low = du.astype(LOW)
        start = down_pair(arriving, pair) * parcel_ref[block, :].astype(WIDE)
        start = start + second * first_ref[block, :]
        later = behind[block, :]
        start_low, later_low = start.astype(LOW), later.astype(LOW)
        pulls = []
        for k in range(2):
            head = 2 * pair + k
            own = (lanes < HDIM) if k == 0 else (lanes >= HDIM)
            gap = cum_rows[head : head + 1, :] - cum[:, head : head + 1]
            decay = jnp.exp(jnp.where(causal, gap, MASKED))
            pulls.append(dot((decay * cross).astype(LOW), du_low))
            dmix = dot(jnp.where(own, inputs, jnp.zeros_like(inputs)), du_low, 1, 1) * decay
            stepped = step[:, head : head + 1]
            dcross = dcross + dmix * stepped
            dgap = dmix * cross
            pulled = jnp.where(lanes == head, jnp.sum(dgap, axis=1, keepdims=True), pulled)
            arrived.append(jnp.sum(dgap * stepped, axis=0, keepdims=True))
        pull = jnp.where(lanes < HDIM, pulls[0], pulls[1])
        grown_pair = over_pair(grown, pair, du.shape)
        grown_du = grown_pair * du
        grown_low = grown_du.astype(LOW)
        behind[block, :] = down_pair(faded, pair) * later + dot(grown_low, readout, 0, 0)
        readout_grad = readout_grad + dot(grown_low, start_low)
        sums = lane_sums(grown_du * dot(readout, start_low, 1, 1))
        carried_sum = jnp.where(lanes == 2 * pair, sums[0], carried_sum)
        carried_sum = jnp.where(lanes == 2 * pair + 1, sums[1], carried_sum)
        tail_pair = over_pair(tail, pair, du.shape)
        from_later = dot(entry, later_low, 1, 1)
        entry_grad = entry_grad + dot((tail_pair * inputs_wide).astype(LOW), later_low)
        sums = lane_sums(inputs_wide * from_later)
        final_sum = jnp.where(lanes == 2 * pair, sums[0], final_sum)
        final_sum = jnp.where(lanes == 2 * pair + 1, sums[1], final_sum)
        product = start * later
        for k in range(2):
            total = jnp.sum(
                jnp.sum(product[k * HDIM : (k + 1) * HDIM], axis=0, keepdims=True),
                axis=1,
                keepdims=True,
            )
            state_sum = jnp.where(small == 2 * pair + k, total, state_sum)
        skip = over_pair(heads_ref[2:3, :], pair, (1, LANES))
        dact[:, block] = (
            skip * du + over_pair(step, pair, du.shape) * pull + tail_pair * from_later
        )
    dcross_low = dcross.astype(LOW)
    dact[:, channels : channels + STATE] = entry_grad + dot(dcross_low, readout)
    dact[:, channels + STATE :] = readout_grad + dot(dcross_low, entry, 0, 0)
    arrived.append(jnp.zeros((LANES - heads, rows), WIDE))
    arrived_columns = jnp.concatenate(arrived, axis=0).T
    weighted = tail * final_sum
    dcum = arrived_columns - step * pulled + carried_sum - weighted
    at_last = jnp.sum(weighted, axis=0, keepdims=True) + faded * state_sum
    dcum = dcum + jnp.where(row_iota(dcum.shape) == rows - 1, at_last, 0.0)
    dlog = dot(lower_ones(rows, True), dcum, precision=HIGHEST)
    rate = jnp.exp(heads_ref[0:1, :])
    dstep = pulled + decayed * final_sum - rate * dlog
    dstep_pre = dstep * sigmoid(side_ref[...] + heads_ref[1:2, :])
    dstep_pre = jnp.where(lanes < heads, dstep_pre, 0.0)
    dstep_ref[...] = dstep_pre.astype(LOW)
    dheads_ref[...] = jnp.zeros(dheads_ref.shape, WIDE)
    dheads_ref[0:1, :] = -rate * jnp.sum(step * dlog, axis=0, keepdims=True)
    dheads_ref[1:2, :] = jnp.sum(dstep_pre, axis=0, keepdims=True)

    padded[8 : 8 + rows, :] = stk_ref[...].astype(WIDE)
    before = convolved(padded, taps_ref, rows)
    sigma = sigmoid(before)
    dbefore = dact[...] * sigma * (1.0 + before * (1.0 - sigma))
    after[0:8, :] = jnp.zeros((8, width), WIDE)
    after[8 : 8 + rows, :] = dbefore
    dtaps_ref[...] = jnp.zeros(dtaps_ref.shape, WIDE)
    back = None
    for j in range(CONV):
        first = 8 - CONV + 1 + j
        dtaps_ref[j : j + 1, :] = jnp.sum(
            after[8 : 8 + rows, :] * padded[first : first + rows, :], axis=0, keepdims=True
        )
        first = CONV - 1 - j
        term = taps_ref[j : j + 1, :] * after[first : first + rows + 8, :]
        back = term if back is None else back + term
    dtaps_ref[CONV : CONV + 1, :] = jnp.sum(after[8 : 8 + rows, :], axis=0, keepdims=True)
    drim_ref[...] = back[0:8]
    dstk_ref[...] = back[8:]


def scan_back(
    du, x, bc, stk, rim, cum, all_cum, step, side, first, parcel, later, taps, heads, rows
):
    total, channels = du.shape
    count = total // rows
    width = channels + 2 * STATE

    def back_block(cols, col=0):
        return pl.BlockSpec((rows, cols), lambda s: (count - 1 - s, col))

    return kernel_call(
        scan_back_body,
        (count,),
        [
            back_block(channels),
            back_block(channels),
            back_block(2 * STATE),
            back_block(width),
            pl.BlockSpec((16, width), lambda s: (rows // 16 - 1, 0)),
            whole((8, width)),
            back_block(LANES),
            back_block(LANES),
            back_block(LANES),
            back_block(LANES, 2 * STATE // LANES),
            whole((channels, STATE)),
            whole((channels + PARCEL_ROWS, STATE)),
            whole((channels + PARCEL_ROWS, STATE)),
            whole((8, width)),
            whole((8, LANES)),
        ],
        [
            back_block(width),
            whole((8, width)),
            back_block(LANES),
            sequence_block(8, width),
            sequence_block(8, LANES),
        ],
        [
            jax.ShapeDtypeStruct((total, width), WIDE),
            jax.ShapeDtypeStruct((8, width), WIDE),
            jax.ShapeDtypeStruct((total, LANES), LOW),
            jax.ShapeDtypeStruct((count, 8, width), WIDE),
            jax.ShapeDtypeStruct((count, 8, LANES), WIDE),
        ],
        [
            pltpu.VMEM((rows + 8, width), WIDE),
            pltpu.VMEM((rows, width), WIDE),
            pltpu.VMEM((rows + 16, width), WIDE),
            pltpu.VMEM((channels, STATE), WIDE),
        ],
        flops=total * rows * channels * 20,
        moved=total * width * 24,
    )(du, x, bc, stk, stk, rim, cum, all_cum, step, side, first, parcel, later, taps, heads)


def unit_scale(values):
    return lax.rsqrt(jnp.mean(values * values, axis=-1, keepdims=True) + EPSILON)


def normalize(values, gain):
    return (values * unit_scale(values) * gain).astype(LOW)


def norm_grad_body(
    kept_ref, gain_ref, own_ref, peer_ref, base_ref, out_ref, low_ref, sums_ref
):
    kept = kept_ref[...]
    scale = unit_scale(kept)
    unit = kept * scale
    upstream = own_ref[...].astype(WIDE) + peer_ref[...].astype(WIDE)
    scaled = upstream * gain_ref[...]
    inner = jnp.mean(scaled * unit, axis=-1, keepdims=True)
    out = base_ref[...] + scale * (scaled - unit * inner)
    out_ref[...] = out
    low_ref[...] = out.astype(LOW)
    sums = jnp.sum(upstream * unit, axis=0, keepdims=True)

    @pl.when(pl.program_id(0) == 0)
    def _():
        sums_ref[...] = jnp.broadcast_to(sums, sums_ref.shape)

    @pl.when(pl.program_id(0) > 0)
    def _():
        sums_ref[...] += jnp.broadcast_to(sums, sums_ref.shape)


def norm_grad(kept, gain, partial_grad, base):
    own = partial_grad.astype(LOW)
    rows, features = kept.shape
    tile = min(rows, 256)
    out, low, sums = kernel_call(
        norm_grad_body,
        (rows // tile,),
        [rows_block(tile, features), whole((1, features))] + [rows_block(tile, features)] * 3,
        [rows_block(tile, features), rows_block(tile, features), whole((8, features))],
        [
            jax.ShapeDtypeStruct((rows, features), WIDE),
            jax.ShapeDtypeStruct((rows, features), LOW),
            jax.ShapeDtypeStruct((8, features), WIDE),
        ],
        flops=rows * features * 12,
        moved=rows * features * 18,
    )(kept, gain[None], own, tp_peer(own), base)
    return out, low, sums[0]


def product(a, b):
    return jnp.dot(a, b, preferred_element_type=WIDE)


def against_rows(a, b):
    return dot(a, b, 1, 1)


def halves(values):
    cut = half_lanes(values.shape[1])
    return values[:, :cut], values[:, cut:]


def over_rows(a, b):
    return dot(a, b, 0, 0).astype(LOW)


def weight_rows(layer, pieces):
    zx, mix, attn, attn_out, mlp, mlp_out = (p[layer] for p in pieces)
    rows = zx.shape[0]
    return (
        jnp.concatenate([zx.reshape(rows, -1), attn.reshape(rows, -1)], axis=1),
        jnp.concatenate([mix.T, attn_out.T], axis=1),
        mlp.reshape(rows, -1),
        mlp_out.T,
    )


def own_part(values, size, axis):
    return lax.dynamic_slice_in_dim(values, lax.axis_index("tp") * size, size, axis)


def padded_to(values, rows, lanes):
    return jnp.pad(values, ((0, rows - values.shape[0]), (0, lanes - values.shape[1])))


def local_small(order, layer, norm_gains, mamba_shared, conv_weight, conv_bias, head_params, mamba_gain):
    tp = lax.axis_size("tp")
    heads = head_params.shape[2] // tp
    full_ssm = mamba_gain.shape[1]
    channels = full_ssm // tp
    shared_all = mamba_shared[layer]
    shared = jnp.concatenate(
        [
            shared_all[:, : 2 * STATE],
            own_part(shared_all[:, 2 * STATE :], heads, 1),
            jnp.zeros((shared_all.shape[0], LANES - heads), LOW),
        ],
        axis=1,
    )
    taps_all = jnp.concatenate([conv_weight[layer], conv_bias[layer][None]], axis=0).astype(WIDE)
    taps = jnp.concatenate(
        [own_part(taps_all[:, :full_ssm], channels, 1), taps_all[:, full_ssm:]], axis=1
    )
    return (
        product(norm_gains[layer], order),
        dot(order, shared, 0, 0).astype(LOW),
        padded_to(taps, 8, taps.shape[1]),
        padded_to(own_part(head_params[layer], heads, 1), 8, LANES),
        own_part(mamba_gain[layer].astype(WIDE), channels, 0)[None],
    )


def layer_forward(hidden, layer, gathers, late, small, tables, place, sequences, moves):
    zx_w = gathers.take(2 * layer)
    gains, shared, taps, heads, gain = small
    rows = hidden.shape[0] // sequences
    channels = gain.shape[1]
    head_count = channels // HDIM
    normed = normalize(hidden, gains[0])
    projected = product(normed, zx_w)
    side = product(normed, shared)
    if layer == 0:
        late[:], projected = together(late, projected)
        late[:] = [lax.all_gather(v, "fsdp", axis=1).reshape(-1, v.shape[-1]) for v in late]
    mlp_out_w = late[layer]
    edge = jnp.concatenate(
        [projected[-CONV + 1 :, channels : 2 * channels], side[-CONV + 1 :, : 2 * STATE]], axis=1
    )
    came = next_half(edge.astype(LOW), True).astype(WIDE)
    rim = jnp.pad(came, ((8 - CONV + 1, 0), (0, 0)))
    queries, kv = split_qkv(projected, tables, rows, 2 * channels // (zx_w.shape[1] - 2 * channels))
    kv_came = next_half(kv, True)
    (kv_came,), rim = together((kv_came,), rim)
    rim = gathers.begin(rim)
    stk, x, bc, y_local, first, parcel_out, cum, all_cum, step = scan_local(
        projected, side, rim, taps, heads, rows, channels
    )
    parcel = next_half(parcel_out, True)
    attended, log_total = attend(place, queries, kv, kv_came, rows)
    if layer > 0:
        moves, parcel = together(moves, parcel)
        mlp_w = late[len(late) // 2 + layer]
        (mlp_w,), parcel = together((mlp_w,), parcel)
    (attended, parcel), y_local = together((attended, parcel), y_local)
    parcel = gathers.step(parcel)
    parcel = gathers.begin(parcel)
    y, mamba_norm = gate_tail(y_local, all_cum, bc, x, projected, heads, gain, parcel, rows)
    both = jnp.concatenate([mamba_norm, attended], axis=1)
    rest = gathers.take(2 * layer + 1)
    mix_w = rest[:, : both.shape[1]]
    if layer == 0:
        mlp_w = rest[:, both.shape[1] :]
    else:
        (mlp_out_w,), both = together((mlp_out_w,), both)
    after_mix = hidden + tp_sum(against_rows(both, mix_w))
    normed_two = normalize(after_mix, gains[1])
    gate_up = product(normed_two, mlp_w)
    ff = gate_up.shape[1] // 2
    activated = (jax.nn.silu(gate_up[:, :ff]) * gate_up[:, ff:]).astype(LOW)
    if gathers.near[-1] is None:
        activated = gathers.step(activated)
    result = after_mix + tp_sum(against_rows(activated, mlp_out_w))
    saved = (
        hidden, normed, projected, side, rim, queries, kv, kv_came, stk, x, bc, cum, all_cum, step,
        first, parcel, log_total, y, both, after_mix, normed_two, gate_up, activated,
    )
    return result, saved, (zx_w, mix_w, mlp_w, mlp_out_w), moves


def layer_backward(
    upstream, grad_mlp, saved, weights, small, tables, place, sequences, scatters, split, done, extra
):
    (
        hidden, normed, projected, side, rim, queries, kv, kv_came, stk, x, bc, cum, all_cum, step,
        first, parcel, log_total, y, both, after_mix, normed_two, gate_up, activated,
    ) = saved
    zx_w, mix_w, mlp_w, mlp_out_w = weights
    gains, shared, taps, heads, gain = small
    rows = hidden.shape[0] // sequences
    channels = gain.shape[1]
    head_count = channels // HDIM
    grad_act = product(grad_mlp, mlp_out_w)
    ff = grad_act.shape[1]
    gate_part, up_part = gate_up[:, :ff], gate_up[:, ff:]
    sigma = jax.nn.sigmoid(gate_part)
    grad_gu = jnp.concatenate(
        [
            grad_act * up_part * sigma * (1.0 + gate_part * (1.0 - sigma)),
            grad_act * gate_part * sigma,
        ],
        axis=1,
    ).astype(LOW)
    table = scatters.add_fsdp_first(normed_two, grad_gu, 2, functools.partial(done, 3))
    _, grad_gu = together((table,), grad_gu)
    grad_mid, grad_mix, grad_gain_two = norm_grad(
        after_mix, gains[1], against_rows(grad_gu, mlp_w), upstream
    )
    grad_mid = scatters.step(grad_mid)
    if extra:
        extra[:], grad_mix = together(extra, grad_mix)
    table = scatters.add(
        [(grad_mlp, activated), (grad_mix, both)],
        512,
        None if split else False,
        (0, 0),
        functools.partial(done, 0),
    )
    _, grad_mix = together((table,), grad_mix)
    grad_norm = product(grad_mix, mix_w[:, :channels])
    grad_attended = product(grad_mix, mix_w[:, channels:]).astype(LOW)
    du, grad_gate, state_grads, tail_sums = gate_tail_back(
        grad_norm, y, all_cum, bc, x, projected, heads, gain, rows
    )
    later = next_half(state_grads, False)
    grad_q, own_kv, sent_kv = attend_back(
        place, queries, grad_attended, log_total, tables, kv, kv_came, rows
    )
    came_kv = [next_half(sent_kv, False)]
    (later, *came_kv), grad_gate = together((later, *came_kv), grad_gate)
    later = scatters.step(later)
    if split:
        mid = jnp.concatenate([grad_gate, grad_q], axis=1)
        table = scatters.add([(normed, mid)], 512, True, (0, 0), functools.partial(done, 2))
        _, later = together((table,), later)
    dstk, drim, grad_step, dtaps, dheads = scan_back(
        du, x, bc, stk, rim, cum, all_cum, step, side, first, parcel, later, taps, heads, rows
    )
    drim = scatters.step(drim)
    returned = next_half(drim[8 - CONV + 1 :], False)
    dstk = dstk + jnp.pad(returned, ((dstk.shape[0] - CONV + 1, 0), (0, 0)))
    grad_kv = finish_keys(own_kv, came_kv, tables, rows)
    grad_late = jnp.concatenate([dstk[:, :channels].astype(LOW), grad_kv], axis=1)
    grad_first = jnp.concatenate(
        [grad_gate, grad_late[:, :channels], grad_q, grad_late[:, channels:]], axis=1
    )
    grad_side = jnp.concatenate([dstk[:, channels:].astype(LOW), grad_step], axis=1)
    if split:
        late, tile = [grad_late, grad_side], 640
    else:
        late = [grad_gate, grad_q, grad_late[:, channels:], grad_late[:, :channels], grad_side]
        tile = 384
    late = jnp.concatenate(late, axis=1)
    table = scatters.add([(normed, late)], tile, split, (0, 0), functools.partial(done, 1))
    _, grad_first = together((table,), grad_first)
    below, grad_mlp, grad_gain_one = norm_grad(
        hidden,
        gains[0],
        against_rows(grad_first, zx_w) + against_rows(grad_side, shared),
        grad_mid,
    )
    tail_sums = jnp.sum(tail_sums, axis=0)
    dheads = jnp.sum(dheads, axis=0)
    skip_grad = jnp.sum(tail_sums[1].reshape(head_count, HDIM), axis=1)
    skip_grad = jnp.pad(skip_grad, (0, LANES - head_count))[None]
    small_grads = (
        jnp.stack([grad_gain_one, grad_gain_two]),
        jnp.sum(dtaps, axis=0),
        jnp.where(row_iota(dheads.shape) == 2, skip_grad, dheads),
        tail_sums[0],
    )
    below, grad_mlp = scatters.step((below, grad_mlp))
    return below, grad_mlp, small_grads


def tp_ordered(a, b):
    low_half = lax.axis_index("tp") == 0
    return jnp.where(
        low_half, jnp.concatenate([a, b], axis=-1), jnp.concatenate([b, a], axis=-1)
    )


def settle_side(scatters, sums, half_heads, done):
    def run():
        fsdp = lax.axis_size("fsdp")
        layers = sums
        own = layers[0]
        rows = own.shape[0]
        wide = jnp.stack([v[:, : 2 * STATE].reshape(rows, 2, STATE) for v in layers])
        place = lax.axis_index("tp")
        (came,) = yield (tp_peer(pick(wide, 1 - place, 2)),), 0, ()
        mine = pick(wide, place, 2) + came
        steps = jnp.stack([v[:, 2 * STATE : 2 * STATE + half_heads] for v in layers]).reshape(-1)
        packed = jnp.concatenate([mine.reshape(-1), steps])
        packed = jnp.pad(packed, (0, -packed.size % (16 * LANES))).reshape(-1, LANES)
        joined = yield from join_rows(packed.astype(LOW))
        (theirs,) = yield (tp_peer(joined),), 0, ()
        count = len(layers)
        places = fsdp * lax.axis_size("ctx")

        def taken(values):
            flat = values.reshape(places, -1)
            wide_size = count * rows * STATE
            first = flat[:, :wide_size].reshape(places, count, rows, STATE)
            second = flat[:, wide_size : wide_size + count * rows * half_heads]
            return first, second.reshape(places, count, rows, half_heads)

        (wide_own, step_own), (wide_peer, step_peer) = taken(joined), taken(theirs)
        full = jnp.concatenate(
            [tp_ordered(wide_own, wide_peer), tp_ordered(step_own, step_peer)], axis=-1
        )
        done(full.transpose(1, 0, 2, 3).reshape(count, places * rows, -1).astype(WIDE))

    scatters.begin(run())


def settle_small(scatters, small_grads, half_heads, done):
    def run():
        layers = len(small_grads)
        shapes = [v.shape for v in small_grads[0]]
        flat = [v.reshape(-1, LANES) for grads in small_grads for v in grads]
        flat = [jnp.pad(v, ((0, -v.shape[0] % 8), (0, 0))) for v in flat]
        packed = yield from sum_everywhere(jnp.concatenate(flat, axis=0))
        (packed_peer,) = yield (tp_peer(packed),), 0, ()
        own, peer = [], []
        first = 0
        for values, shape in zip(flat, shapes * layers):
            for source, parts in ((packed, own), (packed_peer, peer)):
                piece = source[first : first + math.prod(shape) // LANES]
                parts.append(piece.reshape(shape))
            first += values.shape[0]
        count = len(shapes)
        for l in range(layers):
            (gains, taps, heads, gain), (gains_p, taps_p, heads_p, gain_p) = (
                v[l * count : (l + 1) * count] for v in (own, peer)
            )
            channels = gain.shape[0]
            taps_full = jnp.concatenate(
                [
                    tp_ordered(taps[:, :channels], taps_p[:, :channels]),
                    taps[:, channels:] + taps_p[:, channels:],
                ],
                axis=1,
            )
            done(
                l,
                (
                    jnp.where(lax.axis_index("tp") == 0, gains, gains_p),
                    taps_full[:CONV],
                    taps_full[CONV],
                    tp_ordered(heads[:3, :half_heads], heads_p[:3, :half_heads]),
                    tp_ordered(gain, gain_p),
                ),
            )

    scatters.begin(run())


def local(
    hidden_in, lengths, norm_gains, mamba_zx, mamba_shared, conv_weight, conv_bias, head_params,
    mamba_gain, mamba_out, attn_in, attn_out, mlp_in, mlp_out, out_grad,
):
    layers = norm_gains.shape[0]
    micro, own_seqs, rows, features = hidden_in.shape
    sequences = micro * own_seqs
    full_ssm = mamba_gain.shape[1]
    heads_total = head_params.shape[2]
    ctx_place = lax.axis_index("ctx")
    place = (ctx_place % 2).astype(jnp.int32).reshape(1)
    start_row = ctx_place % 2 * rows * 2
    pieces = (mamba_zx, mamba_out, attn_in, attn_out, mlp_in, mlp_out)
    shards = [weight_rows(l, pieces) for l in range(layers)]
    quarters = (sequences, rows, features)
    moves = to_halves_moves(hidden_in.reshape(quarters))
    first_shards = [shards[0][0], jnp.concatenate(shards[0][1:3], axis=1)]
    first_shards += [shards[l][i] for l in range(1, layers) for i in range(2)]
    late_pieces = [shards[l][3] for l in range(layers)] + [shards[l][2] for l in range(1, layers)]
    came = fsdp_moves(first_shards[0])
    late_block = jnp.concatenate(late_pieces, axis=1)[None]
    near = spread_first(late_block)
    moved = lax.optimization_barrier(moves + came + near)
    given = to_halves(*moved[:2])
    first_block = fsdp_join(first_shards[0], moved[2:-2])
    blocks, first_block = gathered_blocks(first_shards, first_block)
    gathers = Gathers([first_block] + blocks)
    late = gathered_ctx(late_block, moved[-2:], [v.shape[1] for v in late_pieces])
    small_args = (norm_gains, mamba_shared, conv_weight, conv_bias, head_params, mamba_gain)
    gathers.near[0], (given, small_args, start_row) = together(
        gathers.near[0], (given, small_args, start_row)
    )
    tables = turn_tables(start_row, 2 * rows)
    order = own_order(features * lax.axis_size("tp"), LOW)
    smalls = [
        local_small(order, l, *small_args)
        for l in range(layers)
    ]
    length = pick(lengths.reshape(sequences), ctx_place // 2, 0)
    keep = (start_row + jnp.arange(2 * rows) < length).astype(WIDE)[:, None]
    hidden = product(tp_join(given), order)
    saved, weights = [], []
    for l in range(layers):
        if l == layers - 1:
            (cotangent,), hidden = together((out_grad.reshape(quarters),), hidden)
            moves = to_halves_moves(cotangent)
        hidden, kept, used, moves = layer_forward(
            hidden, l, gathers, late, smalls[l], tables, place, sequences, moves
        )
        saved.append(kept)
        weights.append(used)
    upstream = product(tp_join(to_halves(*moves)), order) * keep
    own_rows = own_part(order, features, 0)
    mixed_out = against_rows((hidden * keep).astype(LOW), own_rows).astype(LOW)
    mixed_out = to_quarters(mixed_out)
    big, rest = [[None] * 4 for _ in range(layers)], [None] * layers
    scatters = Scatters()
    side_total = []

    def finished(layer, part, total):
        big[layer][part] = total
        if layer == 0 and part == 1:
            sides = [big[l][1][:, -3 * LANES :] for l in range(layers)]
            settle_side(scatters, sides, heads_total // lax.axis_size("tp"), side_total.append)

    small_grads = [None] * layers
    grad_low = upstream.astype(LOW)
    extra = [mixed_out]
    for l in reversed(range(layers)):
        upstream, grad_low, small_grads[l] = layer_backward(
            upstream, grad_low, saved[l], weights[l], smalls[l], tables, place, sequences,
            scatters, l == 0, functools.partial(finished, l), extra if l == layers - 1 else [],
        )
    input_grad = dot(upstream, own_rows.astype(WIDE), 1, 1, HIGHEST)
    input_grad = to_quarters(input_grad.astype(LOW)).astype(WIDE).reshape(hidden_in.shape)
    gains = jnp.concatenate([grads[0] for grads in small_grads], axis=0)
    gains = dot(gains, order.astype(WIDE), 1, 1, HIGHEST)
    small_grads = [
        (gains[2 * l : 2 * l + 2],) + small_grads[l][1:] for l in range(layers)
    ]
    settle_small(
        scatters, small_grads, heads_total // lax.axis_size("tp"), rest.__setitem__
    )
    scatters.finish()
    channels = mamba_out.shape[1]
    ff = mlp_out.shape[1]
    zx_grads, attn_grads, mix_grads, up_grads, down_grads = [], [], [], [], []
    for l in range(layers):
        early, late, mid, up = big[l]
        half = early.shape[1] // 2
        firsts, seconds = early[:, :half], early[:, half:]

        def rejoined(first, last):
            return jnp.concatenate([firsts[:, first:last], seconds[:, first:last]], axis=1)

        down_grads.append(rejoined(0, ff // 2).T)
        up_grads.append(up)
        both = rejoined(ff // 2, half)
        mix_grads.append((both[:, :channels].T, both[:, channels:].T))
        if mid is None:
            half = late.shape[1] // 2
            gate, x_part = late[:, :channels], late[:, half : half + channels]
            attn_grads.append(late[:, channels:half])
        else:
            gate, x_part = mid[:, :channels], late[:, :channels]
            keys = late[:, channels : channels + LANES]
            attn_grads.append(jnp.concatenate([mid[:, channels:], keys], axis=1))
        zx_grads.append(jnp.concatenate([gate, x_part], axis=1))

    def stacked(pick):
        return jnp.stack([pick(l) for l in range(layers)])

    return (
        extra[0].reshape(hidden_in.shape),
        input_grad,
        stacked(lambda l: rest[l][0]),
        jnp.stack(zx_grads).reshape(mamba_zx.shape),
        side_total[0],
        stacked(lambda l: rest[l][1]),
        stacked(lambda l: rest[l][2]),
        stacked(lambda l: rest[l][3]),
        stacked(lambda l: rest[l][4]),
        stacked(lambda l: mix_grads[l][0]),
        jnp.stack(attn_grads).reshape(attn_in.shape),
        stacked(lambda l: mix_grads[l][1]),
        jnp.stack(up_grads).reshape(mlp_in.shape),
        jnp.stack(down_grads),
    )


def solution(mesh):
    placed = (
        P(None, "fsdp", "ctx", "tp"),
        P(None, "fsdp"),
        P(),
        P(None, ("fsdp", "ctx"), None, "tp"),
        P(),
        P(),
        P(),
        P(),
        P(),
        P(None, "tp", ("fsdp", "ctx")),
        P(None, ("fsdp", "ctx"), "tp", None),
        P(None, "tp", ("fsdp", "ctx")),
        P(None, ("fsdp", "ctx"), None, "tp"),
        P(None, "tp", ("fsdp", "ctx")),
        P(None, "fsdp", "ctx", "tp"),
    )
    return jax.shard_map(
        local,
        mesh=mesh,
        in_specs=placed,
        out_specs=(
            P(None, "fsdp", "ctx", "tp"),
            P(None, "fsdp", "ctx", "tp"),
            P(),
            P(None, ("fsdp", "ctx"), None, "tp"),
            P(),
            P(),
            P(),
            P(),
            P(),
            P(None, "tp", ("fsdp", "ctx")),
            P(None, ("fsdp", "ctx"), "tp", None),
            P(None, "tp", ("fsdp", "ctx")),
            P(None, ("fsdp", "ctx"), None, "tp"),
            P(None, "tp", ("fsdp", "ctx")),
        ),
        check_vma=False,
    )
```

```python
import functools
import math

import jax
import jax.numpy as jnp
from jax import lax
from jax.experimental import pallas as pl
from jax.experimental.pallas import tpu as pltpu
from jax.sharding import PartitionSpec as P

HDIM = 64
STATE = 128
CONV = 4
ADIM = 64
GROUP = 4
LANES = 128
EPSILON = 1e-05
THETA = 100000000000.0
HIGHEST = lax.Precision.HIGHEST
LOW = jnp.bfloat16
WIDE = jnp.float32
MASKED = -1e30
VMEM_LIMIT = 56 * 1024 * 1024
PARCEL_ROWS = 16


def dot(a, b, ca=1, cb=0, precision=None):
    return lax.dot_general(
        a, b, (((ca,), (cb,)), ((), ())), preferred_element_type=WIDE, precision=precision
    )


def lane_iota(shape):
    return lax.broadcasted_iota(jnp.int32, shape, len(shape) - 1)


def row_iota(shape):
    return lax.broadcasted_iota(jnp.int32, shape, 0)


def kernel_call(body, grid, in_specs, out_specs, out_shape, scratch=(), flops=0, moved=0):
    return pl.pallas_call(
        body,
        grid=grid,
        in_specs=in_specs,
        out_specs=out_specs,
        out_shape=out_shape,
        scratch_shapes=list(scratch),
        compiler_params=pltpu.CompilerParams(vmem_limit_bytes=VMEM_LIMIT),
        cost_estimate=pl.CostEstimate(flops=flops, bytes_accessed=moved, transcendentals=0),
    )


def whole(shape):
    return pl.BlockSpec(shape, lambda s: (0,) * len(shape))


def rows_block(rows, cols, col=0):
    return pl.BlockSpec((rows, cols), lambda s: (s, col))


def sequence_block(*shape):
    return pl.BlockSpec((None,) + shape, lambda s: (s,) + (0,) * len(shape))


def xor_pairs(count, bit):
    return [(i, i ^ bit) for i in range(count)]


def next_half(x, forward):
    firsts = range(0, lax.axis_size("ctx"), 2)
    return lax.ppermute(x, "ctx", [(i, i + 1) if forward else (i + 1, i) for i in firsts])


STRAIGHT = ((0, 0), (2, 1), (1, 2), (3, 3))
CROSSED = ((1, 0), (3, 1), (0, 2), (2, 3))


def to_halves_moves(quarters):
    place = lax.axis_index("ctx")
    a = lax.ppermute(pick(quarters, place % 2, 0), "ctx", STRAIGHT)
    b = lax.ppermute(pick(quarters, 1 - place % 2, 0), "ctx", CROSSED)
    return a, b


def to_halves(a, b):
    place = lax.axis_index("ctx")
    return jnp.where(place < 2, jnp.concatenate([a, b]), jnp.concatenate([b, a]))


def to_quarters(half):
    place = lax.axis_index("ctx")
    parts = half.reshape((2, -1) + half.shape[1:])
    late = place // 2
    a = lax.ppermute(pick(parts, late, 0), "ctx", [(j, i) for i, j in STRAIGHT])
    b = lax.ppermute(pick(parts, 1 - late, 0), "ctx", [(j, i) for i, j in CROSSED])
    return jnp.where(place % 2 == 0, jnp.stack([a, b]), jnp.stack([b, a]))


def tp_peer(x):
    return lax.ppermute(x, "tp", xor_pairs(lax.axis_size("tp"), 1))


def tp_join(x):
    peer = tp_peer(x)
    first = lax.axis_index("tp") == 0
    return jnp.where(
        first, jnp.concatenate([x, peer], axis=-1), jnp.concatenate([peer, x], axis=-1)
    )


def tp_sum(partial_sum):
    low = partial_sum.astype(LOW)
    peer = tp_peer(low)
    return low.astype(WIDE) + peer.astype(WIDE)


def bits_of(axis):
    return [1 << i for i in range(lax.axis_size(axis).bit_length() - 1)]


def together(values, anchor):
    return lax.optimization_barrier((tuple(values), anchor))


def added(*parts):
    total = parts[0].astype(WIDE)
    for part in parts[1:]:
        total = total + part.astype(WIDE)
    return total


def ctx_swap(values, step):
    return lax.ppermute(values, "ctx", xor_pairs(lax.axis_size("ctx"), step))


def pick(values, place, dim):
    return lax.dynamic_index_in_dim(values, place, dim, False)


def half_lanes(width):
    return width // 256 * 128


FLIPS = (0, 1, 3, 2)


def own_order(features, dtype):
    fsdp, ctx = lax.axis_size("fsdp"), lax.axis_size("ctx")
    rows = features // (fsdp * ctx)
    own = jnp.arange(features)
    flip, rest = jnp.array(FLIPS)[own // (fsdp * rows)], own % (fsdp * rows)
    common = (rest // rows) * ctx * rows + (flip ^ lax.axis_index("ctx")) * rows + rest % rows
    return (jnp.arange(features)[:, None] == common[None, :]).astype(dtype)


def spread_first(block):
    return ctx_swap(block, 1), ctx_swap(block, 2)


def spread_parts(came):
    cut = half_lanes(came[0].shape[-1])
    return came[0][..., :cut], came[1][..., cut:]


def spread_second(parts):
    return ctx_swap(parts[0], 2), ctx_swap(parts[1], 1)


def spread_whole(block, came, far):
    width = block.shape[-1]
    return jnp.concatenate(
        [v.reshape(-1, width) for v in (block, came[0], jnp.concatenate(far, axis=-1), came[1])], axis=0
    )


def fsdp_moves(piece):
    count = lax.axis_size("fsdp")
    if count > 4:
        return ()
    return tuple(lax.ppermute(piece, "fsdp", xor_pairs(count, step)) for step in range(1, count))


def fsdp_join(piece, came):
    if not came:
        return lax.all_gather(piece, "fsdp", axis=0)
    place = lax.axis_index("fsdp")
    shape = (len(came) + 1,) + piece.shape
    out = lax.dynamic_update_index_in_dim(jnp.zeros(shape, piece.dtype), piece, place, 0)
    for step, values in enumerate(came, 1):
        out = lax.dynamic_update_index_in_dim(out, values, place ^ step, 0)
    return out


def gathered_blocks(pieces, anchor):
    following, anchor = together((pieces[1], jnp.concatenate(pieces[2:], axis=1)), anchor)
    blocks = [lax.all_gather(following[0], "fsdp", axis=0)]
    rest = lax.all_gather(following[1], "fsdp", axis=0)
    first = 0
    for piece in pieces[2:]:
        blocks.append(rest[..., first : first + piece.shape[1]])
        first += piece.shape[1]
    return blocks, anchor


class Gathers:
    def __init__(self, blocks):
        self.blocks = blocks
        self.near = [None] * len(blocks)
        self.far = [None] * len(blocks)
        self.first = 0
        self.near[0] = spread_first(self.blocks[0])

    def step(self, anchor):
        i = self.first
        if i >= len(self.blocks):
            return anchor
        self.near[i], anchor = together(self.near[i], anchor)
        parts = spread_parts(self.near[i])
        self.far[i] = spread_second(parts)
        _, anchor = together(parts, anchor)
        self.first = i + 1
        return anchor

    def begin(self, anchor):
        i = self.first
        if i < len(self.blocks) and self.near[i] is None:
            (self.blocks[i],), anchor = together((self.blocks[i],), anchor)
            self.near[i] = spread_first(self.blocks[i])
        return anchor

    def take(self, i):
        if self.first <= i:
            self.step(self.near[i][0])
        return spread_whole(self.blocks[i], self.near[i], self.far[i])


def gathered_ctx(block, near, widths):
    far = spread_second(spread_parts(near))
    rows = spread_whole(block, near, far).reshape((4,) + block.shape[1:])
    out, first = [], 0
    for width in widths:
        out.append(rows[..., first : first + width])
        first += width
    return out


def table_body(spans, *refs):
    count = len(spans)
    left_refs, a_refs, b_refs = (refs[i * count : (i + 1) * count] for i in range(3))
    up_ref, across_ref, x_ref, y_ref, own_a_ref, own_b_ref, turned_ref = refs[3 * count :]
    size = own_a_ref.shape[0]
    place = pl.program_id(0)
    for left_ref, a_ref, b_ref, (first, last) in zip(left_refs, a_refs, b_refs, spans):

        @pl.when(place == first)
        def _(left_ref=left_ref):
            turned_ref[...] = left_ref[...].astype(WIDE).T.astype(LOW)

        @pl.when((place >= first) & (place < last))
        def _(a_ref=a_ref, b_ref=b_ref):
            table = dot(turned_ref[...], a_ref[...]).astype(LOW)
            own_a_ref[...] = table[:size]
            x_ref[...] = table[size : 2 * size]
            up_ref[...] = table[2 * size :]
            table = dot(turned_ref[...], b_ref[...]).astype(LOW)
            own_b_ref[...] = table[:size]
            across_ref[...] = table[size : 3 * size]
            y_ref[...] = table[3 * size :]


def tables(pairs, tile):
    rows, features = pairs[0][0].shape
    size = features // len(FLIPS)
    spans, first = [], 0
    for _, right in pairs:
        spans.append((first, first + right.shape[1] // (2 * tile)))
        first = spans[-1][1]
    width = first * tile

    def columns(first, last, skip):
        return pl.BlockSpec(
            (rows, tile), lambda j: (0, skip + jnp.clip(j, first, last - 1) - first)
        )

    def tall(height):
        return pl.BlockSpec((height, tile), lambda j: (0, j))

    heights = (2 * size, 2 * size, size, size, size, size)
    return kernel_call(
        functools.partial(table_body, tuple(spans)),
        (first,),
        [whole((rows, features))] * len(pairs)
        + [columns(*span, 0) for span in spans]
        + [columns(*span, span[1] - span[0]) for span in spans],
        [tall(h) for h in heights],
        [jax.ShapeDtypeStruct((h, width), LOW) for h in heights],
        [pltpu.VMEM((features, rows), LOW)],
        flops=4 * rows * features * width,
        moved=width * (4 * rows + 4 * features),
    )(*[p[0] for p in pairs], *[p[1] for p in pairs], *[p[1] for p in pairs])


def fsdp_table_body(left_ref, right_ref, out_ref, turned_ref):
    @pl.when(pl.program_id(0) == 0)
    def _():
        turned_ref[...] = left_ref[...].astype(WIDE).T.astype(LOW)

    table = dot(turned_ref[...], right_ref[...])
    fsdp, flips, rows, _ = out_ref.shape
    for flip in range(flips):
        for place in range(fsdp):
            first = (flip * fsdp + place) * rows
            out_ref[place, flip] = table[first : first + rows].astype(LOW)


def fsdp_table(left, right, tile):
    rows, features = left.shape
    width = right.shape[1]
    fsdp, flips = lax.axis_size("fsdp"), len(FLIPS)
    shape = (fsdp, flips, features // (fsdp * flips))
    return kernel_call(
        fsdp_table_body,
        (width // tile,),
        [whole((rows, features)), pl.BlockSpec((rows, tile), lambda j: (0, j))],
        pl.BlockSpec(shape + (tile,), lambda j: (0, 0, 0, j)),
        jax.ShapeDtypeStruct(shape + (width,), LOW),
        [pltpu.VMEM((features, rows), LOW)],
        flops=2 * rows * features * width,
        moved=width * (2 * rows + 2 * features),
    )(left, right)


def pass_body(x_ref, y_ref, from_y_ref, from_x_ref, to_x_ref, to_y_ref):
    size = x_ref.shape[0]
    to_x_ref[...] = (x_ref[...].astype(WIDE) + from_y_ref[:size].astype(WIDE)).astype(LOW)
    to_y_ref[...] = (y_ref[...].astype(WIDE) + from_x_ref[size:].astype(WIDE)).astype(LOW)


def keep_body(own_a_ref, own_b_ref, from_y_ref, from_x_ref, last_x_ref, last_y_ref, out_ref):
    size, width = own_a_ref.shape
    out_ref[:, :width] = (
        own_a_ref[...].astype(WIDE) + from_y_ref[size:].astype(WIDE) + last_x_ref[...].astype(WIDE)
    ).astype(LOW)
    out_ref[:, width:] = (
        own_b_ref[...].astype(WIDE) + from_x_ref[:size].astype(WIDE) + last_y_ref[...].astype(WIDE)
    ).astype(LOW)


def once(body, out_shapes, *operands):
    outs = [jax.ShapeDtypeStruct(shape, LOW) for shape in out_shapes]
    return kernel_call(
        body,
        (1,),
        [whole(v.shape) for v in operands],
        [whole(shape) for shape in out_shapes],
        outs,
        moved=sum(v.size * 2 for v in operands) + sum(2 * math.prod(x) for x in out_shapes),
    )(*operands)


def ctx_scatter(cuts, waits):
    up, across, x, y, own_a, own_b = cuts
    from_y, from_x = yield (ctx_swap(up, 2), ctx_swap(across, 1)), waits[0], (up, across)
    to_x, to_y = once(pass_body, (x.shape, y.shape), x, y, from_y, from_x)
    last_x, last_y = yield (ctx_swap(to_x, 1), ctx_swap(to_y, 2)), waits[1], (to_x, to_y)
    size, width = own_a.shape
    (out,) = once(keep_body, ((size, 2 * width),), own_a, own_b, from_y, from_x, last_x, last_y)
    return out


def fsdp_scatter(table, direct):
    count = lax.axis_size("fsdp")
    if count > 4 or not direct:
        total = lax.psum_scatter(table, "fsdp", scatter_dimension=0, tiled=False)
        if direct is None:
            (total,) = yield (total,), 0, (table,)
        else:
            yield (), 0, (table,)
        return total.astype(WIDE)
    place = lax.axis_index("fsdp")
    came = tuple(
        lax.ppermute(pick(table, place ^ step, 0), "fsdp", xor_pairs(count, step))
        for step in range(1, count)
    )
    came = yield came, 0, (table,)
    return added(pick(table, place, 0), *came)


class Scatters:
    def __init__(self):
        self.active = []

    def add(self, pairs, tile, direct, waits, done):
        cuts = tables(pairs, tile)

        def run():
            part = yield from ctx_scatter(cuts, waits)
            fsdp = lax.axis_size("fsdp")
            part = part.reshape(fsdp, -1, part.shape[1])
            done((yield from fsdp_scatter(part, direct)))

        self.begin(run())
        return cuts[0]

    def add_fsdp_first(self, left, right, waits, done):
        table = fsdp_table(left, right, 512)
        fsdp, flips, rows, width = table.shape

        def run():
            moved = table.reshape(fsdp, flips * rows, width)
            total = lax.psum_scatter(moved, "fsdp", scatter_dimension=0, tiled=False)
            (total,) = yield (total,), waits, (moved,)
            cut = half_lanes(width)
            own, x, far, y = (total[i * rows : (i + 1) * rows] for i in range(flips))
            cuts = (
                total[2 * rows :, :cut],
                total[rows : 3 * rows, cut:],
                x[:, :cut],
                y[:, cut:],
                own[:, :cut],
                own[:, cut:],
            )
            done((yield from ctx_scatter(cuts, (0, 0))).astype(WIDE))

        self.begin(run())
        return table

    def begin(self, work):
        self.active.append([work, *next(work)])

    def step(self, anchor):
        ready = [item for item in self.active if anchor is None or item[2] == 0]
        for item in self.active:
            item[2] = max(item[2] - 1, 0)
        values = [v for item in ready for v in item[1]]
        if anchor is not None:
            values, anchor = together(values, anchor)
        elif values:
            values = lax.optimization_barrier(tuple(values))
        first, sent = 0, ()
        for item in ready:
            came = tuple(values[first : first + len(item[1])])
            first += len(item[1])
            try:
                item[1:] = item[0].send(came)
                sent += item[3]
            except StopIteration:
                self.active.remove(item)
        if sent and anchor is not None:
            _, anchor = together(sent, anchor)
        return anchor

    def finish(self):
        while self.active:
            self.step(None)


def join_rows(piece):
    v = piece[None, None]
    for dim, axis in enumerate(("fsdp", "ctx")):
        place = lax.axis_index(axis)
        for step in bits_of(axis):
            (came,) = yield (lax.ppermute(v, axis, xor_pairs(lax.axis_size(axis), step)),), 0, ()
            v = jnp.where(
                (place & step) == 0,
                jnp.concatenate([v, came], axis=dim),
                jnp.concatenate([came, v], axis=dim),
            )
    return v


def sum_everywhere(v):
    for axis in ("fsdp", "ctx"):
        for step in bits_of(axis):
            (came,) = yield (lax.ppermute(v, axis, xor_pairs(lax.axis_size(axis), step)),), 0, ()
            v = v + came
    return v


def turn_tables(start_row, rows):
    half = ADIM // 2
    places = (start_row + jnp.arange(rows)).astype(WIDE)
    rates = jnp.exp(-math.log(THETA) * jnp.arange(half).astype(WIDE) / half)
    angles = places[:, None] * rates[None, :]
    cosine, sine = jnp.cos(angles), jnp.sin(angles)
    one_cos = jnp.concatenate([cosine, cosine], axis=1)
    one_sin = jnp.concatenate([-sine, sine], axis=1)
    still = jnp.ones_like(one_cos)
    return (
        jnp.concatenate([one_cos, one_cos, one_cos, still], axis=1),
        jnp.concatenate([one_sin, one_sin, one_sin, jnp.zeros_like(one_sin)], axis=1),
    )


def turned(values, cosine, sine):
    lanes = lane_iota(values.shape) % ADIM
    swapped = jnp.where(
        lanes < ADIM // 2,
        pltpu.roll(values, LANES - ADIM // 2, 1),
        pltpu.roll(values, ADIM // 2, 1),
    )
    return values * cosine + swapped * sine


def qkv_body(rows_ref, cos_ref, sin_ref, q_ref, kv_ref):
    for pair in range(GROUP // 2):
        lanes = slice(pair * LANES, (pair + 1) * LANES)
        q_ref[:, lanes] = turned(
            rows_ref[:, lanes], cos_ref[:, :LANES], sin_ref[:, :LANES]
        ).astype(LOW)
    width = GROUP * ADIM
    kv_ref[...] = turned(
        rows_ref[:, width : width + LANES], cos_ref[:, LANES:], sin_ref[:, LANES:]
    ).astype(LOW)


def split_qkv(projected, tables, rows, column):
    total = projected.shape[0]
    width = GROUP * ADIM
    return kernel_call(
        qkv_body,
        (total // rows,),
        [rows_block(rows, width + LANES, column)] + [rows_block(rows, 2 * LANES)] * 2,
        [rows_block(rows, width), rows_block(rows, LANES)],
        [
            jax.ShapeDtypeStruct((total, width), LOW),
            jax.ShapeDtypeStruct((total, LANES), LOW),
        ],
        flops=total * 400 * 4,
        moved=total * 384 * 6,
    )(projected, *tables)


def head_lanes(values, head):
    pair = values[:, head // 2 * LANES : (head // 2 + 1) * LANES]
    if head % 2:
        pair = pltpu.roll(pair, ADIM, 1)
    return jnp.where(lane_iota(pair.shape) < ADIM, pair, jnp.zeros_like(pair))


def seen_keys(place, rows, total):
    shape = (rows, 2 * total)
    column = lane_iota(shape)
    own = (column < total) & (column <= row_iota(shape) + pl.program_id(0) * rows)
    return own | ((column >= total) & (column < total * (1 + place)))


def attend_body(place_ref, q_ref, own_ref, came_ref, out_ref, total_ref, keys):
    rows, total = q_ref.shape[0], own_ref.shape[0]
    keys[:total, :] = own_ref[...]
    keys[total:, :] = came_ref[...]
    seen = seen_keys(place_ref[0], rows, total)
    q_all = q_ref[...].astype(WIDE)
    all_keys = keys[...]
    totals = jnp.zeros((rows, LANES), WIDE)
    lanes = lane_iota((rows, LANES))
    outs = []
    for head in range(GROUP):
        query = (head_lanes(q_all, head) * ADIM**-0.5).astype(LOW)
        scores = jnp.where(seen, dot(query, all_keys, 1, 1), MASKED)
        top = jnp.max(scores, axis=1, keepdims=True)
        raised = jnp.exp(scores - top)
        row_total = jnp.sum(raised, axis=1, keepdims=True)
        outs.append(dot(raised.astype(LOW), all_keys) * (1.0 / row_total))
        totals = jnp.where(lanes == head, top + jnp.log(row_total), totals)
    total_ref[...] = totals
    for pair in range(GROUP // 2):
        first = pltpu.roll(outs[2 * pair], ADIM, 1)
        out_ref[:, pair * LANES : (pair + 1) * LANES] = jnp.where(
            lanes < ADIM, first, outs[2 * pair + 1]
        ).astype(LOW)


def attend(place, queries, own, came, rows):
    total, width = queries.shape
    return kernel_call(
        attend_body,
        (total // rows,),
        [
            pl.BlockSpec(memory_space=pltpu.SMEM),
            rows_block(rows, width),
            whole((total, LANES)),
            whole((total, LANES)),
        ],
        [rows_block(rows, width), rows_block(rows, LANES)],
        [
            jax.ShapeDtypeStruct((total, width), LOW),
            jax.ShapeDtypeStruct((total, LANES), WIDE),
        ],
        [pltpu.VMEM((2 * total, LANES), LOW)],
        flops=total * total * 2 * GROUP * LANES * 4,
        moved=total * (width * 4 + LANES * 12),
    )(place, queries, own, came)


def attend_back_body(
    place_ref, q_ref, grad_ref, total_ref, cos_ref, sin_ref, own_ref, came_ref,
    dq_ref, own_grad_ref, came_grad_ref, keys, grads,
):
    rows, total = q_ref.shape[0], own_ref.shape[0]
    keys[:total, :] = own_ref[...]
    keys[total:, :] = came_ref[...]
    seen = seen_keys(place_ref[0], rows, total)
    q_all = q_ref[...].astype(WIDE)
    grad_all = grad_ref[...].astype(WIDE)
    all_keys = keys[...]
    lanes = lane_iota((rows, LANES))
    grad_kv = None
    dqs = []
    for head in range(GROUP):
        query = (head_lanes(q_all, head) * ADIM**-0.5).astype(LOW)
        upper = pltpu.roll(head_lanes(grad_all, head), ADIM, 1).astype(LOW)
        scores = jnp.where(seen, dot(query, all_keys, 1, 1), MASKED)
        probs = jnp.exp(scores - total_ref[:, head : head + 1])
        grad_probs = dot(upper, all_keys, 1, 1)
        inner = jnp.sum(probs * grad_probs, axis=1, keepdims=True)
        grad_scores = (probs * (grad_probs - inner)).astype(LOW)
        dqs.append(dot(grad_scores, all_keys) * ADIM**-0.5)
        fresh = dot(grad_scores, query, 0, 0) + dot(probs.astype(LOW), upper, 0, 0)
        grad_kv = fresh if grad_kv is None else grad_kv + fresh
    for pair in range(GROUP // 2):
        both = jnp.where(lanes < ADIM, dqs[2 * pair], pltpu.roll(dqs[2 * pair + 1], ADIM, 1))
        dq_ref[:, pair * LANES : (pair + 1) * LANES] = turned(
            both, cos_ref[:, :LANES], -sin_ref[:, :LANES]
        ).astype(LOW)
    place = pl.program_id(0)

    @pl.when(place == 0)
    def _():
        grads[...] = grad_kv

    @pl.when(place > 0)
    def _():
        grads[...] += grad_kv

    own_grad_ref[...] = grads[:total, :]
    came_grad_ref[...] = grads[total:, :].astype(LOW)


def attend_back(place, queries, grad_out, log_total, tables, own, came, rows):
    total, width = queries.shape
    return kernel_call(
        attend_back_body,
        (total // rows,),
        [
            pl.BlockSpec(memory_space=pltpu.SMEM),
            rows_block(rows, width),
            rows_block(rows, width),
            rows_block(rows, LANES),
            rows_block(rows, 2 * LANES),
            rows_block(rows, 2 * LANES),
            whole((total, LANES)),
            whole((total, LANES)),
        ],
        [rows_block(rows, width), whole((total, LANES)), whole((total, LANES))],
        [
            jax.ShapeDtypeStruct((total, width), LOW),
            jax.ShapeDtypeStruct((total, LANES), WIDE),
            jax.ShapeDtypeStruct((total, LANES), LOW),
        ],
        [pltpu.VMEM((2 * total, LANES), LOW), pltpu.VMEM((2 * total, LANES), WIDE)],
        flops=total * total * 2 * GROUP * LANES * 10,
        moved=total * (width * 6 + LANES * 20),
    )(place, queries, grad_out, log_total, *tables, own, came)


def key_body(own_ref, *refs):
    came, (cos_ref, sin_ref, out_ref) = refs[:-3], refs[-3:]
    values = own_ref[...]
    for ref in came:
        values = values + ref[...].astype(WIDE)
    out_ref[...] = turned(values, cos_ref[:, LANES:], -sin_ref[:, LANES:]).astype(LOW)


def finish_keys(own, came, tables, rows):
    total = own.shape[0]
    return kernel_call(
        key_body,
        (total // rows,),
        [rows_block(rows, LANES)] * (1 + len(came)) + [rows_block(rows, 2 * LANES)] * 2,
        rows_block(rows, LANES),
        jax.ShapeDtypeStruct((total, LANES), LOW),
        flops=total * LANES * 10,
        moved=total * LANES * 12,
    )(own, *came, *tables)


def sigmoid(v):
    return 1.0 / (1.0 + jnp.exp(-v))


def softplus(v):
    return jnp.maximum(v, 0.0) + jnp.log1p(jnp.exp(-jnp.abs(v)))


def over_pair(values, pair, shape):
    first = values[:, 2 * pair : 2 * pair + 1]
    second = values[:, 2 * pair + 1 : 2 * pair + 2]
    return jnp.where(lane_iota(shape) < HDIM, first, second)


def down_pair(values, pair):
    shape = (LANES, LANES)
    first = jnp.broadcast_to(values[:, 2 * pair : 2 * pair + 1], shape)
    second = jnp.broadcast_to(values[:, 2 * pair + 1 : 2 * pair + 2], shape)
    return jnp.where(row_iota(shape) < HDIM, first, second)


def head_matrix(channels):
    shape = (LANES, channels)
    return jnp.where(lane_iota(shape) // HDIM == row_iota(shape), 1.0, 0.0).astype(LOW)


def two_parts(values):
    high = values.astype(LOW)
    return high, (values - high.astype(WIDE)).astype(LOW)


def over_heads(values, matrix):
    high, low = two_parts(values)
    return dot(high, matrix) + dot(low, matrix)


def by_heads(values, matrix):
    high, low = two_parts(values)
    return dot(high, matrix, 1, 1) + dot(low, matrix, 1, 1)


def lower_ones(rows, flip):
    shape = (rows, rows)
    t, s = row_iota(shape), lane_iota(shape)
    return jnp.where((t <= s) if flip else (t >= s), 1.0, 0.0).astype(WIDE)


def convolved(padded, taps_ref, rows):
    total = taps_ref[CONV : CONV + 1, :]
    for j in range(CONV):
        first = 8 - CONV + 1 + j
        total = total + taps_ref[j : j + 1, :] * padded[first : first + rows, :]
    return total


def scan_body(
    zx_ref, side_ref, rim_ref, taps_ref, heads_ref,
    stk_ref, x_ref, bc_ref, y_ref, first_ref, parcel_ref, cum_ref, all_ref, step_ref,
    padded, state, before_it,
):
    rows, channels = zx_ref.shape
    heads = channels // HDIM
    place = pl.program_id(0)

    @pl.when(place == 0)
    def _():
        padded[0:8, :] = rim_ref[...]
        state[...] = jnp.zeros(state.shape, WIDE)
        before_it[...] = jnp.zeros(before_it.shape, WIDE)

    @pl.when(place > 0)
    def _():
        padded[0:8, :] = padded[rows : rows + 8, :]

    stk_ref[:, :channels] = zx_ref[...].astype(LOW)
    stk_ref[:, channels:] = side_ref[:, : 2 * STATE].astype(LOW)
    padded[8 : 8 + rows, :] = stk_ref[...].astype(WIDE)
    before = convolved(padded, taps_ref, rows)
    active = (before * sigmoid(before)).astype(LOW)
    x_ref[...] = active[:, :channels]
    bc_ref[...] = active[:, channels:]
    step = softplus(side_ref[:, 2 * STATE :] + heads_ref[1:2, :])
    cum = dot(lower_ones(rows, False), -step * jnp.exp(heads_ref[0:1, :]), precision=HIGHEST)
    step_ref[...] = step
    cum_ref[...] = cum
    all_ref[...] = cum + before_it[0:1, :]
    cum_rows, step_rows = cum.T, step.T
    last = cum[rows - 1 : rows, :]
    before_it[...] = jnp.broadcast_to(before_it[0:1, :] + last, before_it.shape)
    matrix = head_matrix(channels)
    tail = over_heads(jnp.exp(last - cum) * step, matrix)
    grown, faded = over_heads(jnp.exp(cum), matrix), jnp.exp(last)
    entry, readout = bc_ref[:, :STATE], bc_ref[:, STATE:]
    cross = dot(readout, entry, 1, 1)
    shape = (rows, rows)
    causal = row_iota(shape) >= lane_iota(shape)
    lanes = lane_iota((rows, LANES))
    for pair in range(heads // 2):
        block = slice(pair * LANES, (pair + 1) * LANES)
        inputs = x_ref[:, block]
        outs = []
        for head in (2 * pair, 2 * pair + 1):
            gap = cum[:, head : head + 1] - cum_rows[head : head + 1, :]
            decay = jnp.exp(jnp.where(causal, gap, MASKED))
            mixed = (decay * cross * step_rows[head : head + 1, :]).astype(LOW)
            outs.append(dot(mixed, inputs))
        carried = dot(readout, state[block, :].astype(LOW), 1, 1)
        y_ref[:, block] = jnp.where(lanes < HDIM, outs[0], outs[1]) + carried * grown[:, block]
        scaled = (tail[:, block] * inputs.astype(WIDE)).astype(LOW)
        fresh = down_pair(faded, pair) * state[block, :] + dot(scaled, entry, 0, 0)
        state[block, :] = fresh
        parcel_ref[block, :] = fresh.astype(LOW)
    write_decays(parcel_ref, channels, before_it[0:1, :])

    @pl.when(place == 0)
    def _():
        first_ref[...] = state[...]


def scan_local(projected, side, rim, taps, heads, rows, channels):
    total = projected.shape[0]
    count = total // rows
    width = channels + 2 * STATE
    return kernel_call(
        scan_body,
        (count,),
        [
            rows_block(rows, channels, 1),
            rows_block(rows, side.shape[1]),
            whole((8, width)),
            whole((8, width)),
            whole((8, LANES)),
        ],
        [
            rows_block(rows, width),
            rows_block(rows, channels),
            rows_block(rows, 2 * STATE),
            rows_block(rows, channels),
            whole((channels, STATE)),
            whole((channels + PARCEL_ROWS, STATE)),
            rows_block(rows, LANES),
            rows_block(rows, LANES),
            rows_block(rows, LANES),
        ],
        [
            jax.ShapeDtypeStruct((total, width), LOW),
            jax.ShapeDtypeStruct((total, channels), LOW),
            jax.ShapeDtypeStruct((total, 2 * STATE), LOW),
            jax.ShapeDtypeStruct((total, channels), WIDE),
            jax.ShapeDtypeStruct((channels, STATE), WIDE),
            jax.ShapeDtypeStruct((channels + PARCEL_ROWS, STATE), LOW),
            jax.ShapeDtypeStruct((total, LANES), WIDE),
            jax.ShapeDtypeStruct((total, LANES), WIDE),
            jax.ShapeDtypeStruct((total, LANES), WIDE),
        ],
        [
            pltpu.VMEM((rows + 8, width), WIDE),
            pltpu.VMEM((channels, STATE), WIDE),
            pltpu.VMEM((8, LANES), WIDE),
        ],
        flops=total * rows * channels * 8,
        moved=total * width * 16,
    )(projected, side, rim, taps, heads)


def tail_body(
    y_ref, cum_ref, bc_ref, x_ref, gate_ref, heads_ref, gain_ref, parcel_ref, out_ref, norm_ref
):
    rows, channels = y_ref.shape
    readout = bc_ref[:, STATE:]
    grown = over_heads(jnp.exp(cum_ref[...]), head_matrix(channels))
    square = jnp.zeros((rows, 1), WIDE)
    for pair in range(channels // LANES):
        block = slice(pair * LANES, (pair + 1) * LANES)
        carried = dot(readout, parcel_ref[block, :], 1, 1)
        y = y_ref[:, block] + grown[:, block] * carried
        out_ref[:, block] = y
        skip = over_pair(heads_ref[2:3, :], pair, (1, LANES))
        gate = gate_ref[:, block]
        mixed = (y + skip * x_ref[:, block].astype(WIDE)) * (gate * sigmoid(gate))
        square = square + jnp.sum(mixed * mixed, axis=1, keepdims=True)
    scale = lax.rsqrt(square * (1.0 / channels) + EPSILON)
    for pair in range(channels // LANES):
        block = slice(pair * LANES, (pair + 1) * LANES)
        skip = over_pair(heads_ref[2:3, :], pair, (1, LANES))
        gate = gate_ref[:, block]
        mixed = (out_ref[:, block] + skip * x_ref[:, block].astype(WIDE)) * (gate * sigmoid(gate))
        norm_ref[:, block] = (mixed * scale * gain_ref[:, block]).astype(LOW)


def gate_tail(y, cum, bc, x, projected, heads, gain, parcel, rows):
    total, channels = y.shape
    return kernel_call(
        tail_body,
        (total // rows,),
        [
            rows_block(rows, channels),
            rows_block(rows, LANES),
            rows_block(rows, 2 * STATE),
            rows_block(rows, channels),
            rows_block(rows, channels, 0),
            whole((8, LANES)),
            whole((1, channels)),
            whole((channels + PARCEL_ROWS, STATE)),
        ],
        [rows_block(rows, channels), rows_block(rows, channels)],
        [
            jax.ShapeDtypeStruct((total, channels), WIDE),
            jax.ShapeDtypeStruct((total, channels), LOW),
        ],
        flops=total * channels * (2 * STATE + 40),
        moved=total * channels * 18,
    )(y, cum, bc, x, projected, heads, gain, parcel)


def tail_back_body(
    dn_ref, y_ref, cum_ref, bc_ref, x_ref, gate_ref, heads_ref, gain_ref,
    du_ref, dgate_ref, parcel_ref, sums_ref, state,
):
    @pl.when(pl.program_id(0) == 0)
    def _():
        state[...] = jnp.zeros(state.shape, WIDE)

    rows, channels = y_ref.shape
    readout = bc_ref[:, STATE:]
    grown = over_heads(jnp.exp(cum_ref[...]), head_matrix(channels))
    square = jnp.zeros((rows, 1), WIDE)
    inner = jnp.zeros((rows, 1), WIDE)
    for pair in range(channels // LANES):
        block = slice(pair * LANES, (pair + 1) * LANES)
        skip = over_pair(heads_ref[2:3, :], pair, (1, LANES))
        gate = gate_ref[:, block]
        mixed = (y_ref[:, block] + skip * x_ref[:, block].astype(WIDE)) * (gate * sigmoid(gate))
        square = square + jnp.sum(mixed * mixed, axis=1, keepdims=True)
        inner = inner + jnp.sum(
            dn_ref[:, block] * gain_ref[:, block] * mixed, axis=1, keepdims=True
        )
    scale = lax.rsqrt(square * (1.0 / channels) + EPSILON)
    inner = inner * scale * (1.0 / channels)
    sums_ref[...] = jnp.zeros(sums_ref.shape, WIDE)
    for pair in range(channels // LANES):
        block = slice(pair * LANES, (pair + 1) * LANES)
        skip = over_pair(heads_ref[2:3, :], pair, (1, LANES))
        gate = gate_ref[:, block]
        inputs = x_ref[:, block].astype(WIDE)
        sigma = sigmoid(gate)
        value = y_ref[:, block] + skip * inputs
        unit = value * (gate * sigma) * scale
        upstream = dn_ref[:, block]
        dmixed = scale * (upstream * gain_ref[:, block] - unit * inner)
        du = dmixed * gate * sigma
        du_ref[:, block] = du
        dgate_ref[:, block] = (
            dmixed * value * (sigma * (1.0 + gate * (1.0 - sigma)))
        ).astype(LOW)
        sums_ref[0:1, block] = jnp.sum(upstream * unit, axis=0, keepdims=True)
        sums_ref[1:2, block] = jnp.sum(du * inputs, axis=0, keepdims=True)
        fresh = state[block, :] + dot(
            (grown[:, block] * du).astype(LOW), readout, 0, 0
        )
        state[block, :] = fresh
        parcel_ref[block, :] = fresh.astype(LOW)
    write_decays(parcel_ref, channels, cum_ref[rows - 1 : rows, :])


def gate_tail_back(dn, y, cum, bc, x, projected, heads, gain, rows):
    total, channels = y.shape
    count = total // rows
    return kernel_call(
        tail_back_body,
        (count,),
        [
            rows_block(rows, channels),
            rows_block(rows, channels),
            rows_block(rows, LANES),
            rows_block(rows, 2 * STATE),
            rows_block(rows, channels),
            rows_block(rows, channels, 0),
            whole((8, LANES)),
            whole((1, channels)),
        ],
        [
            rows_block(rows, channels),
            rows_block(rows, channels),
            whole((channels + PARCEL_ROWS, STATE)),
            sequence_block(8, channels),
        ],
        [
            jax.ShapeDtypeStruct((total, channels), WIDE),
            jax.ShapeDtypeStruct((total, channels), LOW),
            jax.ShapeDtypeStruct((channels + PARCEL_ROWS, STATE), LOW),
            jax.ShapeDtypeStruct((count, 8, channels), WIDE),
        ],
        [pltpu.VMEM((channels, STATE), WIDE)],
        flops=total * channels * (2 * STATE + 60),
        moved=total * channels * 22,
    )(dn, y, cum, bc, x, projected, heads, gain)


def write_decays(parcel_ref, channels, last):
    high = jnp.broadcast_to(jnp.exp(last), (PARCEL_ROWS, LANES))
    top = high.astype(LOW).astype(WIDE)
    row = row_iota(high.shape)
    parcel_ref[channels:, :] = jnp.where(
        row == 0, top, jnp.where(row == 1, high - top, 0.0)
    ).astype(LOW)


def scan_back_body(
    du_ref, x_ref, bc_ref, stk_ref, prior_ref, rim_ref, cum_ref, all_ref, step_ref, side_ref,
    first_ref, parcel_ref, later_ref, taps_ref, heads_ref,
    dstk_ref, drim_ref, dstep_ref, dtaps_ref, dheads_ref, padded, dact, after, behind,
    carried_all, final_all,
):
    place = pl.program_id(0)
    second = jnp.where(place == 0, 1.0, 0.0).astype(WIDE)
    rows, channels = du_ref.shape
    heads = channels // HDIM
    width = channels + 2 * STATE
    entry, readout = bc_ref[:, :STATE], bc_ref[:, STATE:]
    cum, step = cum_ref[...], step_ref[...]
    cum_rows = cum.T
    last = cum[rows - 1 : rows, :]
    faded, arriving = jnp.exp(last), jnp.exp(all_ref[0:1, :] - cum[0:1, :])

    @pl.when(place == 0)
    def _():
        behind[...] = later_ref[:channels, :].astype(WIDE)
        after[8 + rows : 16 + rows, :] = jnp.zeros((8, width), WIDE)
        padded[0:8, :] = prior_ref[8:16, :].astype(WIDE)

    @pl.when(place > 0)
    def _():
        after[8 + rows : 16 + rows, :] = after[8:16, :]
        padded[0:8, :] = rim_ref[...]

    grown = jnp.exp(cum)
    decayed = jnp.exp(last - cum)
    tail = decayed * step
    matrix = head_matrix(channels)
    grown_all, tail_all, step_all = (over_heads(v, matrix) for v in (grown, tail, step))
    cross = dot(entry, readout, 1, 1)
    shape = (rows, rows)
    causal = row_iota(shape) <= lane_iota(shape)
    lanes = lane_iota((rows, LANES))
    small = lane_iota((1, LANES))
    dcross = jnp.zeros(shape, WIDE)
    entry_grad = jnp.zeros((rows, STATE), WIDE)
    readout_grad = jnp.zeros((rows, STATE), WIDE)
    pulled = jnp.zeros((rows, LANES), WIDE)
    arrived = []
    state_sum = jnp.zeros((1, LANES), WIDE)
    for pair in range(heads // 2):
        block = slice(pair * LANES, (pair + 1) * LANES)
        inputs = x_ref[:, block]
        inputs_wide = inputs.astype(WIDE)
        du = du_ref[:, block]
        du_low = du.astype(LOW)
        start = down_pair(arriving, pair) * parcel_ref[block, :].astype(WIDE)
        start = start + second * first_ref[block, :]
        later = behind[block, :]
        start_low, later_low = start.astype(LOW), later.astype(LOW)
        pulls = []
        for k in range(2):
            head = 2 * pair + k
            own = (lanes < HDIM) if k == 0 else (lanes >= HDIM)
            gap = cum_rows[head : head + 1, :] - cum[:, head : head + 1]
            decay = jnp.exp(jnp.where(causal, gap, MASKED))
            pulls.append(dot((decay * cross).astype(LOW), du_low))
            dmix = dot(jnp.where(own, inputs, jnp.zeros_like(inputs)), du_low, 1, 1) * decay
            stepped = step[:, head : head + 1]
            dcross = dcross + dmix * stepped
            dgap = dmix * cross
            pulled = jnp.where(lanes == head, jnp.sum(dgap, axis=1, keepdims=True), pulled)
            arrived.append(jnp.sum(dgap * stepped, axis=0, keepdims=True))
        pull = jnp.where(lanes < HDIM, pulls[0], pulls[1])
        grown_pair = grown_all[:, block]
        grown_du = grown_pair * du
        grown_low = grown_du.astype(LOW)
        behind[block, :] = down_pair(faded, pair) * later + dot(grown_low, readout, 0, 0)
        readout_grad = readout_grad + dot(grown_low, start_low)
        carried_all[:, block] = grown_du * dot(readout, start_low, 1, 1)
        tail_pair = tail_all[:, block]
        from_later = dot(entry, later_low, 1, 1)
        entry_grad = entry_grad + dot((tail_pair * inputs_wide).astype(LOW), later_low)
        final_all[:, block] = inputs_wide * from_later
        product = start * later
        for k in range(2):
            total = jnp.sum(
                jnp.sum(product[k * HDIM : (k + 1) * HDIM], axis=0, keepdims=True),
                axis=1,
                keepdims=True,
            )
            state_sum = jnp.where(small == 2 * pair + k, total, state_sum)
        skip = over_pair(heads_ref[2:3, :], pair, (1, LANES))
        dact[:, block] = (
            skip * du + step_all[:, block] * pull + tail_pair * from_later
        )
    dcross_low = dcross.astype(LOW)
    dact[:, channels : channels + STATE] = entry_grad + dot(dcross_low, readout)
    dact[:, channels + STATE :] = readout_grad + dot(dcross_low, entry, 0, 0)
    arrived.append(jnp.zeros((LANES - heads, rows), WIDE))
    carried_sum, final_sum = by_heads(carried_all[...], matrix), by_heads(final_all[...], matrix)
    arrived_columns = jnp.concatenate(arrived, axis=0).T
    weighted = tail * final_sum
    dcum = arrived_columns - step * pulled + carried_sum - weighted
    at_last = jnp.sum(weighted, axis=0, keepdims=True) + faded * state_sum
    dcum = dcum + jnp.where(row_iota(dcum.shape) == rows - 1, at_last, 0.0)
    dlog = dot(lower_ones(rows, True), dcum, precision=HIGHEST)
    rate = jnp.exp(heads_ref[0:1, :])
    dstep = pulled + decayed * final_sum - rate * dlog
    dstep_pre = dstep * sigmoid(side_ref[...] + heads_ref[1:2, :])
    dstep_pre = jnp.where(lanes < heads, dstep_pre, 0.0)
    dstep_ref[...] = dstep_pre.astype(LOW)
    dheads_ref[...] = jnp.zeros(dheads_ref.shape, WIDE)
    dheads_ref[0:1, :] = -rate * jnp.sum(step * dlog, axis=0, keepdims=True)
    dheads_ref[1:2, :] = jnp.sum(dstep_pre, axis=0, keepdims=True)

    padded[8 : 8 + rows, :] = stk_ref[...].astype(WIDE)
    before = convolved(padded, taps_ref, rows)
    sigma = sigmoid(before)
    dbefore = dact[...] * sigma * (1.0 + before * (1.0 - sigma))
    after[0:8, :] = jnp.zeros((8, width), WIDE)
    after[8 : 8 + rows, :] = dbefore
    dtaps_ref[...] = jnp.zeros(dtaps_ref.shape, WIDE)
    back = None
    for j in range(CONV):
        first = 8 - CONV + 1 + j
        dtaps_ref[j : j + 1, :] = jnp.sum(
            after[8 : 8 + rows, :] * padded[first : first + rows, :], axis=0, keepdims=True
        )
        first = CONV - 1 - j
        term = taps_ref[j : j + 1, :] * after[first : first + rows + 8, :]
        back = term if back is None else back + term
    dtaps_ref[CONV : CONV + 1, :] = jnp.sum(after[8 : 8 + rows, :], axis=0, keepdims=True)
    drim_ref[...] = back[0:8]
    dstk_ref[...] = back[8:].astype(LOW)


def scan_back(
    du, x, bc, stk, rim, cum, all_cum, step, side, first, parcel, later, taps, heads, rows
):
    total, channels = du.shape
    count = total // rows
    width = channels + 2 * STATE

    def back_block(cols, col=0):
        return pl.BlockSpec((rows, cols), lambda s: (count - 1 - s, col))

    return kernel_call(
        scan_back_body,
        (count,),
        [
            back_block(channels),
            back_block(channels),
            back_block(2 * STATE),
            back_block(width),
            pl.BlockSpec((16, width), lambda s: (rows // 16 - 1, 0)),
            whole((8, width)),
            back_block(LANES),
            back_block(LANES),
            back_block(LANES),
            back_block(LANES, 2 * STATE // LANES),
            whole((channels, STATE)),
            whole((channels + PARCEL_ROWS, STATE)),
            whole((channels + PARCEL_ROWS, STATE)),
            whole((8, width)),
            whole((8, LANES)),
        ],
        [
            back_block(width),
            whole((8, width)),
            back_block(LANES),
            sequence_block(8, width),
            sequence_block(8, LANES),
        ],
        [
            jax.ShapeDtypeStruct((total, width), LOW),
            jax.ShapeDtypeStruct((8, width), WIDE),
            jax.ShapeDtypeStruct((total, LANES), LOW),
            jax.ShapeDtypeStruct((count, 8, width), WIDE),
            jax.ShapeDtypeStruct((count, 8, LANES), WIDE),
        ],
        [
            pltpu.VMEM((rows + 8, width), WIDE),
            pltpu.VMEM((rows, width), WIDE),
            pltpu.VMEM((rows + 16, width), WIDE),
            pltpu.VMEM((channels, STATE), WIDE),
            pltpu.VMEM((rows, channels), WIDE),
            pltpu.VMEM((rows, channels), WIDE),
        ],
        flops=total * rows * channels * 20,
        moved=total * width * 24,
    )(du, x, bc, stk, stk, rim, cum, all_cum, step, side, first, parcel, later, taps, heads)


def unit_scale(values):
    return lax.rsqrt(jnp.mean(values * values, axis=-1, keepdims=True) + EPSILON)


def normalize(values, gain):
    return (values * unit_scale(values) * gain).astype(LOW)


def norm_grad_body(
    kept_ref, gain_ref, own_ref, peer_ref, base_ref, out_ref, low_ref, sums_ref
):
    kept = kept_ref[...]
    scale = unit_scale(kept)
    unit = kept * scale
    upstream = own_ref[...].astype(WIDE) + peer_ref[...].astype(WIDE)
    scaled = upstream * gain_ref[...]
    inner = jnp.mean(scaled * unit, axis=-1, keepdims=True)
    out = base_ref[...] + scale * (scaled - unit * inner)
    out_ref[...] = out
    low_ref[...] = out.astype(LOW)
    sums = jnp.sum(upstream * unit, axis=0, keepdims=True)

    @pl.when(pl.program_id(0) == 0)
    def _():
        sums_ref[...] = jnp.broadcast_to(sums, sums_ref.shape)

    @pl.when(pl.program_id(0) > 0)
    def _():
        sums_ref[...] += jnp.broadcast_to(sums, sums_ref.shape)


def norm_grad(kept, gain, partial_grad, base):
    own = partial_grad.astype(LOW)
    rows, features = kept.shape
    tile = min(rows, 256)
    out, low, sums = kernel_call(
        norm_grad_body,
        (rows // tile,),
        [rows_block(tile, features), whole((1, features))] + [rows_block(tile, features)] * 3,
        [rows_block(tile, features), rows_block(tile, features), whole((8, features))],
        [
            jax.ShapeDtypeStruct((rows, features), WIDE),
            jax.ShapeDtypeStruct((rows, features), LOW),
            jax.ShapeDtypeStruct((8, features), WIDE),
        ],
        flops=rows * features * 12,
        moved=rows * features * 18,
    )(kept, gain[None], own, tp_peer(own), base)
    return out, low, sums[0]


def product(a, b):
    return jnp.dot(a, b, preferred_element_type=WIDE)


def against_rows(a, b):
    return dot(a, b, 1, 1)


def halves(values):
    cut = half_lanes(values.shape[1])
    return values[:, :cut], values[:, cut:]


def over_rows(a, b):
    return dot(a, b, 0, 0).astype(LOW)


def weight_rows(layer, pieces):
    zx, mix, attn, attn_out, mlp, mlp_out = (p[layer] for p in pieces)
    rows = zx.shape[0]
    return (
        jnp.concatenate([zx.reshape(rows, -1), attn.reshape(rows, -1)], axis=1),
        jnp.concatenate([mix.T, attn_out.T], axis=1),
        mlp.reshape(rows, -1),
        mlp_out.T,
    )


def own_part(values, size, axis):
    return lax.dynamic_slice_in_dim(values, lax.axis_index("tp") * size, size, axis)


def padded_to(values, rows, lanes):
    return jnp.pad(values, ((0, rows - values.shape[0]), (0, lanes - values.shape[1])))


def local_small(order, layer, norm_gains, mamba_shared, conv_weight, conv_bias, head_params, mamba_gain):
    tp = lax.axis_size("tp")
    heads = head_params.shape[2] // tp
    full_ssm = mamba_gain.shape[1]
    channels = full_ssm // tp
    shared_all = mamba_shared[layer]
    shared = jnp.concatenate(
        [
            shared_all[:, : 2 * STATE],
            own_part(shared_all[:, 2 * STATE :], heads, 1),
            jnp.zeros((shared_all.shape[0], LANES - heads), LOW),
        ],
        axis=1,
    )
    taps_all = jnp.concatenate([conv_weight[layer], conv_bias[layer][None]], axis=0).astype(WIDE)
    taps = jnp.concatenate(
        [own_part(taps_all[:, :full_ssm], channels, 1), taps_all[:, full_ssm:]], axis=1
    )
    return (
        product(norm_gains[layer], order),
        dot(order, shared, 0, 0).astype(LOW),
        padded_to(taps, 8, taps.shape[1]),
        padded_to(own_part(head_params[layer], heads, 1), 8, LANES),
        own_part(mamba_gain[layer].astype(WIDE), channels, 0)[None],
    )


def layer_forward(hidden, layer, gathers, late, small, tables, place, sequences, moves):
    zx_w = gathers.take(2 * layer)
    gains, shared, taps, heads, gain = small
    rows = hidden.shape[0] // sequences
    channels = gain.shape[1]
    head_count = channels // HDIM
    normed = normalize(hidden, gains[0])
    projected = product(normed, zx_w)
    side = product(normed, shared)
    if layer == 0:
        late[:], projected = together(late, projected)
        late[:] = [lax.all_gather(v, "fsdp", axis=1).reshape(-1, v.shape[-1]) for v in late]
    mlp_out_w = late[layer]
    edge = jnp.concatenate(
        [projected[-CONV + 1 :, channels : 2 * channels], side[-CONV + 1 :, : 2 * STATE]], axis=1
    )
    came = next_half(edge.astype(LOW), True).astype(WIDE)
    rim = jnp.pad(came, ((8 - CONV + 1, 0), (0, 0)))
    queries, kv = split_qkv(projected, tables, rows, 2 * channels // (zx_w.shape[1] - 2 * channels))
    kv_came = next_half(kv, True)
    (kv_came,), rim = together((kv_came,), rim)
    rim = gathers.begin(rim)
    stk, x, bc, y_local, first, parcel_out, cum, all_cum, step = scan_local(
        projected, side, rim, taps, heads, rows, channels
    )
    parcel = next_half(parcel_out, True)
    attended, log_total = attend(place, queries, kv, kv_came, rows)
    if layer > 0:
        moves, parcel = together(moves, parcel)
        mlp_w = late[len(late) // 2 + layer]
        (mlp_w,), parcel = together((mlp_w,), parcel)
    (attended, parcel), y_local = together((attended, parcel), y_local)
    parcel = gathers.step(parcel)
    parcel = gathers.begin(parcel)
    y, mamba_norm = gate_tail(y_local, all_cum, bc, x, projected, heads, gain, parcel, rows)
    both = jnp.concatenate([mamba_norm, attended], axis=1)
    rest = gathers.take(2 * layer + 1)
    mix_w = rest[:, : both.shape[1]]
    if layer == 0:
        mlp_w = rest[:, both.shape[1] :]
    else:
        (mlp_out_w,), both = together((mlp_out_w,), both)
    after_mix = hidden + tp_sum(against_rows(both, mix_w))
    normed_two = normalize(after_mix, gains[1])
    gate_up = product(normed_two, mlp_w)
    ff = gate_up.shape[1] // 2
    activated = (jax.nn.silu(gate_up[:, :ff]) * gate_up[:, ff:]).astype(LOW)
    if gathers.near[-1] is None:
        activated = gathers.step(activated)
    result = after_mix + tp_sum(against_rows(activated, mlp_out_w))
    saved = (
        hidden, normed, projected, side, rim, queries, kv, kv_came, stk, x, bc, cum, all_cum, step,
        first, parcel, log_total, y, both, after_mix, normed_two, gate_up, activated,
    )
    return result, saved, (zx_w, mix_w, mlp_w, mlp_out_w), moves


def layer_backward(
    upstream, grad_mlp, saved, weights, small, tables, place, sequences, scatters, split, done, extra
):
    (
        hidden, normed, projected, side, rim, queries, kv, kv_came, stk, x, bc, cum, all_cum, step,
        first, parcel, log_total, y, both, after_mix, normed_two, gate_up, activated,
    ) = saved
    zx_w, mix_w, mlp_w, mlp_out_w = weights
    gains, shared, taps, heads, gain = small
    rows = hidden.shape[0] // sequences
    channels = gain.shape[1]
    head_count = channels // HDIM
    grad_act = product(grad_mlp, mlp_out_w)
    ff = grad_act.shape[1]
    gate_part, up_part = gate_up[:, :ff], gate_up[:, ff:]
    sigma = jax.nn.sigmoid(gate_part)
    grad_gu = jnp.concatenate(
        [
            grad_act * up_part * sigma * (1.0 + gate_part * (1.0 - sigma)),
            grad_act * gate_part * sigma,
        ],
        axis=1,
    ).astype(LOW)
    table = scatters.add_fsdp_first(normed_two, grad_gu, 2, functools.partial(done, 3))
    _, grad_gu = together((table,), grad_gu)
    grad_mid, grad_mix, grad_gain_two = norm_grad(
        after_mix, gains[1], against_rows(grad_gu, mlp_w), upstream
    )
    grad_mid = scatters.step(grad_mid)
    if extra:
        extra[:], grad_mix = together(extra, grad_mix)
    table = scatters.add(
        [(grad_mlp, activated), (grad_mix, both)],
        512,
        None if split else False,
        (0, 0),
        functools.partial(done, 0),
    )
    _, grad_mix = together((table,), grad_mix)
    grad_norm = product(grad_mix, mix_w[:, :channels])
    grad_attended = product(grad_mix, mix_w[:, channels:]).astype(LOW)
    du, grad_gate, state_grads, tail_sums = gate_tail_back(
        grad_norm, y, all_cum, bc, x, projected, heads, gain, rows
    )
    later = next_half(state_grads, False)
    grad_q, own_kv, sent_kv = attend_back(
        place, queries, grad_attended, log_total, tables, kv, kv_came, 2 * rows
    )
    came_kv = [next_half(sent_kv, False)]
    (later, *came_kv), grad_gate = together((later, *came_kv), grad_gate)
    later = scatters.step(later)
    if split:
        mid = jnp.concatenate([grad_gate, grad_q], axis=1)
        table = scatters.add([(normed, mid)], 512, True, (0, 0), functools.partial(done, 2))
        _, later = together((table,), later)
    dstk, drim, grad_step, dtaps, dheads = scan_back(
        du, x, bc, stk, rim, cum, all_cum, step, side, first, parcel, later, taps, heads, rows
    )
    drim = scatters.step(drim)
    returned = next_half(drim[8 - CONV + 1 :], False)
    last_rows = (dstk[-CONV + 1 :].astype(WIDE) + returned).astype(LOW)
    dstk = lax.dynamic_update_slice(dstk, last_rows, (dstk.shape[0] - CONV + 1, 0))
    grad_kv = finish_keys(own_kv, came_kv, tables, rows)
    grad_late = jnp.concatenate([dstk[:, :channels], grad_kv], axis=1)
    grad_first = jnp.concatenate(
        [grad_gate, grad_late[:, :channels], grad_q, grad_late[:, channels:]], axis=1
    )
    grad_side = jnp.concatenate([dstk[:, channels:], grad_step], axis=1)
    if split:
        late, tile = [grad_late, grad_side], 640
    else:
        late = [grad_gate, grad_q, grad_late[:, channels:], grad_late[:, :channels], grad_side]
        tile = 1152
    late = jnp.concatenate(late, axis=1)
    table = scatters.add([(normed, late)], tile, split, (0, 0), functools.partial(done, 1))
    _, grad_first = together((table,), grad_first)
    below, grad_mlp, grad_gain_one = norm_grad(
        hidden,
        gains[0],
        against_rows(grad_first, zx_w) + against_rows(grad_side, shared),
        grad_mid,
    )
    tail_sums = jnp.sum(tail_sums, axis=0)
    dheads = jnp.sum(dheads, axis=0)
    skip_grad = jnp.sum(tail_sums[1].reshape(head_count, HDIM), axis=1)
    skip_grad = jnp.pad(skip_grad, (0, LANES - head_count))[None]
    small_grads = (
        jnp.stack([grad_gain_one, grad_gain_two]),
        jnp.sum(dtaps, axis=0),
        jnp.where(row_iota(dheads.shape) == 2, skip_grad, dheads),
        tail_sums[0],
    )
    below, grad_mlp = scatters.step((below, grad_mlp))
    return below, grad_mlp, small_grads


def tp_ordered(a, b):
    low_half = lax.axis_index("tp") == 0
    return jnp.where(
        low_half, jnp.concatenate([a, b], axis=-1), jnp.concatenate([b, a], axis=-1)
    )


def settle_side(scatters, sums, half_heads, done):
    def run():
        fsdp = lax.axis_size("fsdp")
        layers = sums
        own = layers[0]
        rows = own.shape[0]
        wide = jnp.stack([v[:, : 2 * STATE].reshape(rows, 2, STATE) for v in layers])
        place = lax.axis_index("tp")
        (came,) = yield (tp_peer(pick(wide, 1 - place, 2)),), 0, ()
        mine = pick(wide, place, 2) + came
        steps = jnp.stack([v[:, 2 * STATE : 2 * STATE + half_heads] for v in layers]).reshape(-1)
        packed = jnp.concatenate([mine.reshape(-1), steps])
        packed = jnp.pad(packed, (0, -packed.size % (16 * LANES))).reshape(-1, LANES)
        joined = yield from join_rows(packed.astype(LOW))
        (theirs,) = yield (tp_peer(joined),), 0, ()
        count = len(layers)
        places = fsdp * lax.axis_size("ctx")

        def taken(values):
            flat = values.reshape(places, -1)
            wide_size = count * rows * STATE
            first = flat[:, :wide_size].reshape(places, count, rows, STATE)
            second = flat[:, wide_size : wide_size + count * rows * half_heads]
            return first, second.reshape(places, count, rows, half_heads)

        (wide_own, step_own), (wide_peer, step_peer) = taken(joined), taken(theirs)
        full = jnp.concatenate(
            [tp_ordered(wide_own, wide_peer), tp_ordered(step_own, step_peer)], axis=-1
        )
        done(full.transpose(1, 0, 2, 3).reshape(count, places * rows, -1).astype(WIDE))

    scatters.begin(run())


def settle_small(scatters, small_grads, half_heads, done):
    def run():
        layers = len(small_grads)
        shapes = [v.shape for v in small_grads[0]]
        flat = [v.reshape(-1, LANES) for grads in small_grads for v in grads]
        flat = [jnp.pad(v, ((0, -v.shape[0] % 8), (0, 0))) for v in flat]
        packed = yield from sum_everywhere(jnp.concatenate(flat, axis=0))
        (packed_peer,) = yield (tp_peer(packed),), 0, ()
        own, peer = [], []
        first = 0
        for values, shape in zip(flat, shapes * layers):
            for source, parts in ((packed, own), (packed_peer, peer)):
                piece = source[first : first + math.prod(shape) // LANES]
                parts.append(piece.reshape(shape))
            first += values.shape[0]
        count = len(shapes)
        for l in range(layers):
            (gains, taps, heads, gain), (gains_p, taps_p, heads_p, gain_p) = (
                v[l * count : (l + 1) * count] for v in (own, peer)
            )
            channels = gain.shape[0]
            taps_full = jnp.concatenate(
                [
                    tp_ordered(taps[:, :channels], taps_p[:, :channels]),
                    taps[:, channels:] + taps_p[:, channels:],
                ],
                axis=1,
            )
            done(
                l,
                (
                    jnp.where(lax.axis_index("tp") == 0, gains, gains_p),
                    taps_full[:CONV],
                    taps_full[CONV],
                    tp_ordered(heads[:3, :half_heads], heads_p[:3, :half_heads]),
                    tp_ordered(gain, gain_p),
                ),
            )

    scatters.begin(run())


def local(
    hidden_in, lengths, norm_gains, mamba_zx, mamba_shared, conv_weight, conv_bias, head_params,
    mamba_gain, mamba_out, attn_in, attn_out, mlp_in, mlp_out, out_grad,
):
    layers = norm_gains.shape[0]
    micro, own_seqs, rows, features = hidden_in.shape
    sequences = micro * own_seqs
    full_ssm = mamba_gain.shape[1]
    heads_total = head_params.shape[2]
    ctx_place = lax.axis_index("ctx")
    place = (ctx_place % 2).astype(jnp.int32).reshape(1)
    start_row = ctx_place % 2 * rows * 2
    pieces = (mamba_zx, mamba_out, attn_in, attn_out, mlp_in, mlp_out)
    shards = [weight_rows(l, pieces) for l in range(layers)]
    quarters = (sequences, rows, features)
    moves = to_halves_moves(hidden_in.reshape(quarters))
    first_shards = [shards[0][0], jnp.concatenate(shards[0][1:3], axis=1)]
    first_shards += [shards[l][i] for l in range(1, layers) for i in range(2)]
    late_pieces = [shards[l][3] for l in range(layers)] + [shards[l][2] for l in range(1, layers)]
    came = fsdp_moves(first_shards[0])
    late_block = jnp.concatenate(late_pieces, axis=1)[None]
    near = spread_first(late_block)
    moved = lax.optimization_barrier(moves + came + near)
    given = to_halves(*moved[:2])
    first_block = fsdp_join(first_shards[0], moved[2:-2])
    blocks, first_block = gathered_blocks(first_shards, first_block)
    gathers = Gathers([first_block] + blocks)
    late = gathered_ctx(late_block, moved[-2:], [v.shape[1] for v in late_pieces])
    small_args = (norm_gains, mamba_shared, conv_weight, conv_bias, head_params, mamba_gain)
    gathers.near[0], (given, small_args, start_row) = together(
        gathers.near[0], (given, small_args, start_row)
    )
    tables = turn_tables(start_row, 2 * rows)
    order = own_order(features * lax.axis_size("tp"), LOW)
    smalls = [
        local_small(order, l, *small_args)
        for l in range(layers)
    ]
    length = pick(lengths.reshape(sequences), ctx_place // 2, 0)
    keep = (start_row + jnp.arange(2 * rows) < length).astype(WIDE)[:, None]
    hidden = product(tp_join(given), order)
    saved, weights = [], []
    for l in range(layers):
        if l == layers - 1:
            (cotangent,), hidden = together((out_grad.reshape(quarters),), hidden)
            moves = to_halves_moves(cotangent)
        hidden, kept, used, moves = layer_forward(
            hidden, l, gathers, late, smalls[l], tables, place, sequences, moves
        )
        saved.append(kept)
        weights.append(used)
    upstream = product(tp_join(to_halves(*moves)), order) * keep
    own_rows = own_part(order, features, 0)
    mixed_out = against_rows((hidden * keep).astype(LOW), own_rows).astype(LOW)
    mixed_out = to_quarters(mixed_out)
    big, rest = [[None] * 4 for _ in range(layers)], [None] * layers
    scatters = Scatters()
    side_total = []

    def finished(layer, part, total):
        big[layer][part] = total
        if layer == 0 and part == 1:
            sides = [big[l][1][:, -3 * LANES :] for l in range(layers)]
            settle_side(scatters, sides, heads_total // lax.axis_size("tp"), side_total.append)

    small_grads = [None] * layers
    grad_low = upstream.astype(LOW)
    extra = [mixed_out]
    for l in reversed(range(layers)):
        upstream, grad_low, small_grads[l] = layer_backward(
            upstream, grad_low, saved[l], weights[l], smalls[l], tables, place, sequences,
            scatters, l == 0, functools.partial(finished, l), extra if l == layers - 1 else [],
        )
    input_grad = dot(upstream, own_rows.astype(WIDE), 1, 1, HIGHEST)
    input_grad = to_quarters(input_grad.astype(LOW)).astype(WIDE).reshape(hidden_in.shape)
    gains = jnp.concatenate([grads[0] for grads in small_grads], axis=0)
    gains = dot(gains, order.astype(WIDE), 1, 1, HIGHEST)
    small_grads = [
        (gains[2 * l : 2 * l + 2],) + small_grads[l][1:] for l in range(layers)
    ]
    settle_small(
        scatters, small_grads, heads_total // lax.axis_size("tp"), rest.__setitem__
    )
    scatters.finish()
    channels = mamba_out.shape[1]
    ff = mlp_out.shape[1]
    zx_grads, attn_grads, mix_grads, up_grads, down_grads = [], [], [], [], []
    for l in range(layers):
        early, late, mid, up = big[l]
        half = early.shape[1] // 2
        firsts, seconds = early[:, :half], early[:, half:]

        def rejoined(first, last):
            return jnp.concatenate([firsts[:, first:last], seconds[:, first:last]], axis=1)

        down_grads.append(rejoined(0, ff // 2).T)
        up_grads.append(up)
        both = rejoined(ff // 2, half)
        mix_grads.append((both[:, :channels].T, both[:, channels:].T))
        if mid is None:
            half = late.shape[1] // 2
            gate, x_part = late[:, :channels], late[:, half : half + channels]
            attn_grads.append(late[:, channels:half])
        else:
            gate, x_part = mid[:, :channels], late[:, :channels]
            keys = late[:, channels : channels + LANES]
            attn_grads.append(jnp.concatenate([mid[:, channels:], keys], axis=1))
        zx_grads.append(jnp.concatenate([gate, x_part], axis=1))

    def stacked(pick):
        return jnp.stack([pick(l) for l in range(layers)])

    return (
        extra[0].reshape(hidden_in.shape),
        input_grad,
        stacked(lambda l: rest[l][0]),
        jnp.stack(zx_grads).reshape(mamba_zx.shape),
        side_total[0],
        stacked(lambda l: rest[l][1]),
        stacked(lambda l: rest[l][2]),
        stacked(lambda l: rest[l][3]),
        stacked(lambda l: rest[l][4]),
        stacked(lambda l: mix_grads[l][0]),
        jnp.stack(attn_grads).reshape(attn_in.shape),
        stacked(lambda l: mix_grads[l][1]),
        jnp.stack(up_grads).reshape(mlp_in.shape),
        jnp.stack(down_grads),
    )


def solution(mesh):
    placed = (
        P(None, "fsdp", "ctx", "tp"),
        P(None, "fsdp"),
        P(),
        P(None, ("fsdp", "ctx"), None, "tp"),
        P(),
        P(),
        P(),
        P(),
        P(),
        P(None, "tp", ("fsdp", "ctx")),
        P(None, ("fsdp", "ctx"), "tp", None),
        P(None, "tp", ("fsdp", "ctx")),
        P(None, ("fsdp", "ctx"), None, "tp"),
        P(None, "tp", ("fsdp", "ctx")),
        P(None, "fsdp", "ctx", "tp"),
    )
    return jax.shard_map(
        local,
        mesh=mesh,
        in_specs=placed,
        out_specs=(
            P(None, "fsdp", "ctx", "tp"),
            P(None, "fsdp", "ctx", "tp"),
            P(),
            P(None, ("fsdp", "ctx"), None, "tp"),
            P(),
            P(),
            P(),
            P(),
            P(),
            P(None, "tp", ("fsdp", "ctx")),
            P(None, ("fsdp", "ctx"), "tp", None),
            P(None, "tp", ("fsdp", "ctx")),
            P(None, ("fsdp", "ctx"), None, "tp"),
            P(None, "tp", ("fsdp", "ctx")),
        ),
        check_vma=False,
    )
```

```python
import functools
import math

import jax
import jax.numpy as jnp
from jax import lax
from jax.experimental import pallas as pl
from jax.experimental.pallas import tpu as pltpu
from jax.sharding import PartitionSpec as P

HDIM = 64
STATE = 128
CONV = 4
ADIM = 64
GROUP = 4
LANES = 128
EPSILON = 1e-05
THETA = 100000000000.0
HIGHEST = lax.Precision.HIGHEST
LOW = jnp.bfloat16
WIDE = jnp.float32
MASKED = -1e30
VMEM_LIMIT = 56 * 1024 * 1024
PARCEL_ROWS = 16


def dot(a, b, ca=1, cb=0, precision=None):
    return lax.dot_general(
        a, b, (((ca,), (cb,)), ((), ())), preferred_element_type=WIDE, precision=precision
    )


def lane_iota(shape):
    return lax.broadcasted_iota(jnp.int32, shape, len(shape) - 1)


def row_iota(shape):
    return lax.broadcasted_iota(jnp.int32, shape, 0)


def kernel_call(body, grid, in_specs, out_specs, out_shape, scratch=(), flops=0, moved=0):
    return pl.pallas_call(
        body,
        grid=grid,
        in_specs=in_specs,
        out_specs=out_specs,
        out_shape=out_shape,
        scratch_shapes=list(scratch),
        compiler_params=pltpu.CompilerParams(vmem_limit_bytes=VMEM_LIMIT),
        cost_estimate=pl.CostEstimate(flops=flops, bytes_accessed=moved, transcendentals=0),
    )


def whole(shape):
    return pl.BlockSpec(shape, lambda s: (0,) * len(shape))


def rows_block(rows, cols, col=0):
    return pl.BlockSpec((rows, cols), lambda s: (s, col))


def sequence_block(*shape):
    return pl.BlockSpec((None,) + shape, lambda s: (s,) + (0,) * len(shape))


def xor_pairs(count, bit):
    return [(i, i ^ bit) for i in range(count)]


def next_half(x, forward):
    firsts = range(0, lax.axis_size("ctx"), 2)
    return lax.ppermute(x, "ctx", [(i, i + 1) if forward else (i + 1, i) for i in firsts])


STRAIGHT = ((0, 0), (2, 1), (1, 2), (3, 3))
CROSSED = ((1, 0), (3, 1), (0, 2), (2, 3))


def to_halves_moves(quarters):
    place = lax.axis_index("ctx")
    a = lax.ppermute(pick(quarters, place % 2, 0), "ctx", STRAIGHT)
    b = lax.ppermute(pick(quarters, 1 - place % 2, 0), "ctx", CROSSED)
    return a, b


def to_halves(a, b):
    place = lax.axis_index("ctx")
    return jnp.where(place < 2, jnp.concatenate([a, b]), jnp.concatenate([b, a]))


def to_quarters(half):
    place = lax.axis_index("ctx")
    parts = half.reshape((2, -1) + half.shape[1:])
    late = place // 2
    a = lax.ppermute(pick(parts, late, 0), "ctx", [(j, i) for i, j in STRAIGHT])
    b = lax.ppermute(pick(parts, 1 - late, 0), "ctx", [(j, i) for i, j in CROSSED])
    return jnp.where(place % 2 == 0, jnp.stack([a, b]), jnp.stack([b, a]))


def tp_peer(x):
    return lax.ppermute(x, "tp", xor_pairs(lax.axis_size("tp"), 1))


def tp_join(x):
    peer = tp_peer(x)
    first = lax.axis_index("tp") == 0
    return jnp.where(
        first, jnp.concatenate([x, peer], axis=-1), jnp.concatenate([peer, x], axis=-1)
    )


def tp_sum(partial_sum):
    low = partial_sum.astype(LOW)
    peer = tp_peer(low)
    return low.astype(WIDE) + peer.astype(WIDE)


def bits_of(axis):
    return [1 << i for i in range(lax.axis_size(axis).bit_length() - 1)]


def together(values, anchor):
    return lax.optimization_barrier((tuple(values), anchor))


def added(*parts):
    total = parts[0].astype(WIDE)
    for part in parts[1:]:
        total = total + part.astype(WIDE)
    return total


def ctx_swap(values, step):
    return lax.ppermute(values, "ctx", xor_pairs(lax.axis_size("ctx"), step))


def pick(values, place, dim):
    return lax.dynamic_index_in_dim(values, place, dim, False)


def half_lanes(width):
    return width // 256 * 128


FLIPS = (0, 1, 3, 2)


def own_order(features, dtype):
    fsdp, ctx = lax.axis_size("fsdp"), lax.axis_size("ctx")
    rows = features // (fsdp * ctx)
    own = jnp.arange(features)
    flip, rest = jnp.array(FLIPS)[own // (fsdp * rows)], own % (fsdp * rows)
    common = (rest // rows) * ctx * rows + (flip ^ lax.axis_index("ctx")) * rows + rest % rows
    return (jnp.arange(features)[:, None] == common[None, :]).astype(dtype)


def spread_first(block):
    return ctx_swap(block, 1), ctx_swap(block, 2)


def spread_parts(came):
    cut = half_lanes(came[0].shape[-1])
    return came[0][..., :cut], came[1][..., cut:]


def spread_second(parts):
    return ctx_swap(parts[0], 2), ctx_swap(parts[1], 1)


def spread_whole(block, came, far):
    width = block.shape[-1]
    return jnp.concatenate(
        [v.reshape(-1, width) for v in (block, came[0], jnp.concatenate(far, axis=-1), came[1])], axis=0
    )


def fsdp_moves(piece):
    count = lax.axis_size("fsdp")
    if count > 4:
        return ()
    return tuple(lax.ppermute(piece, "fsdp", xor_pairs(count, step)) for step in range(1, count))


def fsdp_join(piece, came):
    if not came:
        return lax.all_gather(piece, "fsdp", axis=0)
    place = lax.axis_index("fsdp")
    shape = (len(came) + 1,) + piece.shape
    out = lax.dynamic_update_index_in_dim(jnp.zeros(shape, piece.dtype), piece, place, 0)
    for step, values in enumerate(came, 1):
        out = lax.dynamic_update_index_in_dim(out, values, place ^ step, 0)
    return out


def gathered_blocks(pieces, anchor):
    following, anchor = together((pieces[1], jnp.concatenate(pieces[2:], axis=1)), anchor)
    blocks = [lax.all_gather(following[0], "fsdp", axis=0)]
    rest = lax.all_gather(following[1], "fsdp", axis=0)
    first = 0
    for piece in pieces[2:]:
        blocks.append(rest[..., first : first + piece.shape[1]])
        first += piece.shape[1]
    return blocks, anchor


class Gathers:
    def __init__(self, blocks):
        self.blocks = blocks
        self.near = [None] * len(blocks)
        self.far = [None] * len(blocks)
        self.first = 0
        self.near[0] = spread_first(self.blocks[0])

    def step(self, anchor):
        i = self.first
        if i >= len(self.blocks):
            return anchor
        self.near[i], anchor = together(self.near[i], anchor)
        parts = spread_parts(self.near[i])
        self.far[i] = spread_second(parts)
        _, anchor = together(parts, anchor)
        self.first = i + 1
        return anchor

    def begin(self, anchor):
        i = self.first
        if i < len(self.blocks) and self.near[i] is None:
            (self.blocks[i],), anchor = together((self.blocks[i],), anchor)
            self.near[i] = spread_first(self.blocks[i])
        return anchor

    def take(self, i):
        if self.first <= i:
            self.step(self.near[i][0])
        return spread_whole(self.blocks[i], self.near[i], self.far[i])


def gathered_ctx(block, near, widths):
    far = spread_second(spread_parts(near))
    rows = spread_whole(block, near, far).reshape((4,) + block.shape[1:])
    out, first = [], 0
    for width in widths:
        out.append(rows[..., first : first + width])
        first += width
    return out


def table_body(spans, *refs):
    count = len(spans)
    left_refs, a_refs, b_refs = (refs[i * count : (i + 1) * count] for i in range(3))
    up_ref, across_ref, x_ref, y_ref, own_a_ref, own_b_ref, turned_ref = refs[3 * count :]
    size = own_a_ref.shape[0]
    place = pl.program_id(0)
    for left_ref, a_ref, b_ref, (first, last) in zip(left_refs, a_refs, b_refs, spans):

        @pl.when(place == first)
        def _(left_ref=left_ref):
            turned_ref[...] = left_ref[...].astype(WIDE).T.astype(LOW)

        @pl.when((place >= first) & (place < last))
        def _(a_ref=a_ref, b_ref=b_ref):
            table = dot(turned_ref[...], a_ref[...]).astype(LOW)
            own_a_ref[...] = table[:size]
            x_ref[...] = table[size : 2 * size]
            up_ref[...] = table[2 * size :]
            table = dot(turned_ref[...], b_ref[...]).astype(LOW)
            own_b_ref[...] = table[:size]
            across_ref[...] = table[size : 3 * size]
            y_ref[...] = table[3 * size :]


def tables(pairs, tile):
    rows, features = pairs[0][0].shape
    size = features // len(FLIPS)
    spans, first = [], 0
    for _, right in pairs:
        spans.append((first, first + right.shape[1] // (2 * tile)))
        first = spans[-1][1]
    width = first * tile

    def columns(first, last, skip):
        return pl.BlockSpec(
            (rows, tile), lambda j: (0, skip + jnp.clip(j, first, last - 1) - first)
        )

    def tall(height):
        return pl.BlockSpec((height, tile), lambda j: (0, j))

    heights = (2 * size, 2 * size, size, size, size, size)
    return kernel_call(
        functools.partial(table_body, tuple(spans)),
        (first,),
        [whole((rows, features))] * len(pairs)
        + [columns(*span, 0) for span in spans]
        + [columns(*span, span[1] - span[0]) for span in spans],
        [tall(h) for h in heights],
        [jax.ShapeDtypeStruct((h, width), LOW) for h in heights],
        [pltpu.VMEM((features, rows), LOW)],
        flops=4 * rows * features * width,
        moved=width * (4 * rows + 4 * features),
    )(*[p[0] for p in pairs], *[p[1] for p in pairs], *[p[1] for p in pairs])


def fsdp_table_body(left_ref, right_ref, out_ref, turned_ref):
    @pl.when(pl.program_id(0) == 0)
    def _():
        turned_ref[...] = left_ref[...].astype(WIDE).T.astype(LOW)

    table = dot(turned_ref[...], right_ref[...])
    fsdp, flips, rows, _ = out_ref.shape
    for flip in range(flips):
        for place in range(fsdp):
            first = (flip * fsdp + place) * rows
            out_ref[place, flip] = table[first : first + rows].astype(LOW)


def fsdp_table(left, right, tile):
    rows, features = left.shape
    width = right.shape[1]
    fsdp, flips = lax.axis_size("fsdp"), len(FLIPS)
    shape = (fsdp, flips, features // (fsdp * flips))
    return kernel_call(
        fsdp_table_body,
        (width // tile,),
        [whole((rows, features)), pl.BlockSpec((rows, tile), lambda j: (0, j))],
        pl.BlockSpec(shape + (tile,), lambda j: (0, 0, 0, j)),
        jax.ShapeDtypeStruct(shape + (width,), LOW),
        [pltpu.VMEM((features, rows), LOW)],
        flops=2 * rows * features * width,
        moved=width * (2 * rows + 2 * features),
    )(left, right)


def pass_body(x_ref, y_ref, from_y_ref, from_x_ref, to_x_ref, to_y_ref):
    size = x_ref.shape[0]
    to_x_ref[...] = (x_ref[...].astype(WIDE) + from_y_ref[:size].astype(WIDE)).astype(LOW)
    to_y_ref[...] = (y_ref[...].astype(WIDE) + from_x_ref[size:].astype(WIDE)).astype(LOW)


def keep_body(own_a_ref, own_b_ref, from_y_ref, from_x_ref, last_x_ref, last_y_ref, out_ref):
    size, width = own_a_ref.shape
    out_ref[:, :width] = (
        own_a_ref[...].astype(WIDE) + from_y_ref[size:].astype(WIDE) + last_x_ref[...].astype(WIDE)
    ).astype(LOW)
    out_ref[:, width:] = (
        own_b_ref[...].astype(WIDE) + from_x_ref[:size].astype(WIDE) + last_y_ref[...].astype(WIDE)
    ).astype(LOW)


def once(body, out_shapes, *operands):
    outs = [jax.ShapeDtypeStruct(shape, LOW) for shape in out_shapes]
    return kernel_call(
        body,
        (1,),
        [whole(v.shape) for v in operands],
        [whole(shape) for shape in out_shapes],
        outs,
        moved=sum(v.size * 2 for v in operands) + sum(2 * math.prod(x) for x in out_shapes),
    )(*operands)


def ctx_scatter(cuts, waits):
    up, across, x, y, own_a, own_b = cuts
    from_y, from_x = yield (ctx_swap(up, 2), ctx_swap(across, 1)), waits[0], (up, across)
    to_x, to_y = once(pass_body, (x.shape, y.shape), x, y, from_y, from_x)
    last_x, last_y = yield (ctx_swap(to_x, 1), ctx_swap(to_y, 2)), waits[1], (to_x, to_y)
    size, width = own_a.shape
    (out,) = once(keep_body, ((size, 2 * width),), own_a, own_b, from_y, from_x, last_x, last_y)
    return out


def fsdp_scatter(table, direct):
    count = lax.axis_size("fsdp")
    if count > 4 or not direct:
        total = lax.psum_scatter(table, "fsdp", scatter_dimension=0, tiled=False)
        if direct is None:
            (total,) = yield (total,), 0, (table,)
        else:
            yield (), 0, (table,)
        return total.astype(WIDE)
    place = lax.axis_index("fsdp")
    came = tuple(
        lax.ppermute(pick(table, place ^ step, 0), "fsdp", xor_pairs(count, step))
        for step in range(1, count)
    )
    came = yield came, 0, (table,)
    return added(pick(table, place, 0), *came)


class Scatters:
    def __init__(self):
        self.active = []

    def add(self, pairs, tile, direct, waits, done):
        cuts = tables(pairs, tile)

        def run():
            part = yield from ctx_scatter(cuts, waits)
            fsdp = lax.axis_size("fsdp")
            part = part.reshape(fsdp, -1, part.shape[1])
            done((yield from fsdp_scatter(part, direct)))

        self.begin(run())
        return cuts[0]

    def add_fsdp_first(self, left, right, waits, done):
        table = fsdp_table(left, right, 512)
        fsdp, flips, rows, width = table.shape

        def run():
            moved = table.reshape(fsdp, flips * rows, width)
            total = lax.psum_scatter(moved, "fsdp", scatter_dimension=0, tiled=False)
            (total,) = yield (total,), waits, (moved,)
            cut = half_lanes(width)
            own, x, far, y = (total[i * rows : (i + 1) * rows] for i in range(flips))
            cuts = (
                total[2 * rows :, :cut],
                total[rows : 3 * rows, cut:],
                x[:, :cut],
                y[:, cut:],
                own[:, :cut],
                own[:, cut:],
            )
            done((yield from ctx_scatter(cuts, (0, 0))).astype(WIDE))

        self.begin(run())
        return table

    def begin(self, work):
        self.active.append([work, *next(work)])

    def step(self, anchor):
        ready = [item for item in self.active if anchor is None or item[2] == 0]
        for item in self.active:
            item[2] = max(item[2] - 1, 0)
        values = [v for item in ready for v in item[1]]
        if anchor is not None:
            values, anchor = together(values, anchor)
        elif values:
            values = lax.optimization_barrier(tuple(values))
        first, sent = 0, ()
        for item in ready:
            came = tuple(values[first : first + len(item[1])])
            first += len(item[1])
            try:
                item[1:] = item[0].send(came)
                sent += item[3]
            except StopIteration:
                self.active.remove(item)
        if sent and anchor is not None:
            _, anchor = together(sent, anchor)
        return anchor

    def finish(self):
        while self.active:
            self.step(None)


def join_rows(piece):
    v = piece[None, None]
    for dim, axis in enumerate(("fsdp", "ctx")):
        place = lax.axis_index(axis)
        for step in bits_of(axis):
            (came,) = yield (lax.ppermute(v, axis, xor_pairs(lax.axis_size(axis), step)),), 0, ()
            v = jnp.where(
                (place & step) == 0,
                jnp.concatenate([v, came], axis=dim),
                jnp.concatenate([came, v], axis=dim),
            )
    return v


def sum_everywhere(v):
    for axis in ("fsdp", "ctx"):
        for step in bits_of(axis):
            (came,) = yield (lax.ppermute(v, axis, xor_pairs(lax.axis_size(axis), step)),), 0, ()
            v = v + came
    return v


def turn_tables(start_row, rows):
    half = ADIM // 2
    places = (start_row + jnp.arange(rows)).astype(WIDE)
    rates = jnp.exp(-math.log(THETA) * jnp.arange(half).astype(WIDE) / half)
    angles = places[:, None] * rates[None, :]
    cosine, sine = jnp.cos(angles), jnp.sin(angles)
    one_cos = jnp.concatenate([cosine, cosine], axis=1)
    one_sin = jnp.concatenate([-sine, sine], axis=1)
    still = jnp.ones_like(one_cos)
    return (
        jnp.concatenate([one_cos, one_cos, one_cos, still], axis=1),
        jnp.concatenate([one_sin, one_sin, one_sin, jnp.zeros_like(one_sin)], axis=1),
    )


def turned(values, cosine, sine):
    lanes = lane_iota(values.shape) % ADIM
    swapped = jnp.where(
        lanes < ADIM // 2,
        pltpu.roll(values, LANES - ADIM // 2, 1),
        pltpu.roll(values, ADIM // 2, 1),
    )
    return values * cosine + swapped * sine


def qkv_body(rows_ref, cos_ref, sin_ref, q_ref, kv_ref):
    for pair in range(GROUP // 2):
        lanes = slice(pair * LANES, (pair + 1) * LANES)
        q_ref[:, lanes] = turned(
            rows_ref[:, lanes], cos_ref[:, :LANES], sin_ref[:, :LANES]
        ).astype(LOW)
    width = GROUP * ADIM
    kv_ref[...] = turned(
        rows_ref[:, width : width + LANES], cos_ref[:, LANES:], sin_ref[:, LANES:]
    ).astype(LOW)


def split_qkv(projected, tables, rows, column):
    total = projected.shape[0]
    width = GROUP * ADIM
    return kernel_call(
        qkv_body,
        (total // rows,),
        [rows_block(rows, width + LANES, column)] + [rows_block(rows, 2 * LANES)] * 2,
        [rows_block(rows, width), rows_block(rows, LANES)],
        [
            jax.ShapeDtypeStruct((total, width), LOW),
            jax.ShapeDtypeStruct((total, LANES), LOW),
        ],
        flops=total * 400 * 4,
        moved=total * 384 * 6,
    )(projected, *tables)


def head_lanes(values, head):
    pair = values[:, head // 2 * LANES : (head // 2 + 1) * LANES]
    if head % 2:
        pair = pltpu.roll(pair, ADIM, 1)
    return jnp.where(lane_iota(pair.shape) < ADIM, pair, jnp.zeros_like(pair))


def seen_keys(place, rows, total):
    shape = (rows, 2 * total)
    column = lane_iota(shape)
    own = (column < total) & (column <= row_iota(shape) + pl.program_id(0) * rows)
    return own | ((column >= total) & (column < total * (1 + place)))


def attend_body(place_ref, q_ref, own_ref, came_ref, out_ref, total_ref, keys):
    rows, total = q_ref.shape[0], own_ref.shape[0]
    keys[:total, :] = own_ref[...]
    keys[total:, :] = came_ref[...]
    seen = seen_keys(place_ref[0], rows, total)
    q_all = q_ref[...].astype(WIDE)
    all_keys = keys[...]
    totals = jnp.zeros((rows, LANES), WIDE)
    lanes = lane_iota((rows, LANES))
    outs = []
    for head in range(GROUP):
        query = (head_lanes(q_all, head) * ADIM**-0.5).astype(LOW)
        scores = jnp.where(seen, dot(query, all_keys, 1, 1), MASKED)
        top = jnp.max(scores, axis=1, keepdims=True)
        raised = jnp.exp(scores - top)
        row_total = jnp.sum(raised, axis=1, keepdims=True)
        outs.append(dot(raised.astype(LOW), all_keys) * (1.0 / row_total))
        totals = jnp.where(lanes == head, top + jnp.log(row_total), totals)
    total_ref[...] = totals
    for pair in range(GROUP // 2):
        first = pltpu.roll(outs[2 * pair], ADIM, 1)
        out_ref[:, pair * LANES : (pair + 1) * LANES] = jnp.where(
            lanes < ADIM, first, outs[2 * pair + 1]
        ).astype(LOW)


def attend(place, queries, own, came, rows):
    total, width = queries.shape
    return kernel_call(
        attend_body,
        (total // rows,),
        [
            pl.BlockSpec(memory_space=pltpu.SMEM),
            rows_block(rows, width),
            whole((total, LANES)),
            whole((total, LANES)),
        ],
        [rows_block(rows, width), rows_block(rows, LANES)],
        [
            jax.ShapeDtypeStruct((total, width), LOW),
            jax.ShapeDtypeStruct((total, LANES), WIDE),
        ],
        [pltpu.VMEM((2 * total, LANES), LOW)],
        flops=total * total * 2 * GROUP * LANES * 4,
        moved=total * (width * 4 + LANES * 12),
    )(place, queries, own, came)


def attend_back_body(
    place_ref, q_ref, grad_ref, total_ref, cos_ref, sin_ref, own_ref, came_ref,
    dq_ref, own_grad_ref, came_grad_ref, keys, grads,
):
    rows, total = q_ref.shape[0], own_ref.shape[0]
    keys[:total, :] = own_ref[...]
    keys[total:, :] = came_ref[...]
    seen = seen_keys(place_ref[0], rows, total)
    q_all = q_ref[...].astype(WIDE)
    grad_all = grad_ref[...].astype(WIDE)
    all_keys = keys[...]
    lanes = lane_iota((rows, LANES))
    grad_kv = None
    dqs = []
    for head in range(GROUP):
        query = (head_lanes(q_all, head) * ADIM**-0.5).astype(LOW)
        upper = pltpu.roll(head_lanes(grad_all, head), ADIM, 1).astype(LOW)
        scores = jnp.where(seen, dot(query, all_keys, 1, 1), MASKED)
        probs = jnp.exp(scores - total_ref[:, head : head + 1])
        grad_probs = dot(upper, all_keys, 1, 1)
        inner = jnp.sum(probs * grad_probs, axis=1, keepdims=True)
        grad_scores = (probs * (grad_probs - inner)).astype(LOW)
        dqs.append(dot(grad_scores, all_keys) * ADIM**-0.5)
        fresh = dot(grad_scores, query, 0, 0) + dot(probs.astype(LOW), upper, 0, 0)
        grad_kv = fresh if grad_kv is None else grad_kv + fresh
    for pair in range(GROUP // 2):
        both = jnp.where(lanes < ADIM, dqs[2 * pair], pltpu.roll(dqs[2 * pair + 1], ADIM, 1))
        dq_ref[:, pair * LANES : (pair + 1) * LANES] = turned(
            both, cos_ref[:, :LANES], -sin_ref[:, :LANES]
        ).astype(LOW)
    place = pl.program_id(0)

    @pl.when(place == 0)
    def _():
        grads[...] = grad_kv

    @pl.when(place > 0)
    def _():
        grads[...] += grad_kv

    own_grad_ref[...] = grads[:total, :]
    came_grad_ref[...] = grads[total:, :].astype(LOW)


def attend_back(place, queries, grad_out, log_total, tables, own, came, rows):
    total, width = queries.shape
    return kernel_call(
        attend_back_body,
        (total // rows,),
        [
            pl.BlockSpec(memory_space=pltpu.SMEM),
            rows_block(rows, width),
            rows_block(rows, width),
            rows_block(rows, LANES),
            rows_block(rows, 2 * LANES),
            rows_block(rows, 2 * LANES),
            whole((total, LANES)),
            whole((total, LANES)),
        ],
        [rows_block(rows, width), whole((total, LANES)), whole((total, LANES))],
        [
            jax.ShapeDtypeStruct((total, width), LOW),
            jax.ShapeDtypeStruct((total, LANES), WIDE),
            jax.ShapeDtypeStruct((total, LANES), LOW),
        ],
        [pltpu.VMEM((2 * total, LANES), LOW), pltpu.VMEM((2 * total, LANES), WIDE)],
        flops=total * total * 2 * GROUP * LANES * 10,
        moved=total * (width * 6 + LANES * 20),
    )(place, queries, grad_out, log_total, *tables, own, came)


def key_body(own_ref, *refs):
    came, (cos_ref, sin_ref, out_ref) = refs[:-3], refs[-3:]
    values = own_ref[...]
    for ref in came:
        values = values + ref[...].astype(WIDE)
    out_ref[...] = turned(values, cos_ref[:, LANES:], -sin_ref[:, LANES:]).astype(LOW)


def finish_keys(own, came, tables, rows):
    total = own.shape[0]
    return kernel_call(
        key_body,
        (total // rows,),
        [rows_block(rows, LANES)] * (1 + len(came)) + [rows_block(rows, 2 * LANES)] * 2,
        rows_block(rows, LANES),
        jax.ShapeDtypeStruct((total, LANES), LOW),
        flops=total * LANES * 10,
        moved=total * LANES * 12,
    )(own, *came, *tables)


def sigmoid(v):
    return 1.0 / (1.0 + jnp.exp(-v))


def softplus(v):
    return jnp.maximum(v, 0.0) + jnp.log1p(jnp.exp(-jnp.abs(v)))


def over_pair(values, pair, shape):
    first = values[:, 2 * pair : 2 * pair + 1]
    second = values[:, 2 * pair + 1 : 2 * pair + 2]
    return jnp.where(lane_iota(shape) < HDIM, first, second)


def down_pair(values, pair):
    shape = (LANES, LANES)
    first = jnp.broadcast_to(values[:, 2 * pair : 2 * pair + 1], shape)
    second = jnp.broadcast_to(values[:, 2 * pair + 1 : 2 * pair + 2], shape)
    return jnp.where(row_iota(shape) < HDIM, first, second)


def head_matrix(channels):
    shape = (LANES, channels)
    return jnp.where(lane_iota(shape) // HDIM == row_iota(shape), 1.0, 0.0).astype(LOW)


def two_parts(values):
    high = values.astype(LOW)
    return high, (values - high.astype(WIDE)).astype(LOW)


def over_heads(values, matrix):
    high, low = two_parts(values)
    return dot(high, matrix) + dot(low, matrix)


def by_heads(values, matrix):
    high, low = two_parts(values)
    return dot(high, matrix, 1, 1) + dot(low, matrix, 1, 1)


def lower_ones(rows, flip):
    shape = (rows, rows)
    t, s = row_iota(shape), lane_iota(shape)
    return jnp.where((t <= s) if flip else (t >= s), 1.0, 0.0).astype(WIDE)


def convolved(padded, taps_ref, rows):
    total = taps_ref[CONV : CONV + 1, :]
    for j in range(CONV):
        first = 8 - CONV + 1 + j
        total = total + taps_ref[j : j + 1, :] * padded[first : first + rows, :]
    return total


def scan_body(
    zx_ref, side_ref, rim_ref, taps_ref, heads_ref,
    stk_ref, x_ref, bc_ref, y_ref, first_ref, parcel_ref, cum_ref, all_ref, step_ref,
    padded, state, before_it,
):
    rows, channels = zx_ref.shape
    heads = channels // HDIM
    place = pl.program_id(0)

    @pl.when(place == 0)
    def _():
        padded[0:8, :] = rim_ref[...]
        state[...] = jnp.zeros(state.shape, WIDE)
        before_it[...] = jnp.zeros(before_it.shape, WIDE)

    @pl.when(place > 0)
    def _():
        padded[0:8, :] = padded[rows : rows + 8, :]

    stk_ref[:, :channels] = zx_ref[...].astype(LOW)
    stk_ref[:, channels:] = side_ref[:, : 2 * STATE].astype(LOW)
    padded[8 : 8 + rows, :] = stk_ref[...].astype(WIDE)
    before = convolved(padded, taps_ref, rows)
    active = (before * sigmoid(before)).astype(LOW)
    x_ref[...] = active[:, :channels]
    bc_ref[...] = active[:, channels:]
    step = softplus(side_ref[:, 2 * STATE :] + heads_ref[1:2, :])
    cum = dot(lower_ones(rows, False), -step * jnp.exp(heads_ref[0:1, :]), precision=HIGHEST)
    step_ref[...] = step
    cum_ref[...] = cum
    all_ref[...] = cum + before_it[0:1, :]
    cum_rows, step_rows = cum.T, step.T
    last = cum[rows - 1 : rows, :]
    before_it[...] = jnp.broadcast_to(before_it[0:1, :] + last, before_it.shape)
    matrix = head_matrix(channels)
    tail = over_heads(jnp.exp(last - cum) * step, matrix)
    grown, faded = over_heads(jnp.exp(cum), matrix), jnp.exp(last)
    entry, readout = bc_ref[:, :STATE], bc_ref[:, STATE:]
    cross = dot(readout, entry, 1, 1)
    shape = (rows, rows)
    causal = row_iota(shape) >= lane_iota(shape)
    lanes = lane_iota((rows, LANES))
    for pair in range(heads // 2):
        block = slice(pair * LANES, (pair + 1) * LANES)
        inputs = x_ref[:, block]
        outs = []
        for head in (2 * pair, 2 * pair + 1):
            gap = cum[:, head : head + 1] - cum_rows[head : head + 1, :]
            decay = jnp.exp(jnp.where(causal, gap, MASKED))
            mixed = (decay * cross * step_rows[head : head + 1, :]).astype(LOW)
            outs.append(dot(mixed, inputs))
        carried = dot(readout, state[block, :].astype(LOW), 1, 1)
        y_ref[:, block] = jnp.where(lanes < HDIM, outs[0], outs[1]) + carried * grown[:, block]
        scaled = (tail[:, block] * inputs.astype(WIDE)).astype(LOW)
        fresh = down_pair(faded, pair) * state[block, :] + dot(scaled, entry, 0, 0)
        state[block, :] = fresh
        parcel_ref[block, :] = fresh.astype(LOW)
    write_decays(parcel_ref, channels, before_it[0:1, :])

    @pl.when(place == 0)
    def _():
        first_ref[...] = state[...]


def scan_local(projected, side, rim, taps, heads, rows, channels):
    total = projected.shape[0]
    count = total // rows
    width = channels + 2 * STATE
    return kernel_call(
        scan_body,
        (count,),
        [
            rows_block(rows, channels, 1),
            rows_block(rows, side.shape[1]),
            whole((8, width)),
            whole((8, width)),
            whole((8, LANES)),
        ],
        [
            rows_block(rows, width),
            rows_block(rows, channels),
            rows_block(rows, 2 * STATE),
            rows_block(rows, channels),
            whole((channels, STATE)),
            whole((channels + PARCEL_ROWS, STATE)),
            rows_block(rows, LANES),
            rows_block(rows, LANES),
            rows_block(rows, LANES),
        ],
        [
            jax.ShapeDtypeStruct((total, width), LOW),
            jax.ShapeDtypeStruct((total, channels), LOW),
            jax.ShapeDtypeStruct((total, 2 * STATE), LOW),
            jax.ShapeDtypeStruct((total, channels), WIDE),
            jax.ShapeDtypeStruct((channels, STATE), WIDE),
            jax.ShapeDtypeStruct((channels + PARCEL_ROWS, STATE), LOW),
            jax.ShapeDtypeStruct((total, LANES), WIDE),
            jax.ShapeDtypeStruct((total, LANES), WIDE),
            jax.ShapeDtypeStruct((total, LANES), WIDE),
        ],
        [
            pltpu.VMEM((rows + 8, width), WIDE),
            pltpu.VMEM((channels, STATE), WIDE),
            pltpu.VMEM((8, LANES), WIDE),
        ],
        flops=total * rows * channels * 8,
        moved=total * width * 16,
    )(projected, side, rim, taps, heads)


def tail_body(
    y_ref, cum_ref, bc_ref, x_ref, gate_ref, heads_ref, gain_ref, parcel_ref, out_ref, norm_ref
):
    rows, channels = y_ref.shape
    readout = bc_ref[:, STATE:]
    grown = over_heads(jnp.exp(cum_ref[...]), head_matrix(channels))
    square = jnp.zeros((rows, 1), WIDE)
    for pair in range(channels // LANES):
        block = slice(pair * LANES, (pair + 1) * LANES)
        carried = dot(readout, parcel_ref[block, :], 1, 1)
        y = y_ref[:, block] + grown[:, block] * carried
        out_ref[:, block] = y
        skip = over_pair(heads_ref[2:3, :], pair, (1, LANES))
        gate = gate_ref[:, block]
        mixed = (y + skip * x_ref[:, block].astype(WIDE)) * (gate * sigmoid(gate))
        square = square + jnp.sum(mixed * mixed, axis=1, keepdims=True)
    scale = lax.rsqrt(square * (1.0 / channels) + EPSILON)
    for pair in range(channels // LANES):
        block = slice(pair * LANES, (pair + 1) * LANES)
        skip = over_pair(heads_ref[2:3, :], pair, (1, LANES))
        gate = gate_ref[:, block]
        mixed = (out_ref[:, block] + skip * x_ref[:, block].astype(WIDE)) * (gate * sigmoid(gate))
        norm_ref[:, block] = (mixed * scale * gain_ref[:, block]).astype(LOW)


def gate_tail(y, cum, bc, x, projected, heads, gain, parcel, rows):
    total, channels = y.shape
    return kernel_call(
        tail_body,
        (total // rows,),
        [
            rows_block(rows, channels),
            rows_block(rows, LANES),
            rows_block(rows, 2 * STATE),
            rows_block(rows, channels),
            rows_block(rows, channels, 0),
            whole((8, LANES)),
            whole((1, channels)),
            whole((channels + PARCEL_ROWS, STATE)),
        ],
        [rows_block(rows, channels), rows_block(rows, channels)],
        [
            jax.ShapeDtypeStruct((total, channels), WIDE),
            jax.ShapeDtypeStruct((total, channels), LOW),
        ],
        flops=total * channels * (2 * STATE + 40),
        moved=total * channels * 18,
    )(y, cum, bc, x, projected, heads, gain, parcel)


def tail_back_body(
    dn_ref, y_ref, cum_ref, bc_ref, x_ref, gate_ref, heads_ref, gain_ref,
    du_ref, dgate_ref, parcel_ref, sums_ref, state,
):
    @pl.when(pl.program_id(0) == 0)
    def _():
        state[...] = jnp.zeros(state.shape, WIDE)

    rows, channels = y_ref.shape
    readout = bc_ref[:, STATE:]
    grown = over_heads(jnp.exp(cum_ref[...]), head_matrix(channels))
    square = jnp.zeros((rows, 1), WIDE)
    inner = jnp.zeros((rows, 1), WIDE)
    for pair in range(channels // LANES):
        block = slice(pair * LANES, (pair + 1) * LANES)
        skip = over_pair(heads_ref[2:3, :], pair, (1, LANES))
        gate = gate_ref[:, block]
        mixed = (y_ref[:, block] + skip * x_ref[:, block].astype(WIDE)) * (gate * sigmoid(gate))
        square = square + jnp.sum(mixed * mixed, axis=1, keepdims=True)
        inner = inner + jnp.sum(
            dn_ref[:, block] * gain_ref[:, block] * mixed, axis=1, keepdims=True
        )
    scale = lax.rsqrt(square * (1.0 / channels) + EPSILON)
    inner = inner * scale * (1.0 / channels)
    sums_ref[...] = jnp.zeros(sums_ref.shape, WIDE)
    for pair in range(channels // LANES):
        block = slice(pair * LANES, (pair + 1) * LANES)
        skip = over_pair(heads_ref[2:3, :], pair, (1, LANES))
        gate = gate_ref[:, block]
        inputs = x_ref[:, block].astype(WIDE)
        sigma = sigmoid(gate)
        value = y_ref[:, block] + skip * inputs
        unit = value * (gate * sigma) * scale
        upstream = dn_ref[:, block]
        dmixed = scale * (upstream * gain_ref[:, block] - unit * inner)
        du = dmixed * gate * sigma
        du_ref[:, block] = du
        dgate_ref[:, block] = (
            dmixed * value * (sigma * (1.0 + gate * (1.0 - sigma)))
        ).astype(LOW)
        sums_ref[0:1, block] = jnp.sum(upstream * unit, axis=0, keepdims=True)
        sums_ref[1:2, block] = jnp.sum(du * inputs, axis=0, keepdims=True)
        fresh = state[block, :] + dot(
            (grown[:, block] * du).astype(LOW), readout, 0, 0
        )
        state[block, :] = fresh
        parcel_ref[block, :] = fresh.astype(LOW)
    write_decays(parcel_ref, channels, cum_ref[rows - 1 : rows, :])


def gate_tail_back(dn, y, cum, bc, x, projected, heads, gain, rows):
    total, channels = y.shape
    count = total // rows
    return kernel_call(
        tail_back_body,
        (count,),
        [
            rows_block(rows, channels),
            rows_block(rows, channels),
            rows_block(rows, LANES),
            rows_block(rows, 2 * STATE),
            rows_block(rows, channels),
            rows_block(rows, channels, 0),
            whole((8, LANES)),
            whole((1, channels)),
        ],
        [
            rows_block(rows, channels),
            rows_block(rows, channels),
            whole((channels + PARCEL_ROWS, STATE)),
            sequence_block(8, channels),
        ],
        [
            jax.ShapeDtypeStruct((total, channels), WIDE),
            jax.ShapeDtypeStruct((total, channels), LOW),
            jax.ShapeDtypeStruct((channels + PARCEL_ROWS, STATE), LOW),
            jax.ShapeDtypeStruct((count, 8, channels), WIDE),
        ],
        [pltpu.VMEM((channels, STATE), WIDE)],
        flops=total * channels * (2 * STATE + 60),
        moved=total * channels * 22,
    )(dn, y, cum, bc, x, projected, heads, gain)


def write_decays(parcel_ref, channels, last):
    high = jnp.broadcast_to(jnp.exp(last), (PARCEL_ROWS, LANES))
    top = high.astype(LOW).astype(WIDE)
    row = row_iota(high.shape)
    parcel_ref[channels:, :] = jnp.where(
        row == 0, top, jnp.where(row == 1, high - top, 0.0)
    ).astype(LOW)


def scan_back_body(
    du_ref, x_ref, bc_ref, stk_ref, prior_ref, rim_ref, cum_ref, all_ref, step_ref, side_ref,
    first_ref, parcel_ref, later_ref, taps_ref, heads_ref,
    dstk_ref, drim_ref, dstep_ref, dtaps_ref, dheads_ref, padded, dact, after, behind,
    carried_all, final_all,
):
    place = pl.program_id(0)
    second = jnp.where(place == 0, 1.0, 0.0).astype(WIDE)
    rows, channels = du_ref.shape
    heads = channels // HDIM
    width = channels + 2 * STATE
    entry, readout = bc_ref[:, :STATE], bc_ref[:, STATE:]
    cum, step = cum_ref[...], step_ref[...]
    cum_rows = cum.T
    last = cum[rows - 1 : rows, :]
    faded, arriving = jnp.exp(last), jnp.exp(all_ref[0:1, :] - cum[0:1, :])

    @pl.when(place == 0)
    def _():
        behind[...] = later_ref[:channels, :].astype(WIDE)
        after[8 + rows : 16 + rows, :] = jnp.zeros((8, width), WIDE)
        padded[0:8, :] = prior_ref[8:16, :].astype(WIDE)

    @pl.when(place > 0)
    def _():
        after[8 + rows : 16 + rows, :] = after[8:16, :]
        padded[0:8, :] = rim_ref[...]

    grown = jnp.exp(cum)
    decayed = jnp.exp(last - cum)
    tail = decayed * step
    matrix = head_matrix(channels)
    grown_all, tail_all, step_all = (over_heads(v, matrix) for v in (grown, tail, step))
    cross = dot(entry, readout, 1, 1)
    shape = (rows, rows)
    causal = row_iota(shape) <= lane_iota(shape)
    lanes = lane_iota((rows, LANES))
    small = lane_iota((1, LANES))
    dcross = jnp.zeros(shape, WIDE)
    entry_grad = jnp.zeros((rows, STATE), WIDE)
    readout_grad = jnp.zeros((rows, STATE), WIDE)
    pulled = jnp.zeros((rows, LANES), WIDE)
    arrived = []
    state_sum = jnp.zeros((1, LANES), WIDE)
    for pair in range(heads // 2):
        block = slice(pair * LANES, (pair + 1) * LANES)
        inputs = x_ref[:, block]
        inputs_wide = inputs.astype(WIDE)
        du = du_ref[:, block]
        du_low = du.astype(LOW)
        start = down_pair(arriving, pair) * parcel_ref[block, :].astype(WIDE)
        start = start + second * first_ref[block, :]
        later = behind[block, :]
        start_low, later_low = start.astype(LOW), later.astype(LOW)
        pulls = []
        for k in range(2):
            head = 2 * pair + k
            own = (lanes < HDIM) if k == 0 else (lanes >= HDIM)
            gap = cum_rows[head : head + 1, :] - cum[:, head : head + 1]
            decay = jnp.exp(jnp.where(causal, gap, MASKED))
            pulls.append(dot((decay * cross).astype(LOW), du_low))
            dmix = dot(jnp.where(own, inputs, jnp.zeros_like(inputs)), du_low, 1, 1) * decay
            stepped = step[:, head : head + 1]
            dcross = dcross + dmix * stepped
            dgap = dmix * cross
            pulled = jnp.where(lanes == head, jnp.sum(dgap, axis=1, keepdims=True), pulled)
            arrived.append(jnp.sum(dgap * stepped, axis=0, keepdims=True))
        pull = jnp.where(lanes < HDIM, pulls[0], pulls[1])
        grown_pair = grown_all[:, block]
        grown_du = grown_pair * du
        grown_low = grown_du.astype(LOW)
        behind[block, :] = down_pair(faded, pair) * later + dot(grown_low, readout, 0, 0)
        readout_grad = readout_grad + dot(grown_low, start_low)
        carried_all[:, block] = grown_du * dot(readout, start_low, 1, 1)
        tail_pair = tail_all[:, block]
        from_later = dot(entry, later_low, 1, 1)
        entry_grad = entry_grad + dot((tail_pair * inputs_wide).astype(LOW), later_low)
        final_all[:, block] = inputs_wide * from_later
        product = start * later
        for k in range(2):
            total = jnp.sum(
                jnp.sum(product[k * HDIM : (k + 1) * HDIM], axis=0, keepdims=True),
                axis=1,
                keepdims=True,
            )
            state_sum = jnp.where(small == 2 * pair + k, total, state_sum)
        skip = over_pair(heads_ref[2:3, :], pair, (1, LANES))
        dact[:, block] = (
            skip * du + step_all[:, block] * pull + tail_pair * from_later
        )
    dcross_low = dcross.astype(LOW)
    dact[:, channels : channels + STATE] = entry_grad + dot(dcross_low, readout)
    dact[:, channels + STATE :] = readout_grad + dot(dcross_low, entry, 0, 0)
    arrived.append(jnp.zeros((LANES - heads, rows), WIDE))
    carried_sum, final_sum = by_heads(carried_all[...], matrix), by_heads(final_all[...], matrix)
    arrived_columns = jnp.concatenate(arrived, axis=0).T
    weighted = tail * final_sum
    dcum = arrived_columns - step * pulled + carried_sum - weighted
    at_last = jnp.sum(weighted, axis=0, keepdims=True) + faded * state_sum
    dcum = dcum + jnp.where(row_iota(dcum.shape) == rows - 1, at_last, 0.0)
    dlog = dot(lower_ones(rows, True), dcum, precision=HIGHEST)
    rate = jnp.exp(heads_ref[0:1, :])
    dstep = pulled + decayed * final_sum - rate * dlog
    dstep_pre = dstep * sigmoid(side_ref[...] + heads_ref[1:2, :])
    dstep_pre = jnp.where(lanes < heads, dstep_pre, 0.0)
    dstep_ref[...] = dstep_pre.astype(LOW)
    dheads_ref[...] = jnp.zeros(dheads_ref.shape, WIDE)
    dheads_ref[0:1, :] = -rate * jnp.sum(step * dlog, axis=0, keepdims=True)
    dheads_ref[1:2, :] = jnp.sum(dstep_pre, axis=0, keepdims=True)

    padded[8 : 8 + rows, :] = stk_ref[...].astype(WIDE)
    before = convolved(padded, taps_ref, rows)
    sigma = sigmoid(before)
    dbefore = dact[...] * sigma * (1.0 + before * (1.0 - sigma))
    after[0:8, :] = jnp.zeros((8, width), WIDE)
    after[8 : 8 + rows, :] = dbefore
    dtaps_ref[...] = jnp.zeros(dtaps_ref.shape, WIDE)
    back = None
    for j in range(CONV):
        first = 8 - CONV + 1 + j
        dtaps_ref[j : j + 1, :] = jnp.sum(
            after[8 : 8 + rows, :] * padded[first : first + rows, :], axis=0, keepdims=True
        )
        first = CONV - 1 - j
        term = taps_ref[j : j + 1, :] * after[first : first + rows + 8, :]
        back = term if back is None else back + term
    dtaps_ref[CONV : CONV + 1, :] = jnp.sum(after[8 : 8 + rows, :], axis=0, keepdims=True)
    drim_ref[...] = back[0:8]
    dstk_ref[...] = back[8:].astype(LOW)


def scan_back(
    du, x, bc, stk, rim, cum, all_cum, step, side, first, parcel, later, taps, heads, rows
):
    total, channels = du.shape
    count = total // rows
    width = channels + 2 * STATE

    def back_block(cols, col=0):
        return pl.BlockSpec((rows, cols), lambda s: (count - 1 - s, col))

    return kernel_call(
        scan_back_body,
        (count,),
        [
            back_block(channels),
            back_block(channels),
            back_block(2 * STATE),
            back_block(width),
            pl.BlockSpec((16, width), lambda s: (rows // 16 - 1, 0)),
            whole((8, width)),
            back_block(LANES),
            back_block(LANES),
            back_block(LANES),
            back_block(LANES, 2 * STATE // LANES),
            whole((channels, STATE)),
            whole((channels + PARCEL_ROWS, STATE)),
            whole((channels + PARCEL_ROWS, STATE)),
            whole((8, width)),
            whole((8, LANES)),
        ],
        [
            back_block(width),
            whole((8, width)),
            back_block(LANES),
            sequence_block(8, width),
            sequence_block(8, LANES),
        ],
        [
            jax.ShapeDtypeStruct((total, width), LOW),
            jax.ShapeDtypeStruct((8, width), WIDE),
            jax.ShapeDtypeStruct((total, LANES), LOW),
            jax.ShapeDtypeStruct((count, 8, width), WIDE),
            jax.ShapeDtypeStruct((count, 8, LANES), WIDE),
        ],
        [
            pltpu.VMEM((rows + 8, width), WIDE),
            pltpu.VMEM((rows, width), WIDE),
            pltpu.VMEM((rows + 16, width), WIDE),
            pltpu.VMEM((channels, STATE), WIDE),
            pltpu.VMEM((rows, channels), WIDE),
            pltpu.VMEM((rows, channels), WIDE),
        ],
        flops=total * rows * channels * 20,
        moved=total * width * 24,
    )(du, x, bc, stk, stk, rim, cum, all_cum, step, side, first, parcel, later, taps, heads)


def unit_scale(values):
    return lax.rsqrt(jnp.mean(values * values, axis=-1, keepdims=True) + EPSILON)


def normalize(values, gain):
    return (values * unit_scale(values) * gain).astype(LOW)


def norm_grad_body(
    kept_ref, gain_ref, own_ref, peer_ref, base_ref, out_ref, low_ref, sums_ref
):
    kept = kept_ref[...]
    scale = unit_scale(kept)
    unit = kept * scale
    upstream = own_ref[...].astype(WIDE) + peer_ref[...].astype(WIDE)
    scaled = upstream * gain_ref[...]
    inner = jnp.mean(scaled * unit, axis=-1, keepdims=True)
    out = base_ref[...] + scale * (scaled - unit * inner)
    out_ref[...] = out
    low_ref[...] = out.astype(LOW)
    sums = jnp.sum(upstream * unit, axis=0, keepdims=True)

    @pl.when(pl.program_id(0) == 0)
    def _():
        sums_ref[...] = jnp.broadcast_to(sums, sums_ref.shape)

    @pl.when(pl.program_id(0) > 0)
    def _():
        sums_ref[...] += jnp.broadcast_to(sums, sums_ref.shape)


def norm_grad(kept, gain, partial_grad, base):
    own = partial_grad.astype(LOW)
    rows, features = kept.shape
    tile = min(rows, 256)
    out, low, sums = kernel_call(
        norm_grad_body,
        (rows // tile,),
        [rows_block(tile, features), whole((1, features))] + [rows_block(tile, features)] * 3,
        [rows_block(tile, features), rows_block(tile, features), whole((8, features))],
        [
            jax.ShapeDtypeStruct((rows, features), WIDE),
            jax.ShapeDtypeStruct((rows, features), LOW),
            jax.ShapeDtypeStruct((8, features), WIDE),
        ],
        flops=rows * features * 12,
        moved=rows * features * 18,
    )(kept, gain[None], own, tp_peer(own), base)
    return out, low, sums[0]


def product(a, b):
    return jnp.dot(a, b, preferred_element_type=WIDE)


def against_rows(a, b):
    return dot(a, b, 1, 1)


def halves(values):
    cut = half_lanes(values.shape[1])
    return values[:, :cut], values[:, cut:]


def over_rows(a, b):
    return dot(a, b, 0, 0).astype(LOW)


def weight_rows(layer, pieces):
    zx, mix, attn, attn_out, mlp, mlp_out = (p[layer] for p in pieces)
    rows = zx.shape[0]
    return (
        jnp.concatenate([zx.reshape(rows, -1), attn.reshape(rows, -1)], axis=1),
        jnp.concatenate([mix.T, attn_out.T], axis=1),
        mlp.reshape(rows, -1),
        mlp_out.T,
    )


def own_part(values, size, axis):
    return lax.dynamic_slice_in_dim(values, lax.axis_index("tp") * size, size, axis)


def padded_to(values, rows, lanes):
    return jnp.pad(values, ((0, rows - values.shape[0]), (0, lanes - values.shape[1])))


def local_small(order, layer, norm_gains, mamba_shared, conv_weight, conv_bias, head_params, mamba_gain):
    tp = lax.axis_size("tp")
    heads = head_params.shape[2] // tp
    full_ssm = mamba_gain.shape[1]
    channels = full_ssm // tp
    shared_all = mamba_shared[layer]
    shared = jnp.concatenate(
        [
            shared_all[:, : 2 * STATE],
            own_part(shared_all[:, 2 * STATE :], heads, 1),
            jnp.zeros((shared_all.shape[0], LANES - heads), LOW),
        ],
        axis=1,
    )
    taps_all = jnp.concatenate([conv_weight[layer], conv_bias[layer][None]], axis=0).astype(WIDE)
    taps = jnp.concatenate(
        [own_part(taps_all[:, :full_ssm], channels, 1), taps_all[:, full_ssm:]], axis=1
    )
    return (
        product(norm_gains[layer], order),
        dot(order, shared, 0, 0).astype(LOW),
        padded_to(taps, 8, taps.shape[1]),
        padded_to(own_part(head_params[layer], heads, 1), 8, LANES),
        own_part(mamba_gain[layer].astype(WIDE), channels, 0)[None],
    )


def layer_forward(hidden, layer, gathers, late, small, tables, place, sequences, moves):
    zx_w = gathers.take(2 * layer)
    gains, shared, taps, heads, gain = small
    rows = hidden.shape[0] // sequences
    channels = gain.shape[1]
    head_count = channels // HDIM
    normed = normalize(hidden, gains[0])
    projected = product(normed, zx_w)
    side = product(normed, shared)
    if layer == 0:
        late[:], projected = together(late, projected)
        late[:] = [lax.all_gather(v, "fsdp", axis=1).reshape(-1, v.shape[-1]) for v in late]
    mlp_out_w = late[layer]
    edge = jnp.concatenate(
        [projected[-CONV + 1 :, channels : 2 * channels], side[-CONV + 1 :, : 2 * STATE]], axis=1
    )
    came = next_half(edge.astype(LOW), True).astype(WIDE)
    rim = jnp.pad(came, ((8 - CONV + 1, 0), (0, 0)))
    queries, kv = split_qkv(projected, tables, rows, 2 * channels // (zx_w.shape[1] - 2 * channels))
    kv_came = next_half(kv, True)
    (kv_came,), rim = together((kv_came,), rim)
    rim = gathers.begin(rim)
    stk, x, bc, y_local, first, parcel_out, cum, all_cum, step = scan_local(
        projected, side, rim, taps, heads, rows, channels
    )
    parcel = next_half(parcel_out, True)
    attended, log_total = attend(place, queries, kv, kv_came, 2 * rows)
    if layer > 0:
        moves, parcel = together(moves, parcel)
        mlp_w = late[len(late) // 2 + layer]
        (mlp_w,), parcel = together((mlp_w,), parcel)
    (attended, parcel), y_local = together((attended, parcel), y_local)
    parcel = gathers.step(parcel)
    parcel = gathers.begin(parcel)
    y, mamba_norm = gate_tail(y_local, all_cum, bc, x, projected, heads, gain, parcel, rows)
    both = jnp.concatenate([mamba_norm, attended], axis=1)
    rest = gathers.take(2 * layer + 1)
    mix_w = rest[:, : both.shape[1]]
    if layer == 0:
        mlp_w = rest[:, both.shape[1] :]
    else:
        (mlp_out_w,), both = together((mlp_out_w,), both)
    after_mix = hidden + tp_sum(against_rows(both, mix_w))
    normed_two = normalize(after_mix, gains[1])
    gate_up = product(normed_two, mlp_w)
    ff = gate_up.shape[1] // 2
    activated = (jax.nn.silu(gate_up[:, :ff]) * gate_up[:, ff:]).astype(LOW)
    if gathers.near[-1] is None:
        activated = gathers.step(activated)
    result = after_mix + tp_sum(against_rows(activated, mlp_out_w))
    saved = (
        hidden, normed, projected, side, rim, queries, kv, kv_came, stk, x, bc, cum, all_cum, step,
        first, parcel, log_total, y, both, after_mix, normed_two, gate_up, activated,
    )
    return result, saved, (zx_w, mix_w, mlp_w, mlp_out_w), moves


def layer_backward(
    upstream, grad_mlp, saved, weights, small, tables, place, sequences, scatters, split, done, extra
):
    (
        hidden, normed, projected, side, rim, queries, kv, kv_came, stk, x, bc, cum, all_cum, step,
        first, parcel, log_total, y, both, after_mix, normed_two, gate_up, activated,
    ) = saved
    zx_w, mix_w, mlp_w, mlp_out_w = weights
    gains, shared, taps, heads, gain = small
    rows = hidden.shape[0] // sequences
    channels = gain.shape[1]
    head_count = channels // HDIM
    grad_act = product(grad_mlp, mlp_out_w)
    ff = grad_act.shape[1]
    gate_part, up_part = gate_up[:, :ff], gate_up[:, ff:]
    sigma = jax.nn.sigmoid(gate_part)
    grad_gu = jnp.concatenate(
        [
            grad_act * up_part * sigma * (1.0 + gate_part * (1.0 - sigma)),
            grad_act * gate_part * sigma,
        ],
        axis=1,
    ).astype(LOW)
    table = scatters.add_fsdp_first(normed_two, grad_gu, 2, functools.partial(done, 3))
    _, grad_gu = together((table,), grad_gu)
    grad_mid, grad_mix, grad_gain_two = norm_grad(
        after_mix, gains[1], against_rows(grad_gu, mlp_w), upstream
    )
    grad_mid = scatters.step(grad_mid)
    if extra:
        extra[:], grad_mix = together(extra, grad_mix)
    table = scatters.add(
        [(grad_mlp, activated), (grad_mix, both)],
        512,
        None if split else False,
        (0, 0),
        functools.partial(done, 0),
    )
    _, grad_mix = together((table,), grad_mix)
    grad_norm = product(grad_mix, mix_w[:, :channels])
    grad_attended = product(grad_mix, mix_w[:, channels:]).astype(LOW)
    du, grad_gate, state_grads, tail_sums = gate_tail_back(
        grad_norm, y, all_cum, bc, x, projected, heads, gain, rows
    )
    later = next_half(state_grads, False)
    grad_q, own_kv, sent_kv = attend_back(
        place, queries, grad_attended, log_total, tables, kv, kv_came, 2 * rows
    )
    came_kv = [next_half(sent_kv, False)]
    (later, *came_kv), grad_gate = together((later, *came_kv), grad_gate)
    later = scatters.step(later)
    if split:
        mid = jnp.concatenate([grad_gate, grad_q], axis=1)
        table = scatters.add([(normed, mid)], 512, None, (0, 0), functools.partial(done, 2))
        _, later = together((table,), later)
    dstk, drim, grad_step, dtaps, dheads = scan_back(
        du, x, bc, stk, rim, cum, all_cum, step, side, first, parcel, later, taps, heads, rows
    )
    drim = scatters.step(drim)
    returned = next_half(drim[8 - CONV + 1 :], False)
    last_rows = (dstk[-CONV + 1 :].astype(WIDE) + returned).astype(LOW)
    dstk = lax.dynamic_update_slice(dstk, last_rows, (dstk.shape[0] - CONV + 1, 0))
    grad_kv = finish_keys(own_kv, came_kv, tables, rows)
    grad_late = jnp.concatenate([dstk[:, :channels], grad_kv], axis=1)
    grad_first = jnp.concatenate(
        [grad_gate, grad_late[:, :channels], grad_q, grad_late[:, channels:]], axis=1
    )
    grad_side = jnp.concatenate([dstk[:, channels:], grad_step], axis=1)
    if split:
        late, tile = [grad_late, grad_side], 640
    else:
        late = [grad_gate, grad_q, grad_late[:, channels:], grad_late[:, :channels], grad_side]
        tile = 1152
    late = jnp.concatenate(late, axis=1)
    table = scatters.add([(normed, late)], tile, split, (0, 0), functools.partial(done, 1))
    _, grad_first = together((table,), grad_first)
    below, grad_mlp, grad_gain_one = norm_grad(
        hidden,
        gains[0],
        against_rows(grad_first, zx_w) + against_rows(grad_side, shared),
        grad_mid,
    )
    tail_sums = jnp.sum(tail_sums, axis=0)
    dheads = jnp.sum(dheads, axis=0)
    skip_grad = jnp.sum(tail_sums[1].reshape(head_count, HDIM), axis=1)
    skip_grad = jnp.pad(skip_grad, (0, LANES - head_count))[None]
    small_grads = (
        jnp.stack([grad_gain_one, grad_gain_two]),
        jnp.sum(dtaps, axis=0),
        jnp.where(row_iota(dheads.shape) == 2, skip_grad, dheads),
        tail_sums[0],
    )
    below, grad_mlp = scatters.step((below, grad_mlp))
    return below, grad_mlp, small_grads


def tp_ordered(a, b):
    low_half = lax.axis_index("tp") == 0
    return jnp.where(
        low_half, jnp.concatenate([a, b], axis=-1), jnp.concatenate([b, a], axis=-1)
    )


def settle_side(scatters, sums, half_heads, done):
    def run():
        fsdp = lax.axis_size("fsdp")
        layers = sums
        own = layers[0]
        rows = own.shape[0]
        wide = jnp.stack([v[:, : 2 * STATE].reshape(rows, 2, STATE) for v in layers])
        place = lax.axis_index("tp")
        (came,) = yield (tp_peer(pick(wide, 1 - place, 2)),), 0, ()
        mine = pick(wide, place, 2) + came
        steps = jnp.stack([v[:, 2 * STATE : 2 * STATE + half_heads] for v in layers]).reshape(-1)
        packed = jnp.concatenate([mine.reshape(-1), steps])
        packed = jnp.pad(packed, (0, -packed.size % (16 * LANES))).reshape(-1, LANES)
        joined = yield from join_rows(packed.astype(LOW))
        (theirs,) = yield (tp_peer(joined),), 0, ()
        count = len(layers)
        places = fsdp * lax.axis_size("ctx")

        def taken(values):
            flat = values.reshape(places, -1)
            wide_size = count * rows * STATE
            first = flat[:, :wide_size].reshape(places, count, rows, STATE)
            second = flat[:, wide_size : wide_size + count * rows * half_heads]
            return first, second.reshape(places, count, rows, half_heads)

        (wide_own, step_own), (wide_peer, step_peer) = taken(joined), taken(theirs)
        full = jnp.concatenate(
            [tp_ordered(wide_own, wide_peer), tp_ordered(step_own, step_peer)], axis=-1
        )
        done(full.transpose(1, 0, 2, 3).reshape(count, places * rows, -1).astype(WIDE))

    scatters.begin(run())


def settle_small(scatters, small_grads, half_heads, done):
    def run():
        layers = len(small_grads)
        shapes = [v.shape for v in small_grads[0]]
        flat = [v.reshape(-1, LANES) for grads in small_grads for v in grads]
        flat = [jnp.pad(v, ((0, -v.shape[0] % 8), (0, 0))) for v in flat]
        packed = yield from sum_everywhere(jnp.concatenate(flat, axis=0))
        (packed_peer,) = yield (tp_peer(packed),), 0, ()
        own, peer = [], []
        first = 0
        for values, shape in zip(flat, shapes * layers):
            for source, parts in ((packed, own), (packed_peer, peer)):
                piece = source[first : first + math.prod(shape) // LANES]
                parts.append(piece.reshape(shape))
            first += values.shape[0]
        count = len(shapes)
        for l in range(layers):
            (gains, taps, heads, gain), (gains_p, taps_p, heads_p, gain_p) = (
                v[l * count : (l + 1) * count] for v in (own, peer)
            )
            channels = gain.shape[0]
            taps_full = jnp.concatenate(
                [
                    tp_ordered(taps[:, :channels], taps_p[:, :channels]),
                    taps[:, channels:] + taps_p[:, channels:],
                ],
                axis=1,
            )
            done(
                l,
                (
                    jnp.where(lax.axis_index("tp") == 0, gains, gains_p),
                    taps_full[:CONV],
                    taps_full[CONV],
                    tp_ordered(heads[:3, :half_heads], heads_p[:3, :half_heads]),
                    tp_ordered(gain, gain_p),
                ),
            )

    scatters.begin(run())


def local(
    hidden_in, lengths, norm_gains, mamba_zx, mamba_shared, conv_weight, conv_bias, head_params,
    mamba_gain, mamba_out, attn_in, attn_out, mlp_in, mlp_out, out_grad,
):
    layers = norm_gains.shape[0]
    micro, own_seqs, rows, features = hidden_in.shape
    sequences = micro * own_seqs
    full_ssm = mamba_gain.shape[1]
    heads_total = head_params.shape[2]
    ctx_place = lax.axis_index("ctx")
    place = (ctx_place % 2).astype(jnp.int32).reshape(1)
    start_row = ctx_place % 2 * rows * 2
    pieces = (mamba_zx, mamba_out, attn_in, attn_out, mlp_in, mlp_out)
    shards = [weight_rows(l, pieces) for l in range(layers)]
    quarters = (sequences, rows, features)
    moves = to_halves_moves(hidden_in.reshape(quarters))
    first_shards = [shards[0][0], jnp.concatenate(shards[0][1:3], axis=1)]
    first_shards += [shards[l][i] for l in range(1, layers) for i in range(2)]
    late_pieces = [shards[l][3] for l in range(layers)] + [shards[l][2] for l in range(1, layers)]
    came = fsdp_moves(first_shards[0])
    late_block = jnp.concatenate(late_pieces, axis=1)[None]
    near = spread_first(late_block)
    moved = lax.optimization_barrier(moves + came + near)
    given = to_halves(*moved[:2])
    first_block = fsdp_join(first_shards[0], moved[2:-2])
    blocks, first_block = gathered_blocks(first_shards, first_block)
    gathers = Gathers([first_block] + blocks)
    late = gathered_ctx(late_block, moved[-2:], [v.shape[1] for v in late_pieces])
    small_args = (norm_gains, mamba_shared, conv_weight, conv_bias, head_params, mamba_gain)
    gathers.near[0], (given, small_args, start_row) = together(
        gathers.near[0], (given, small_args, start_row)
    )
    tables = turn_tables(start_row, 2 * rows)
    order = own_order(features * lax.axis_size("tp"), LOW)
    smalls = [
        local_small(order, l, *small_args)
        for l in range(layers)
    ]
    length = pick(lengths.reshape(sequences), ctx_place // 2, 0)
    keep = (start_row + jnp.arange(2 * rows) < length).astype(WIDE)[:, None]
    hidden = product(tp_join(given), order)
    saved, weights = [], []
    for l in range(layers):
        if l == layers - 1:
            (cotangent,), hidden = together((out_grad.reshape(quarters),), hidden)
            moves = to_halves_moves(cotangent)
        hidden, kept, used, moves = layer_forward(
            hidden, l, gathers, late, smalls[l], tables, place, sequences, moves
        )
        saved.append(kept)
        weights.append(used)
    upstream = product(tp_join(to_halves(*moves)), order) * keep
    own_rows = own_part(order, features, 0)
    mixed_out = against_rows((hidden * keep).astype(LOW), own_rows).astype(LOW)
    mixed_out = to_quarters(mixed_out)
    big, rest = [[None] * 4 for _ in range(layers)], [None] * layers
    scatters = Scatters()
    side_total = []

    def finished(layer, part, total):
        big[layer][part] = total
        if layer == 0 and part == 1:
            sides = [big[l][1][:, -3 * LANES :] for l in range(layers)]
            settle_side(scatters, sides, heads_total // lax.axis_size("tp"), side_total.append)

    small_grads = [None] * layers
    grad_low = upstream.astype(LOW)
    extra = [mixed_out]
    for l in reversed(range(layers)):
        upstream, grad_low, small_grads[l] = layer_backward(
            upstream, grad_low, saved[l], weights[l], smalls[l], tables, place, sequences,
            scatters, l == 0, functools.partial(finished, l), extra if l == layers - 1 else [],
        )
    input_grad = dot(upstream, own_rows.astype(WIDE), 1, 1, HIGHEST)
    input_grad = to_quarters(input_grad.astype(LOW)).astype(WIDE).reshape(hidden_in.shape)
    gains = jnp.concatenate([grads[0] for grads in small_grads], axis=0)
    gains = dot(gains, order.astype(WIDE), 1, 1, HIGHEST)
    small_grads = [
        (gains[2 * l : 2 * l + 2],) + small_grads[l][1:] for l in range(layers)
    ]
    settle_small(
        scatters, small_grads, heads_total // lax.axis_size("tp"), rest.__setitem__
    )
    scatters.finish()
    channels = mamba_out.shape[1]
    ff = mlp_out.shape[1]
    zx_grads, attn_grads, mix_grads, up_grads, down_grads = [], [], [], [], []
    for l in range(layers):
        early, late, mid, up = big[l]
        half = early.shape[1] // 2
        firsts, seconds = early[:, :half], early[:, half:]

        def rejoined(first, last):
            return jnp.concatenate([firsts[:, first:last], seconds[:, first:last]], axis=1)

        down_grads.append(rejoined(0, ff // 2).T)
        up_grads.append(up)
        both = rejoined(ff // 2, half)
        mix_grads.append((both[:, :channels].T, both[:, channels:].T))
        if mid is None:
            half = late.shape[1] // 2
            gate, x_part = late[:, :channels], late[:, half : half + channels]
            attn_grads.append(late[:, channels:half])
        else:
            gate, x_part = mid[:, :channels], late[:, :channels]
            keys = late[:, channels : channels + LANES]
            attn_grads.append(jnp.concatenate([mid[:, channels:], keys], axis=1))
        zx_grads.append(jnp.concatenate([gate, x_part], axis=1))

    def stacked(pick):
        return jnp.stack([pick(l) for l in range(layers)])

    return (
        extra[0].reshape(hidden_in.shape),
        input_grad,
        stacked(lambda l: rest[l][0]),
        jnp.stack(zx_grads).reshape(mamba_zx.shape),
        side_total[0],
        stacked(lambda l: rest[l][1]),
        stacked(lambda l: rest[l][2]),
        stacked(lambda l: rest[l][3]),
        stacked(lambda l: rest[l][4]),
        stacked(lambda l: mix_grads[l][0]),
        jnp.stack(attn_grads).reshape(attn_in.shape),
        stacked(lambda l: mix_grads[l][1]),
        jnp.stack(up_grads).reshape(mlp_in.shape),
        jnp.stack(down_grads),
    )


def solution(mesh):
    placed = (
        P(None, "fsdp", "ctx", "tp"),
        P(None, "fsdp"),
        P(),
        P(None, ("fsdp", "ctx"), None, "tp"),
        P(),
        P(),
        P(),
        P(),
        P(),
        P(None, "tp", ("fsdp", "ctx")),
        P(None, ("fsdp", "ctx"), "tp", None),
        P(None, "tp", ("fsdp", "ctx")),
        P(None, ("fsdp", "ctx"), None, "tp"),
        P(None, "tp", ("fsdp", "ctx")),
        P(None, "fsdp", "ctx", "tp"),
    )
    return jax.shard_map(
        local,
        mesh=mesh,
        in_specs=placed,
        out_specs=(
            P(None, "fsdp", "ctx", "tp"),
            P(None, "fsdp", "ctx", "tp"),
            P(),
            P(None, ("fsdp", "ctx"), None, "tp"),
            P(),
            P(),
            P(),
            P(),
            P(),
            P(None, "tp", ("fsdp", "ctx")),
            P(None, ("fsdp", "ctx"), "tp", None),
            P(None, "tp", ("fsdp", "ctx")),
            P(None, ("fsdp", "ctx"), None, "tp"),
            P(None, "tp", ("fsdp", "ctx")),
        ),
        check_vma=False,
    )
```
